32 devices in a mesh: row: 4 (over x, core), col: 8 (over z, y).
Axes of the slice: x: 2, y: 2, z: 4, core: 2. Of those that a mesh axis runs over, the one named last changes fastest.
Arguments:
- weights: float32 [160, 4, 256, 256], P(('row', 'col')), may hold values from 0.05 to 0.5, as said below
- edges: int32 [160, 4, 256, 256], P(('row', 'col')), may hold values from 0 to 1, as said below
- offsets: int32 [160, 4], P(('row', 'col')), may hold values from 0 to 5, as said below
- counts: int32 [160], P(('row', 'col')), may hold values from 1 to 4, as said below
Outputs:
- support: float32 [160, 4, 256, 256], P(('row', 'col'))
The draws below stay inside these ranges and needn't reach their ends.
Inputs may be any that keep to these rules, and one draw needn't show every extreme that they name: Slot 0 of every tile row holds 0 (the diagonal tile). The listed slots (below the row's count) hold distinct offsets o with row + o < 160. Slots at or beyond the count hold arbitrary offsets. `counts`: at most 4 and at most the tile columns left in the row; some row has 4. `edges`: in slot 0 every tile is symmetric with a zero diagonal. `weights`: in slot 0 every tile is symmetric.
All inputs are finite; a program needn't handle non-finite values.
Results may differ from the reference program's by a relative error of at most 0.0003.
Values sent between devices are 32-bit elements; how exact they have to be, the bound alone decides.
No kernel may reach another device: no remote copies, remote signals or barrier semaphores. Data moves between devices by JAX's collectives and lax.ppermute only.
A program may use at most 576 MiB of HBM per device.

```python
import jax
import jax.numpy as jnp
from jax import lax

TILE = 256
LIST = 4
BAND = 6
NTR = 160


def tile_pattern(key):
    row_ids = jnp.arange(NTR, dtype=jnp.int32)
    room_left = jnp.minimum(BAND, NTR - row_ids)
    columns = jnp.arange(1, BAND, dtype=jnp.int32)
    scores = jax.random.randint(jax.random.fold_in(key, 11), (NTR, BAND - 1), 0, 1 << 20) * BAND + columns[None, :]
    scores = jnp.where(columns[None, :] < room_left[:, None], scores, (1 << 26) + columns[None, :])
    ranked = jnp.argsort(scores, axis=1, stable=True).astype(jnp.int32) + 1
    offsets = jnp.concatenate([jnp.zeros((NTR, 1), jnp.int32), ranked[:, :LIST - 1]], axis=1)
    counts = jax.random.randint(jax.random.fold_in(key, 12), (NTR,), 1, LIST + 1)
    counts = jnp.minimum(counts, room_left)
    chosen = jax.random.randint(jax.random.fold_in(key, 13), (), 0, NTR - BAND + 1)
    counts = jnp.where(row_ids == chosen, LIST, counts)
    return (offsets.astype(jnp.int32), counts.astype(jnp.int32))


def draw_offsets(key, part):
    return tile_pattern(key)[0]


def draw_counts(key, part):
    return tile_pattern(key)[1]


def draw_weights(key, part):
    key = jax.random.fold_in(key, 5)
    shape = (NTR, LIST, TILE, TILE)
    values = jnp.exp(jax.random.uniform(key, shape, jnp.float32, jnp.log(0.05), jnp.log(0.5)))
    diagonal = 0.5 * (values[:, 0] + jnp.swapaxes(values[:, 0], 1, 2))
    return values.at[:, 0].set(diagonal)


def draw_edges(key, part):
    key = jax.random.fold_in(key, 7)
    picks = (jax.random.randint(key, (NTR, LIST, TILE, TILE), 0, 100) < 35).astype(jnp.int32)
    upper = jnp.triu(picks[:, 0], 1)
    diagonal = upper + jnp.swapaxes(upper, 1, 2)
    return picks.at[:, 0].set(diagonal).astype(jnp.int32)


def setup_inputs(seed: int = 0) -> dict:
    arg_keys = jax.random.split(jax.random.key(seed), 5)
    weights = draw_weights(jax.random.fold_in(arg_keys[4], 71), 0)
    edges = draw_edges(jax.random.fold_in(arg_keys[4], 71), 0)
    offsets = draw_offsets(jax.random.fold_in(arg_keys[4], 71), 0)
    counts = draw_counts(jax.random.fold_in(arg_keys[4], 71), 0)
    return {"weights": weights, "edges": edges, "offsets": offsets, "counts": counts}


def densify(row_tiles, row_offsets, row_count):
    listed = jnp.arange(row_tiles.shape[0]) < row_count
    onehot = ((row_offsets[:, None] == jnp.arange(BAND)[None, :]) & listed[:, None]).astype(jnp.float32)
    return jnp.einsum("lb,lij->bij", onehot, row_tiles, precision=lax.Precision.HIGHEST)


def band_products(banded, center):
    results = []
    for target in range(BAND):
        running = None
        for middle in range(-(BAND - 1), BAND):
            if middle >= 0:
                left_tile = banded[center + middle][middle]
            else:
                left_tile = banded[center + middle][-middle].T
            remote = target - middle
            if 0 <= remote < BAND:
                right_tile = banded[center + middle][remote]
            elif -BAND < remote < 0:
                right_tile = banded[center + target][-remote].T
            else:
                continue
            partial_value = jnp.dot(left_tile, right_tile, precision=lax.Precision.HIGHEST, preferred_element_type=jnp.float32)
            running = partial_value if running is None else running + partial_value
        results.append(running)
    return jnp.stack(results)


def slot_support(products, row_weighted, row_offsets, row_count):
    listed = jnp.arange(row_weighted.shape[0]) < row_count
    onehot = ((row_offsets[:, None] == jnp.arange(BAND)[None, :]) & listed[:, None]).astype(jnp.float32)
    chosen = jnp.einsum("ab,bij->aij", onehot, products, precision=lax.Precision.HIGHEST)
    return row_weighted * chosen


def reference(weights, edges, offsets, counts):
    weighted = weights * edges.astype(jnp.float32)
    margin = BAND - 1
    padded_tiles = jnp.pad(weighted, ((margin, margin), (0, 0), (0, 0), (0, 0)))
    padded_offsets = jnp.pad(offsets, ((margin, margin), (0, 0)))
    padded_counts = jnp.pad(counts, (margin, margin))

    def row_support(row_index):
        near_tiles = lax.dynamic_slice_in_dim(padded_tiles, row_index, 2 * BAND - 1, 0)
        near_offsets = lax.dynamic_slice_in_dim(padded_offsets, row_index, 2 * BAND - 1, 0)
        near_counts = lax.dynamic_slice_in_dim(padded_counts, row_index, 2 * BAND - 1, 0)
        banded = [densify(near_tiles[place], near_offsets[place], near_counts[place]) for place in range(2 * BAND - 1)]
        products = band_products(banded, margin)
        return slot_support(products, near_tiles[margin], near_offsets[margin], near_counts[margin])

    return lax.map(row_support, jnp.arange(NTR, dtype=jnp.int32))
```

```python
import functools

import jax
import jax.numpy as jnp
from jax import lax
from jax.experimental import pallas as pl
from jax.experimental.pallas import tpu as pltpu
from jax.sharding import PartitionSpec as P

BAND = 6
SLAB = BAND - 1
LANES = 128
AXES = ("row", "col")
MOST_BACK = 15
MOST_FORWARD = 9
SIZES = sorted(
    [(back, forward) for back in (4, 5, 6, 7, 8, 9, 10, 11, 12) for forward in (2, 3)]
    + [(8, 4), (10, 4), (13, 5), (MOST_BACK, MOST_FORWARD)],
    key=sum,
)
VMEM_LIMIT = 56 * 1024 * 1024

F32 = jnp.float32
BF16 = jnp.bfloat16
ANY = pl.BlockSpec(memory_space=pl.ANY)
SMEM = pl.BlockSpec(memory_space=pltpu.SMEM)
VMEM = pl.BlockSpec(memory_space=pltpu.VMEM)


def shifted(value, steps):
    count = lax.axis_size(AXES)
    first, last = (max(0, -steps), min(count, count - steps))
    return lax.ppermute(value, AXES, [(source, source + steps) for source in range(first, last)])


def split(value):
    high = value.astype(BF16)
    low = (value - high.astype(F32)).astype(BF16)
    return high, low


def dot(left, right):
    return jnp.dot(left, right, preferred_element_type=F32)


def product(left_high, left_low, right_high, right_low):
    return dot(left_high, right_high) + (dot(left_high, right_low) + dot(left_low, right_high))


def iotas(size):
    rows = lax.broadcasted_iota(jnp.int32, (size, size), 0)
    columns = lax.broadcasted_iota(jnp.int32, (size, size), 1)
    return rows, columns


def folded(tile):
    half = tile.shape[0] // 2
    rows, columns = iotas(half)
    lower_right = tile[half:, half:]
    mixed = jnp.where(rows <= columns, tile[:half, :half], lower_right)
    diagonal = jnp.sum(jnp.where(rows == columns, lower_right, 0.0), axis=0, keepdims=True)
    return mixed, tile[:half, half:], diagonal


def unfold(store, mixed, upper_right, diagonal):
    half = mixed.shape[0]
    rows, columns = iotas(half)
    turned = mixed.T
    store(0, 0, jnp.where(rows <= columns, mixed, turned))
    store(0, half, upper_right)
    store(half, 0, upper_right.T)
    lower_right = jnp.where(rows > columns, mixed, turned)
    store(half, half, jnp.where(rows == columns, diagonal, lower_right))


def slot_table(table, pattern, row, lists):
    for place in range(SLAB * BAND):
        table[place] = -1
    for slot in range(SLAB * lists):
        offset = pattern[row, slot]
        table[jnp.where(offset >= 0, slot // lists * BAND + offset, SLAB * BAND)] = slot


def listing(items, plan, row, first):
    count = jnp.int32(0)
    for i in range(SLAB):
        mask = plan[row, first + i]
        for bit in range(1, BAND):
            items[count] = i * BAND + bit
            count = count + ((mask >> bit) & 1)
    return count


def slot_copy(source, target, semaphore, slot, lists):
    return pltpu.make_async_copy(source.at[slot // lists, slot % lists], target.at[slot], semaphore)


def call(kernel, **kwargs):
    return pl.pallas_call(
        kernel,
        compiler_params=pltpu.CompilerParams(vmem_limit_bytes=VMEM_LIMIT),
        **kwargs,
    )


def fold_kernel(weights, edges, out):
    weighted = weights[0, 0] * edges[0, 0].astype(F32)
    half = weighted.shape[0] // 2
    mixed, upper_right, _ = folded(weighted)
    out[:, :half] = mixed
    out[:, half:] = upper_right


def fold_diagonals(weights, edges):
    tile = weights.shape[-1]
    block = pl.BlockSpec((1, 1, tile, tile), lambda i: (i, 0, 0, 0))
    return call(
        fold_kernel,
        grid=(SLAB,),
        in_specs=[block, block],
        out_specs=pl.BlockSpec((tile // 2, tile), lambda i: (i, 0)),
        out_shape=jax.ShapeDtypeStruct((SLAB * tile // 2, tile), F32),
    )(weights, edges)


def crossing_slot(pattern, row, slot, lists):
    offset = pattern[row, slot]
    return (offset >= 0) & (slot // lists + offset >= SLAB)


def square_kernel(lists, pattern, weights, edges, out, w, e, total, table, sems):
    tile = weights.shape[-1]
    half = tile // 2
    slot_table(table, pattern, 0, lists)

    @pl.loop(0, SLAB * lists)
    def _(slot):
        @pl.when(crossing_slot(pattern, 0, slot, lists))
        def _():
            slot_copy(weights, w, sems.at[0, slot], slot, lists).start()
            slot_copy(edges, e, sems.at[1, slot], slot, lists).start()

    out[SLAB * half :, :] = jnp.zeros((8, tile), F32)
    for j in range(SLAB):
        total[...] = jnp.zeros((tile, tile), F32)

        @pl.loop(j, SLAB)
        def _(i):
            slot = table[i * BAND + SLAB + j - i]

            @pl.when(slot >= 0)
            def _():
                slot_copy(weights, w, sems.at[0, slot], slot, lists).wait()
                slot_copy(edges, e, sems.at[1, slot], slot, lists).wait()
                value = w[slot] * e[slot].astype(F32)
                total[...] += product(*split(value.T), *split(value))

        mixed, upper_right, diagonal = folded(total[...])
        out[j * half : (j + 1) * half, :half] = mixed
        out[j * half : (j + 1) * half, half:] = upper_right
        out[SLAB * half + j : SLAB * half + j + 1, :half] = diagonal


def square_diagonals(pattern, weights, edges):
    _, lists, tile, _ = weights.shape
    return call(
        functools.partial(square_kernel, lists),
        in_specs=[SMEM, ANY, ANY],
        out_specs=VMEM,
        out_shape=jax.ShapeDtypeStruct((SLAB * tile // 2 + 8, tile), F32),
        scratch_shapes=[
            pltpu.VMEM((SLAB * lists, tile, tile), F32),
            pltpu.VMEM((SLAB * lists, tile, tile), jnp.int32),
            pltpu.VMEM((tile, tile), F32),
            pltpu.SMEM((SLAB * BAND + 1,), jnp.int32),
            pltpu.SemaphoreType.DMA((2, SLAB * lists)),
        ],
    )(pattern, weights, edges)


def plan_kernel(lists, patterns, plan, choice):
    offsets = patterns[...]
    slabs = offsets.shape[0]
    lane = lax.broadcasted_iota(jnp.int32, offsets.shape, 1)
    row = lax.broadcasted_iota(jnp.int32, offsets.shape, 0)
    inside = (offsets >= 0) & (lane < SLAB * lists)
    bits = jnp.where(inside, jnp.left_shift(1, jnp.maximum(offsets, 0)), 0)

    def ahead(value, steps):
        return pltpu.roll(value, LANES - steps, 1) if steps else value

    mask = bits
    for a in range(1, lists):
        mask = mask | ahead(bits, a)
    own = [ahead(mask, i * lists) for i in range(SLAB)]
    rows = own + [pltpu.roll(value, slabs - 1, 0) for value in own]

    def has(r, offset):
        return jnp.right_shift(rows[r], offset) & 1

    zero = jnp.zeros_like(mask)
    need = [zero] * SLAB
    for i in range(SLAB):
        for m in range(SLAB - i, BAND):
            middle = i + m
            wanted = zero
            for t in range(BAND):
                target = i + t
                if target >= SLAB:
                    other, offset = (middle, t - m) if m <= t else (target, m - t)
                    used = has(i, t) & has(middle, m) & has(other, offset)
                    wanted = wanted | used
                    if offset:
                        place = other - SLAB
                        need[place] = need[place] | jnp.left_shift(used, offset)
                elif m > t:
                    wanted = wanted | (has(i, t) & has(middle, m) & has(target, m - t))
            need[middle - SLAB] = need[middle - SLAB] | jnp.left_shift(wanted, m)
    crossing = [jnp.right_shift(jnp.left_shift(rows[i], i), SLAB) for i in range(SLAB)]
    partial = []
    for j in range(SLAB):
        cover = zero
        for i in range(SLAB):
            cover = cover | jnp.where(jnp.right_shift(crossing[i], j) & 1 == 1, crossing[i], 0)
        listed = jnp.left_shift(rows[SLAB + j], j) & ((1 << SLAB) - (2 << j))
        partial.append(cover & listed)
    both = need + partial
    result, counts = zero, []
    for group in (need, partial):
        count = zero
        for value in group:
            for bit in range(1, BAND):
                count = count + (jnp.right_shift(value, bit) & 1)
        count = jnp.where((lane == 0) & (row < slabs - 1), count, 0)
        counts.append(jnp.max(count.astype(F32)).astype(jnp.int32))
    for place, value in enumerate(both):
        value = pltpu.roll(value, place, 1) if place else value
        result = jnp.where((lane == place) & (row < slabs - 1), value, result)
    plan[...] = result
    back, forward = counts
    picked = jnp.int32(len(SIZES) - 1)
    for place in reversed(range(len(SIZES) - 1)):
        fits = (back <= SIZES[place][0]) & (forward <= SIZES[place][1])
        picked = jnp.where(fits, place, picked)
    choice[0] = picked


def travel_plan(patterns, lists):
    return call(
        functools.partial(plan_kernel, lists),
        in_specs=[VMEM],
        out_specs=[VMEM, SMEM],
        out_shape=[
            jax.ShapeDtypeStruct(patterns.shape, jnp.int32),
            jax.ShapeDtypeStruct((1,), jnp.int32),
        ],
    )(patterns)


def neighbours(place, plan):
    me = place[0]
    return me, jnp.where(me > 0, me - 1, plan.shape[0] - 1)


def pack_kernel(
    lists, place, plan, pattern, weights, edges, tiles_out, squares_out,
    w, e, total, table, raw, sums, needed, sems, tile_sem, total_sem,
):
    tile = weights.shape[-1]
    slots = SLAB * lists
    ahead, behind = neighbours(place, plan)
    slot_table(table, pattern, 0, lists)
    raw_count = listing(raw, plan, behind, 0)
    sum_count = listing(sums, plan, ahead, SLAB)

    for slot in range(slots + 1):
        needed[slot] = 0

    def factors(k, i):
        first = SLAB + sums[k] // BAND - i
        second = SLAB + sums[k] % BAND - i
        inside = (first < BAND) & (second < BAND)
        left = table[i * BAND + jnp.minimum(first, BAND - 1)]
        right = table[i * BAND + jnp.minimum(second, BAND - 1)]
        return left, right, inside & (left >= 0) & (right >= 0)

    @pl.loop(0, raw_count)
    def _(k):
        needed[table[raw[k]]] = 1

    @pl.loop(0, sum_count)
    def _(k):
        for i in range(SLAB):
            left, right, both = factors(k, i)
            needed[jnp.where(both, left, slots)] = 1
            needed[jnp.where(both, right, slots)] = 1

    @pl.loop(0, slots)
    def _(slot):
        @pl.when(needed[slot] == 1)
        def _():
            slot_copy(weights, w, sems.at[0, slot], slot, lists).start()
            slot_copy(edges, e, sems.at[1, slot], slot, lists).start()

    @pl.loop(0, slots)
    def _(slot):
        @pl.when(needed[slot] == 1)
        def _():
            slot_copy(weights, w, sems.at[0, slot], slot, lists).wait()
            slot_copy(edges, e, sems.at[1, slot], slot, lists).wait()
            w[slot] = w[slot] * e[slot].astype(F32)

    @pl.loop(0, raw_count)
    def _(k):
        pltpu.make_async_copy(w.at[table[raw[k]]], tiles_out.at[k], tile_sem).start()

    @pl.loop(0, sum_count)
    def _(k):
        total[k] = jnp.zeros((tile, tile), F32)

        @pl.loop(0, SLAB)
        def _(i):
            left, right, both = factors(k, i)

            @pl.when(both)
            def _():
                total[k] += product(*split(w[left].T), *split(w[right]))

        pltpu.make_async_copy(total.at[k], squares_out.at[k], total_sem).start()

    @pl.loop(0, raw_count)
    def _(k):
        pltpu.make_async_copy(w.at[0], tiles_out.at[k], tile_sem).wait()

    @pl.loop(0, sum_count)
    def _(k):
        pltpu.make_async_copy(total.at[k], squares_out.at[k], total_sem).wait()


def pack_tiles(place, plan, pattern, weights, edges):
    _, lists, tile, _ = weights.shape
    slots = SLAB * lists
    return call(
        functools.partial(pack_kernel, lists),
        in_specs=[SMEM, SMEM, SMEM, ANY, ANY],
        out_specs=[ANY, ANY],
        out_shape=[
            jax.ShapeDtypeStruct((MOST_BACK, tile, tile), F32),
            jax.ShapeDtypeStruct((MOST_FORWARD, tile, tile), F32),
        ],
        scratch_shapes=[
            pltpu.VMEM((slots, tile, tile), F32),
            pltpu.VMEM((slots, tile, tile), jnp.int32),
            pltpu.VMEM((MOST_FORWARD, tile, tile), F32),
            pltpu.SMEM((SLAB * BAND + 1,), jnp.int32),
            pltpu.SMEM((SLAB * BAND,), jnp.int32),
            pltpu.SMEM((SLAB * BAND,), jnp.int32),
            pltpu.SMEM((slots + 1,), jnp.int32),
            pltpu.SemaphoreType.DMA((2, slots)),
            pltpu.SemaphoreType.DMA,
            pltpu.SemaphoreType.DMA,
        ],
    )(place, plan, pattern, weights, edges)


def main_kernel(
    lists, pattern, weights, edges, squares, out,
    w, e, high, low, total, result, table, sems, out_sem,
):
    tile = weights.shape[-1]
    half = tile // 2
    slots = SLAB * lists
    slot_table(table, pattern, 0, lists)

    @pl.loop(0, slots)
    def _(slot):
        @pl.when(pattern[0, slot] >= 0)
        def _():
            slot_copy(weights, w, sems.at[0, slot], slot, lists).start()
            slot_copy(edges, e, sems.at[1, slot], slot, lists).start()

    @pl.loop(0, slots)
    def _(slot):
        @pl.when(pattern[0, slot] >= 0)
        def _():
            slot_copy(weights, w, sems.at[0, slot], slot, lists).wait()
            slot_copy(edges, e, sems.at[1, slot], slot, lists).wait()
            value = w[slot] * e[slot].astype(F32)
            w[slot] = value
            high[slot], low[slot] = split(value)

            @pl.when(pattern[0, slot] > 0)
            def _():
                high[slot + slots], low[slot + slots] = split(value.T)

    def own(row, offset):
        inside = (row >= 0) & (row < SLAB) & (offset >= 0) & (offset < BAND)
        return jnp.where(inside, table[jnp.where(inside, row * BAND + offset, 0)], -1)

    def turned(row, offset):
        slot = own(row, offset)
        return jnp.where(slot >= 0, slot + slots, -1)

    @pl.loop(0, slots)
    def _(slot):
        i = slot // lists
        offset = pattern[0, slot]

        @pl.when(offset > 0)
        def _():
            total[...] = jnp.zeros((tile, tile), F32)

        @pl.when(offset == 0)
        def _():
            def store(row, column, quarter):
                total[pl.ds(row, half), pl.ds(column, half)] = quarter

            part = squares[pl.ds(pl.multiple_of(i * half, half), half), :]
            rows = squares[SLAB * half :, :half]
            row = lax.broadcasted_iota(jnp.int32, rows.shape, 0)
            diagonal = jnp.sum(jnp.where(row == i, rows, 0.0), axis=0, keepdims=True)
            unfold(store, part[:, :half], part[:, half:], diagonal)

        @pl.when(offset >= 0)
        def _():
            @pl.loop(1 - BAND, BAND)
            def _(m):
                left = jnp.where(m < 0, turned(i + m, -m), own(i + m, m))
                right = jnp.where(
                    m <= offset, own(i + m, offset - m), turned(i + offset, m - offset)
                )

                @pl.when((left >= 0) & (right >= 0))
                def _():
                    total[...] += product(high[left], low[left], high[right], low[right])

            result[slot] = w[slot] * total[...]

        @pl.when(offset < 0)
        def _():
            result[slot] = jnp.zeros((tile, tile), F32)

        pltpu.make_async_copy(result.at[slot], out.at[i, slot % lists], out_sem).start()

    @pl.loop(0, slots)
    def _(slot):
        pltpu.make_async_copy(result.at[slot], out.at[slot // lists, slot % lists], out_sem).wait()


def main_part(pattern, weights, edges, squares):
    _, lists, tile, _ = weights.shape
    slots = SLAB * lists
    return call(
        functools.partial(main_kernel, lists),
        in_specs=[SMEM, ANY, ANY, VMEM],
        out_specs=ANY,
        out_shape=jax.ShapeDtypeStruct(weights.shape, F32),
        scratch_shapes=[
            pltpu.VMEM((slots, tile, tile), F32),
            pltpu.VMEM((slots, tile, tile), jnp.int32),
            pltpu.VMEM((2 * slots, tile, tile), BF16),
            pltpu.VMEM((2 * slots, tile, tile), BF16),
            pltpu.VMEM((tile, tile), F32),
            pltpu.VMEM((slots, tile, tile), F32),
            pltpu.SMEM((SLAB * BAND + 1,), jnp.int32),
            pltpu.SemaphoreType.DMA((2, slots)),
            pltpu.SemaphoreType.DMA,
        ],
        cost_estimate=pl.CostEstimate(
            flops=6 * 60 * tile**3, bytes_accessed=3 * weights.size * 4, transcendentals=0
        ),
    )(pattern, weights, edges, squares)


def rest_kernel(
    lists, place, plan, pattern, weights, edges, diagonals, tiles, squares, before, out,
    w, e, high, low, result, table, index, raw, sums, target, factor,
    job_slot, job_left, job_right, sems, out_sem,
):
    tile = weights.shape[-1]
    half = tile // 2
    slots = SLAB * lists
    back = tiles.shape[0]
    first_raw = slots + SLAB
    ahead, behind = neighbours(place, plan)
    slot_table(table, pattern, 0, lists)
    raw_count = listing(raw, plan, ahead, 0)
    sum_count = listing(sums, plan, behind, SLAB)

    for row in range(SLAB):
        index[row * BAND] = slots + row
        for offset in range(1, BAND):
            index[row * BAND + offset] = -1

    @pl.loop(0, raw_count)
    def _(k):
        index[raw[k]] = first_raw + k

    for slot in range(slots + 1):
        target[slot] = 0
        factor[slot] = 0

    def jobs_of(slot, count):
        i = slot // lists
        offset = pattern[0, slot]
        for m in range(1, BAND):
            row = i + m - SLAB
            left = index[jnp.maximum(row, 0) * BAND + m]
            column = i + offset
            straight = m <= offset
            gap = jnp.where(straight, offset - m, m - offset)
            later = straight | (column >= SLAB)
            next_row = jnp.where(straight, row, column - SLAB)
            theirs = index[jnp.clip(next_row, 0, SLAB - 1) * BAND + gap]
            theirs = jnp.where(straight | (theirs < 0), theirs, theirs + back)
            ours = table[jnp.clip(column, 0, SLAB - 1) * BAND + gap]
            right = jnp.where(later, theirs, ours)
            valid = (offset >= 0) & (row >= 0) & (left >= 0) & (right >= 0)
            job_slot[count] = slot
            job_left[count] = left
            job_right[count] = right
            target[jnp.where(valid, slot, slots)] = 1
            factor[jnp.where(valid & ~later, ours, slots)] = 1
            count = count + valid.astype(jnp.int32)
        return count

    jobs = lax.fori_loop(0, slots, jobs_of, jnp.int32(0))

    def sum_slot(k):
        return table[sums[k] // BAND * BAND + sums[k] % BAND - sums[k] // BAND]

    @pl.loop(0, sum_count)
    def _(k):
        target[sum_slot(k)] = 1

    def output(slot):
        return pltpu.make_async_copy(result.at[slot], out.at[slot // lists, slot % lists], out_sem)

    @pl.loop(0, slots)
    def _(slot):
        @pl.when(target[slot] + factor[slot] > 0)
        def _():
            slot_copy(weights, w, sems.at[0, slot], slot, lists).start()
            slot_copy(edges, e, sems.at[1, slot], slot, lists).start()

        @pl.when(target[slot] == 1)
        def _():
            slot_copy(before, result, sems.at[2, slot], slot, lists).start()

    for j in range(SLAB):

        def store(row, column, quarter, j=j):
            part = (slots + j, pl.ds(row, half), pl.ds(column, half))
            high[part], low[part] = split(quarter)

        rows = slice(j * half, (j + 1) * half)
        unfold(store, diagonals[rows, :half], diagonals[rows, half:], jnp.zeros((1, half), F32))

    @pl.loop(0, raw_count)
    def _(k):
        value = tiles[k]
        high[first_raw + k], low[first_raw + k] = split(value)
        high[first_raw + back + k], low[first_raw + back + k] = split(value.T)

    @pl.loop(0, slots)
    def _(slot):
        @pl.when(target[slot] + factor[slot] > 0)
        def _():
            slot_copy(weights, w, sems.at[0, slot], slot, lists).wait()
            slot_copy(edges, e, sems.at[1, slot], slot, lists).wait()
            w[slot] = w[slot] * e[slot].astype(F32)

        @pl.when(factor[slot] == 1)
        def _():
            high[slot], low[slot] = split(w[slot].T)

        @pl.when(target[slot] == 1)
        def _():
            slot_copy(before, result, sems.at[2, slot], slot, lists).wait()

    @pl.loop(0, sum_count)
    def _(k):
        slot = sum_slot(k)
        result[slot] += w[slot] * squares[k]

    @pl.loop(0, jobs)
    def _(job):
        slot, left, right = job_slot[job], job_left[job], job_right[job]
        value = product(high[left], low[left], high[right], low[right])
        result[slot] += w[slot] * value

    @pl.loop(0, slots)
    def _(slot):
        @pl.when(target[slot] == 1)
        def _():
            output(slot).start()

    @pl.loop(0, slots)
    def _(slot):
        @pl.when(target[slot] == 1)
        def _():
            output(slot).wait()


def rest_part(place, plan, pattern, weights, edges, diagonals, tiles, squares, before):
    _, lists, tile, _ = weights.shape
    slots = SLAB * lists
    factors = slots + SLAB + 2 * tiles.shape[0]
    jobs = pltpu.SMEM((slots * SLAB + 1,), jnp.int32)
    return call(
        functools.partial(rest_kernel, lists),
        in_specs=[SMEM, SMEM, SMEM, ANY, ANY, VMEM, VMEM, VMEM, ANY],
        out_specs=ANY,
        out_shape=jax.ShapeDtypeStruct(weights.shape, F32),
        input_output_aliases={8: 0},
        scratch_shapes=[
            pltpu.VMEM((slots, tile, tile), F32),
            pltpu.VMEM((slots, tile, tile), jnp.int32),
            pltpu.VMEM((factors, tile, tile), BF16),
            pltpu.VMEM((factors, tile, tile), BF16),
            pltpu.VMEM((slots, tile, tile), F32),
            pltpu.SMEM((SLAB * BAND + 1,), jnp.int32),
            pltpu.SMEM((SLAB * BAND,), jnp.int32),
            pltpu.SMEM((SLAB * BAND,), jnp.int32),
            pltpu.SMEM((SLAB * BAND,), jnp.int32),
            pltpu.SMEM((slots + 1,), jnp.int32),
            pltpu.SMEM((slots + 1,), jnp.int32),
            jobs,
            jobs,
            jobs,
            pltpu.SemaphoreType.DMA((3, slots)),
            pltpu.SemaphoreType.DMA,
        ],
    )(place, plan, pattern, weights, edges, diagonals, tiles, squares, before)


def shards(weights, edges, offsets, counts):
    slab_count, lists = offsets.shape
    place = lax.axis_index(AXES).astype(jnp.int32).reshape(1)
    listed = jnp.arange(lists)[None, :] < counts[:, None]
    pattern = jnp.where(listed, offsets, -1).reshape(1, slab_count * lists)
    pattern = jnp.pad(pattern, ((0, 0), (0, LANES - slab_count * lists)), constant_values=-1)
    patterns = lax.all_gather(pattern, AXES, axis=0, tiled=True)

    diagonals = shifted(fold_diagonals(weights, edges), -1)
    squares = shifted(square_diagonals(pattern, weights, edges), 1)

    plan, choice = travel_plan(patterns, lists)
    tiles_out, squares_out = pack_tiles(place, plan, pattern, weights, edges)

    def branch(back, forward):
        def run(place, plan, pattern, weights, edges, diagonals, squares, tiles_out, squares_out):
            tiles = shifted(tiles_out[:back], -1)
            more = shifted(squares_out[:forward], 1)
            support = main_part(pattern, weights, edges, squares)
            return rest_part(place, plan, pattern, weights, edges, diagonals, tiles, more, support)

        return run

    return lax.switch(
        choice[0],
        [branch(*sizes) for sizes in SIZES],
        place, plan, pattern, weights, edges, diagonals, squares, tiles_out, squares_out,
    )


def solution(mesh):
    in_specs = (
        P(AXES, None, None, None),
        P(AXES, None, None, None),
        P(AXES, None),
        P(AXES),
    )
    out_specs = P(AXES, None, None, None)
    return jax.shard_map(shards, mesh=mesh, in_specs=in_specs, out_specs=out_specs, check_vma=False)
```

```python
import functools

import jax
import jax.numpy as jnp
from jax import lax
from jax.experimental import pallas as pl
from jax.experimental.pallas import tpu as pltpu
from jax.sharding import PartitionSpec as P

BAND = 6
SLAB = BAND - 1
LANES = 128
AXES = ("row", "col")
SIZES = ((9, 3), (11, 4), (15, 9))
VMEM_LIMIT = 56 * 1024 * 1024

F32 = jnp.float32
BF16 = jnp.bfloat16
ANY = pl.BlockSpec(memory_space=pl.ANY)
SMEM = pl.BlockSpec(memory_space=pltpu.SMEM)
VMEM = pl.BlockSpec(memory_space=pltpu.VMEM)


def shifted(value, steps):
    count = lax.axis_size(AXES)
    first, last = (max(0, -steps), min(count, count - steps))
    return lax.ppermute(value, AXES, [(source, source + steps) for source in range(first, last)])


def split(value):
    high = value.astype(BF16)
    low = (value - high.astype(F32)).astype(BF16)
    return high, low


def dot(left, right):
    return jnp.dot(left, right, preferred_element_type=F32)


def product(left_high, left_low, right_high, right_low):
    return dot(left_high, right_high) + (dot(left_high, right_low) + dot(left_low, right_high))


def iotas(size):
    rows = lax.broadcasted_iota(jnp.int32, (size, size), 0)
    columns = lax.broadcasted_iota(jnp.int32, (size, size), 1)
    return rows, columns


def folded(tile):
    half = tile.shape[0] // 2
    rows, columns = iotas(half)
    lower_right = tile[half:, half:]
    mixed = jnp.where(rows <= columns, tile[:half, :half], lower_right)
    diagonal = jnp.sum(jnp.where(rows == columns, lower_right, 0.0), axis=0, keepdims=True)
    return mixed, tile[:half, half:], diagonal


def unfold(store, mixed, upper_right, diagonal):
    half = mixed.shape[0]
    rows, columns = iotas(half)
    turned = mixed.T
    store(0, 0, jnp.where(rows <= columns, mixed, turned))
    store(0, half, upper_right)
    store(half, 0, upper_right.T)
    lower_right = jnp.where(rows > columns, mixed, turned)
    store(half, half, jnp.where(rows == columns, diagonal, lower_right))


def slot_table(table, pattern, row, lists):
    for place in range(SLAB * BAND):
        table[place] = -1
    for slot in range(SLAB * lists):
        offset = pattern[row, slot]
        table[jnp.where(offset >= 0, slot // lists * BAND + offset, SLAB * BAND)] = slot


def listing(items, plan, row, first):
    count = jnp.int32(0)
    for i in range(SLAB):
        mask = plan[row, first + i]
        for bit in range(1, BAND):
            items[count] = i * BAND + bit
            count = count + ((mask >> bit) & 1)
    return count


def slot_copy(source, target, semaphore, slot, lists):
    return pltpu.make_async_copy(source.at[slot // lists, slot % lists], target.at[slot], semaphore)


def call(kernel, **kwargs):
    return pl.pallas_call(
        kernel,
        compiler_params=pltpu.CompilerParams(vmem_limit_bytes=VMEM_LIMIT),
        **kwargs,
    )


def fold_kernel(weights, edges, out):
    weighted = weights[0, 0] * edges[0, 0].astype(F32)
    half = weighted.shape[0] // 2
    mixed, upper_right, _ = folded(weighted)
    out[:, :half] = mixed
    out[:, half:] = upper_right


def fold_diagonals(weights, edges):
    tile = weights.shape[-1]
    block = pl.BlockSpec((1, 1, tile, tile), lambda i: (i, 0, 0, 0))
    return call(
        fold_kernel,
        grid=(SLAB,),
        in_specs=[block, block],
        out_specs=pl.BlockSpec((tile // 2, tile), lambda i: (i, 0)),
        out_shape=jax.ShapeDtypeStruct((SLAB * tile // 2, tile), F32),
    )(weights, edges)


def crossing_slot(pattern, row, slot, lists):
    offset = pattern[row, slot]
    return (offset >= 0) & (slot // lists + offset >= SLAB)


def square_kernel(lists, pattern, weights, edges, out, w, e, total, table, sems):
    tile = weights.shape[-1]
    half = tile // 2
    slot_table(table, pattern, 0, lists)

    @pl.loop(0, SLAB * lists)
    def _(slot):
        @pl.when(crossing_slot(pattern, 0, slot, lists))
        def _():
            slot_copy(weights, w, sems.at[0, slot], slot, lists).start()
            slot_copy(edges, e, sems.at[1, slot], slot, lists).start()

    out[SLAB * half :, :] = jnp.zeros((8, tile), F32)
    for j in range(SLAB):
        total[...] = jnp.zeros((tile, tile), F32)

        @pl.loop(j, SLAB)
        def _(i):
            slot = table[i * BAND + SLAB + j - i]

            @pl.when(slot >= 0)
            def _():
                slot_copy(weights, w, sems.at[0, slot], slot, lists).wait()
                slot_copy(edges, e, sems.at[1, slot], slot, lists).wait()
                value = w[slot] * e[slot].astype(F32)
                total[...] += product(*split(value.T), *split(value))

        mixed, upper_right, diagonal = folded(total[...])
        out[j * half : (j + 1) * half, :half] = mixed
        out[j * half : (j + 1) * half, half:] = upper_right
        out[SLAB * half + j : SLAB * half + j + 1, :half] = diagonal


def square_diagonals(pattern, weights, edges):
    _, lists, tile, _ = weights.shape
    return call(
        functools.partial(square_kernel, lists),
        in_specs=[SMEM, ANY, ANY],
        out_specs=VMEM,
        out_shape=jax.ShapeDtypeStruct((SLAB * tile // 2 + 8, tile), F32),
        scratch_shapes=[
            pltpu.VMEM((SLAB * lists, tile, tile), F32),
            pltpu.VMEM((SLAB * lists, tile, tile), jnp.int32),
            pltpu.VMEM((tile, tile), F32),
            pltpu.SMEM((SLAB * BAND + 1,), jnp.int32),
            pltpu.SemaphoreType.DMA((2, SLAB * lists)),
        ],
    )(pattern, weights, edges)


def plan_kernel(lists, patterns, plan, choice):
    offsets = patterns[...]
    slabs = offsets.shape[0]
    lane = lax.broadcasted_iota(jnp.int32, offsets.shape, 1)
    row = lax.broadcasted_iota(jnp.int32, offsets.shape, 0)
    inside = (offsets >= 0) & (lane < SLAB * lists)
    bits = jnp.where(inside, jnp.left_shift(1, jnp.maximum(offsets, 0)), 0)

    def ahead(value, steps):
        return pltpu.roll(value, LANES - steps, 1) if steps else value

    mask = bits
    for a in range(1, lists):
        mask = mask | ahead(bits, a)
    own = [ahead(mask, i * lists) for i in range(SLAB)]
    rows = own + [pltpu.roll(value, slabs - 1, 0) for value in own]

    def has(r, offset):
        return jnp.right_shift(rows[r], offset) & 1

    zero = jnp.zeros_like(mask)
    need = [zero] * SLAB
    for i in range(SLAB):
        for m in range(SLAB - i, BAND):
            middle = i + m
            wanted = zero
            for t in range(BAND):
                target = i + t
                if target >= SLAB:
                    other, offset = (middle, t - m) if m <= t else (target, m - t)
                    used = has(i, t) & has(middle, m) & has(other, offset)
                    wanted = wanted | used
                    if offset:
                        place = other - SLAB
                        need[place] = need[place] | jnp.left_shift(used, offset)
                elif m > t:
                    wanted = wanted | (has(i, t) & has(middle, m) & has(target, m - t))
            need[middle - SLAB] = need[middle - SLAB] | jnp.left_shift(wanted, m)
    crossing = [jnp.right_shift(jnp.left_shift(rows[i], i), SLAB) for i in range(SLAB)]
    partial = []
    for j in range(SLAB):
        cover = zero
        for i in range(SLAB):
            cover = cover | jnp.where(jnp.right_shift(crossing[i], j) & 1 == 1, crossing[i], 0)
        listed = jnp.left_shift(rows[SLAB + j], j) & ((1 << SLAB) - (2 << j))
        partial.append(cover & listed)
    both = need + partial
    result, counts = zero, []
    for group in (need, partial):
        count = zero
        for value in group:
            for bit in range(1, BAND):
                count = count + (jnp.right_shift(value, bit) & 1)
        count = jnp.where((lane == 0) & (row < slabs - 1), count, 0)
        counts.append(jnp.max(count.astype(F32)).astype(jnp.int32))
    for place, value in enumerate(both):
        value = pltpu.roll(value, place, 1) if place else value
        result = jnp.where((lane == place) & (row < slabs - 1), value, result)
    plan[...] = result
    back, forward = counts
    level = jnp.int32(0)
    for most_back, most_forward in SIZES[:-1]:
        level = level + ((back > most_back) | (forward > most_forward)).astype(jnp.int32)
    choice[0] = level


def travel_plan(patterns, lists):
    return call(
        functools.partial(plan_kernel, lists),
        in_specs=[VMEM],
        out_specs=[VMEM, SMEM],
        out_shape=[
            jax.ShapeDtypeStruct(patterns.shape, jnp.int32),
            jax.ShapeDtypeStruct((1,), jnp.int32),
        ],
    )(patterns)


BEHIND, AHEAD = 0, 1


def pack_kernel(
    lists, plan, pattern, weights, edges, tiles_out, squares_out, more_tiles_out, more_squares_out,
    w, e, total, table, raw, sums, needed, sems, tile_sem, total_sem,
):
    tile = weights.shape[-1]
    slots = SLAB * lists
    slot_table(table, pattern, 0, lists)
    raw_count = listing(raw, plan, BEHIND, 0)
    sum_count = listing(sums, plan, AHEAD, SLAB)

    for slot in range(slots + 1):
        needed[slot] = 0

    def factors(k, i):
        first = SLAB + sums[k] // BAND - i
        second = SLAB + sums[k] % BAND - i
        inside = (first < BAND) & (second < BAND)
        left = table[i * BAND + jnp.minimum(first, BAND - 1)]
        right = table[i * BAND + jnp.minimum(second, BAND - 1)]
        return left, right, inside & (left >= 0) & (right >= 0)

    @pl.loop(0, raw_count)
    def _(k):
        needed[table[raw[k]]] = 1

    @pl.loop(0, sum_count)
    def _(k):
        for i in range(SLAB):
            left, right, both = factors(k, i)
            needed[jnp.where(both, left, slots)] = 1
            needed[jnp.where(both, right, slots)] = 1

    @pl.loop(0, slots)
    def _(slot):
        @pl.when(needed[slot] == 1)
        def _():
            slot_copy(weights, w, sems.at[0, slot], slot, lists).start()
            slot_copy(edges, e, sems.at[1, slot], slot, lists).start()

    @pl.loop(0, slots)
    def _(slot):
        @pl.when(needed[slot] == 1)
        def _():
            slot_copy(weights, w, sems.at[0, slot], slot, lists).wait()
            slot_copy(edges, e, sems.at[1, slot], slot, lists).wait()
            w[slot] = w[slot] * e[slot].astype(F32)

    def send(source, first, more, k, semaphore):
        held = first.shape[0]

        @pl.when(k < held)
        def _():
            pltpu.make_async_copy(source, first.at[k], semaphore).start()

        @pl.when(k >= held)
        def _():
            pltpu.make_async_copy(source, more.at[k - held], semaphore).start()

    @pl.loop(0, raw_count)
    def _(k):
        send(w.at[table[raw[k]]], tiles_out, more_tiles_out, k, tile_sem)

    @pl.loop(0, sum_count)
    def _(k):
        total[k] = jnp.zeros((tile, tile), F32)

        @pl.loop(0, SLAB)
        def _(i):
            left, right, both = factors(k, i)

            @pl.when(both)
            def _():
                total[k] += product(*split(w[left].T), *split(w[right]))

        send(total.at[k], squares_out, more_squares_out, k, total_sem)

    @pl.loop(0, raw_count)
    def _(k):
        pltpu.make_async_copy(w.at[0], tiles_out.at[0], tile_sem).wait()

    @pl.loop(0, sum_count)
    def _(k):
        pltpu.make_async_copy(total.at[k], squares_out.at[0], total_sem).wait()


def pack_tiles(plan, pattern, weights, edges):
    _, lists, tile, _ = weights.shape
    slots = SLAB * lists
    (back, forward), (most_back, most_forward) = SIZES[0], SIZES[-1]

    def tiles(count):
        return jax.ShapeDtypeStruct((count, tile, tile), F32)

    return call(
        functools.partial(pack_kernel, lists),
        in_specs=[SMEM, SMEM, ANY, ANY],
        out_specs=[ANY] * 4,
        out_shape=[
            tiles(back), tiles(forward), tiles(most_back - back), tiles(most_forward - forward),
        ],
        scratch_shapes=[
            pltpu.VMEM((slots, tile, tile), F32),
            pltpu.VMEM((slots, tile, tile), jnp.int32),
            pltpu.VMEM((most_forward, tile, tile), F32),
            pltpu.SMEM((SLAB * BAND + 1,), jnp.int32),
            pltpu.SMEM((SLAB * BAND,), jnp.int32),
            pltpu.SMEM((SLAB * BAND,), jnp.int32),
            pltpu.SMEM((slots + 1,), jnp.int32),
            pltpu.SemaphoreType.DMA((2, slots)),
            pltpu.SemaphoreType.DMA,
            pltpu.SemaphoreType.DMA,
        ],
    )(plan, pattern, weights, edges)


def main_kernel(
    lists, pattern, weights, edges, squares, out,
    w, e, high, low, total, result, table, sems, out_sem,
):
    tile = weights.shape[-1]
    half = tile // 2
    slots = SLAB * lists
    slot_table(table, pattern, 0, lists)

    @pl.loop(0, slots)
    def _(slot):
        @pl.when(pattern[0, slot] >= 0)
        def _():
            slot_copy(weights, w, sems.at[0, slot], slot, lists).start()
            slot_copy(edges, e, sems.at[1, slot], slot, lists).start()

    @pl.loop(0, slots)
    def _(slot):
        @pl.when(pattern[0, slot] >= 0)
        def _():
            slot_copy(weights, w, sems.at[0, slot], slot, lists).wait()
            slot_copy(edges, e, sems.at[1, slot], slot, lists).wait()
            value = w[slot] * e[slot].astype(F32)
            w[slot] = value
            high[slot], low[slot] = split(value)

            @pl.when(pattern[0, slot] > 0)
            def _():
                high[slot + slots], low[slot + slots] = split(value.T)

    def own(row, offset):
        inside = (row >= 0) & (row < SLAB) & (offset >= 0) & (offset < BAND)
        return jnp.where(inside, table[jnp.where(inside, row * BAND + offset, 0)], -1)

    def turned(row, offset):
        slot = own(row, offset)
        return jnp.where(slot >= 0, slot + slots, -1)

    @pl.loop(0, slots)
    def _(slot):
        i = slot // lists
        offset = pattern[0, slot]

        @pl.when(offset > 0)
        def _():
            total[...] = jnp.zeros((tile, tile), F32)

        @pl.when(offset == 0)
        def _():
            def store(row, column, quarter):
                total[pl.ds(row, half), pl.ds(column, half)] = quarter

            part = squares[pl.ds(pl.multiple_of(i * half, half), half), :]
            rows = squares[SLAB * half :, :half]
            row = lax.broadcasted_iota(jnp.int32, rows.shape, 0)
            diagonal = jnp.sum(jnp.where(row == i, rows, 0.0), axis=0, keepdims=True)
            unfold(store, part[:, :half], part[:, half:], diagonal)

        @pl.when(offset >= 0)
        def _():
            @pl.loop(1 - BAND, BAND)
            def _(m):
                left = jnp.where(m < 0, turned(i + m, -m), own(i + m, m))
                right = jnp.where(
                    m <= offset, own(i + m, offset - m), turned(i + offset, m - offset)
                )

                @pl.when((left >= 0) & (right >= 0))
                def _():
                    total[...] += product(high[left], low[left], high[right], low[right])

            result[slot] = w[slot] * total[...]

        @pl.when(offset < 0)
        def _():
            result[slot] = jnp.zeros((tile, tile), F32)

        pltpu.make_async_copy(result.at[slot], out.at[i, slot % lists], out_sem).start()

    @pl.loop(0, slots)
    def _(slot):
        pltpu.make_async_copy(result.at[slot], out.at[slot // lists, slot % lists], out_sem).wait()


def main_part(pattern, weights, edges, squares):
    _, lists, tile, _ = weights.shape
    slots = SLAB * lists
    return call(
        functools.partial(main_kernel, lists),
        in_specs=[SMEM, ANY, ANY, VMEM],
        out_specs=ANY,
        out_shape=jax.ShapeDtypeStruct(weights.shape, F32),
        scratch_shapes=[
            pltpu.VMEM((slots, tile, tile), F32),
            pltpu.VMEM((slots, tile, tile), jnp.int32),
            pltpu.VMEM((2 * slots, tile, tile), BF16),
            pltpu.VMEM((2 * slots, tile, tile), BF16),
            pltpu.VMEM((tile, tile), F32),
            pltpu.VMEM((slots, tile, tile), F32),
            pltpu.SMEM((SLAB * BAND + 1,), jnp.int32),
            pltpu.SemaphoreType.DMA((2, slots)),
            pltpu.SemaphoreType.DMA,
        ],
        cost_estimate=pl.CostEstimate(
            flops=6 * 60 * tile**3, bytes_accessed=3 * weights.size * 4, transcendentals=0
        ),
    )(pattern, weights, edges, squares)


def rest_kernel(
    lists, done, plan, pattern, weights, edges, diagonals, tiles, squares, before, out,
    w, e, high, low, result, table, index, raw, sums, target, factor,
    job_slot, job_left, job_right, sems, out_sem,
):
    tile = weights.shape[-1]
    half = tile // 2
    slots = SLAB * lists
    back = tiles.shape[0]
    first_raw = slots + SLAB
    done_back, done_forward = done
    slot_table(table, pattern, 0, lists)
    raw_count = listing(raw, plan, AHEAD, 0)
    sum_count = listing(sums, plan, BEHIND, SLAB)

    for row in range(SLAB):
        index[row * BAND] = slots + row
        for offset in range(1, BAND):
            index[row * BAND + offset] = -1

    raw_count = jnp.minimum(raw_count, back)
    sum_count = jnp.minimum(sum_count, squares.shape[0])

    @pl.loop(0, raw_count)
    def _(k):
        index[raw[k]] = first_raw + k

    for slot in range(slots + 1):
        target[slot] = 0
        factor[slot] = 0

    def jobs_of(slot, count):
        i = slot // lists
        offset = pattern[0, slot]
        for m in range(1, BAND):
            row = i + m - SLAB
            left = index[jnp.maximum(row, 0) * BAND + m]
            column = i + offset
            straight = m <= offset
            gap = jnp.where(straight, offset - m, m - offset)
            later = straight | (column >= SLAB)
            next_row = jnp.where(straight, row, column - SLAB)
            theirs = index[jnp.clip(next_row, 0, SLAB - 1) * BAND + gap]
            fresh = first_raw + done_back
            new = (left >= fresh) | (later & (theirs >= fresh)) | (done_back == 0)
            theirs = jnp.where(straight | (theirs < 0), theirs, theirs + back)
            ours = table[jnp.clip(column, 0, SLAB - 1) * BAND + gap]
            right = jnp.where(later, theirs, ours)
            valid = (offset >= 0) & (row >= 0) & (left >= 0) & (right >= 0) & new
            job_slot[count] = slot
            job_left[count] = left
            job_right[count] = right
            target[jnp.where(valid, slot, slots)] = 1
            factor[jnp.where(valid & ~later, ours, slots)] = 1
            count = count + valid.astype(jnp.int32)
        return count

    jobs = lax.fori_loop(0, slots, jobs_of, jnp.int32(0))

    def sum_slot(k):
        return table[sums[k] // BAND * BAND + sums[k] % BAND - sums[k] // BAND]

    @pl.loop(done_forward, sum_count)
    def _(k):
        target[sum_slot(k)] = 1

    def output(slot):
        return pltpu.make_async_copy(result.at[slot], out.at[slot // lists, slot % lists], out_sem)

    @pl.loop(0, slots)
    def _(slot):
        @pl.when(target[slot] + factor[slot] > 0)
        def _():
            slot_copy(weights, w, sems.at[0, slot], slot, lists).start()
            slot_copy(edges, e, sems.at[1, slot], slot, lists).start()

        @pl.when(target[slot] == 1)
        def _():
            slot_copy(before, result, sems.at[2, slot], slot, lists).start()

    for j in range(SLAB):

        def store(row, column, quarter, j=j):
            part = (slots + j, pl.ds(row, half), pl.ds(column, half))
            high[part], low[part] = split(quarter)

        rows = slice(j * half, (j + 1) * half)
        unfold(store, diagonals[rows, :half], diagonals[rows, half:], jnp.zeros((1, half), F32))

    @pl.loop(0, raw_count)
    def _(k):
        value = tiles[k]
        high[first_raw + k], low[first_raw + k] = split(value)
        high[first_raw + back + k], low[first_raw + back + k] = split(value.T)

    @pl.loop(0, slots)
    def _(slot):
        @pl.when(target[slot] + factor[slot] > 0)
        def _():
            slot_copy(weights, w, sems.at[0, slot], slot, lists).wait()
            slot_copy(edges, e, sems.at[1, slot], slot, lists).wait()
            w[slot] = w[slot] * e[slot].astype(F32)

        @pl.when(factor[slot] == 1)
        def _():
            high[slot], low[slot] = split(w[slot].T)

        @pl.when(target[slot] == 1)
        def _():
            slot_copy(before, result, sems.at[2, slot], slot, lists).wait()

    @pl.loop(done_forward, sum_count)
    def _(k):
        slot = sum_slot(k)
        result[slot] += w[slot] * squares[k]

    @pl.loop(0, jobs)
    def _(job):
        slot, left, right = job_slot[job], job_left[job], job_right[job]
        value = product(high[left], low[left], high[right], low[right])
        result[slot] += w[slot] * value

    @pl.loop(0, slots)
    def _(slot):
        @pl.when(target[slot] == 1)
        def _():
            output(slot).start()

    @pl.loop(0, slots)
    def _(slot):
        @pl.when(target[slot] == 1)
        def _():
            output(slot).wait()


def rest_part(done, plan, pattern, weights, edges, diagonals, tiles, squares, before):
    _, lists, tile, _ = weights.shape
    slots = SLAB * lists
    factors = slots + SLAB + 2 * tiles.shape[0]
    jobs = pltpu.SMEM((slots * SLAB + 1,), jnp.int32)
    return call(
        functools.partial(rest_kernel, lists, done),
        in_specs=[SMEM, SMEM, ANY, ANY, VMEM, VMEM, VMEM, ANY],
        out_specs=ANY,
        out_shape=jax.ShapeDtypeStruct(weights.shape, F32),
        input_output_aliases={7: 0},
        scratch_shapes=[
            pltpu.VMEM((slots, tile, tile), F32),
            pltpu.VMEM((slots, tile, tile), jnp.int32),
            pltpu.VMEM((factors, tile, tile), BF16),
            pltpu.VMEM((factors, tile, tile), BF16),
            pltpu.VMEM((slots, tile, tile), F32),
            pltpu.SMEM((SLAB * BAND + 1,), jnp.int32),
            pltpu.SMEM((SLAB * BAND,), jnp.int32),
            pltpu.SMEM((SLAB * BAND,), jnp.int32),
            pltpu.SMEM((SLAB * BAND,), jnp.int32),
            pltpu.SMEM((slots + 1,), jnp.int32),
            pltpu.SMEM((slots + 1,), jnp.int32),
            jobs,
            jobs,
            jobs,
            pltpu.SemaphoreType.DMA((3, slots)),
            pltpu.SemaphoreType.DMA,
        ],
    )(plan, pattern, weights, edges, diagonals, tiles, squares, before)


def largest(value):
    columns = lax.axis_size(AXES[1])
    count = lax.axis_size(AXES)
    if count & (count - 1):
        return lax.pmax(value, AXES)
    bits = [1 << bit for bit in range(count.bit_length() - 1)]
    for bit in sorted(bits, key=lambda bit: (bit < columns, bit)):
        other = lax.ppermute(value, AXES, [(device, device ^ bit) for device in range(count)])
        value = jnp.maximum(value, other)
    return value


def shards(weights, edges, offsets, counts):
    slab_count, lists = offsets.shape
    listed = jnp.arange(lists)[None, :] < counts[:, None]
    pattern = jnp.where(listed, offsets, -1).reshape(1, slab_count * lists)
    pattern = jnp.pad(pattern, ((0, 0), (0, LANES - slab_count * lists)), constant_values=-1)
    empty = jnp.full((5, LANES), -1, jnp.int32)
    patterns = jnp.concatenate([shifted(pattern, 1), pattern, shifted(pattern, -1), empty])

    diagonals = shifted(fold_diagonals(weights, edges), -1)
    squares = shifted(square_diagonals(pattern, weights, edges), 1)

    plan, level = travel_plan(patterns, lists)
    tiles_out, sums_out, more_tiles_out, more_sums_out = pack_tiles(plan, pattern, weights, edges)
    tiles = shifted(tiles_out, -1)
    sums = shifted(sums_out, 1)
    support = main_part(pattern, weights, edges, squares)
    level, support = lax.optimization_barrier((level, support))
    level = largest(level)
    support = rest_part((0, 0), plan, pattern, weights, edges, diagonals, tiles, sums, support)

    def branch(back, forward):
        def run(support, plan, pattern, weights, edges, diagonals, tiles, sums, more_tiles, more_sums):
            if (back, forward) == SIZES[0]:
                return support
            more_tiles = shifted(more_tiles[: back - SIZES[0][0]], -1)
            more_sums = shifted(more_sums[: forward - SIZES[0][1]], 1)
            tiles = jnp.concatenate([tiles, more_tiles])
            sums = jnp.concatenate([sums, more_sums])
            return rest_part(SIZES[0], plan, pattern, weights, edges, diagonals, tiles, sums, support)

        return run

    return lax.switch(
        level[0],
        [branch(*sizes) for sizes in SIZES],
        support, plan, pattern, weights, edges, diagonals, tiles, sums, more_tiles_out, more_sums_out,
    )


def solution(mesh):
    in_specs = (
        P(AXES, None, None, None),
        P(AXES, None, None, None),
        P(AXES, None),
        P(AXES),
    )
    out_specs = P(AXES, None, None, None)
    return jax.shard_map(shards, mesh=mesh, in_specs=in_specs, out_specs=out_specs, check_vma=False)
```

```python
import functools

import jax
import jax.numpy as jnp
from jax import lax
from jax.experimental import pallas as pl
from jax.experimental.pallas import tpu as pltpu
from jax.sharding import PartitionSpec as P

BAND = 6
SLAB = BAND - 1
LANES = 128
AXES = ("row", "col")
BACK, FORWARD = 10, 3
MORE = ((0, 0), (2, 1), (8, 6))
BEHIND, AHEAD = 0, 1
JOBS, RAWS, SUMS, DIAGONALS = 0, 1, 2, 3
TARGET, FACTOR, TURNED, PLACE, SUM_SLOT, DIAGONAL = 8, 32, 64, 96, 128, 144
JOB_SLOT, JOB_LEFT, JOB_RIGHT, LIST_SIZE = 160, 272, 384, 512
VMEM_LIMIT = 56 * 1024 * 1024

F32 = jnp.float32
BF16 = jnp.bfloat16
ANY = pl.BlockSpec(memory_space=pl.ANY)
SMEM = pl.BlockSpec(memory_space=pltpu.SMEM)
VMEM = pl.BlockSpec(memory_space=pltpu.VMEM)


def shifted(value, steps):
    count = lax.axis_size(AXES)
    first, last = (max(0, -steps), min(count, count - steps))
    return lax.ppermute(value, AXES, [(source, source + steps) for source in range(first, last)])


def split(value):
    high = value.astype(BF16)
    low = (value - high.astype(F32)).astype(BF16)
    return high, low


def dot(left, right):
    return jnp.dot(left, right, preferred_element_type=F32)


def product(left_high, left_low, right_high, right_low):
    return dot(left_high, right_high) + (dot(left_high, right_low) + dot(left_low, right_high))


def iotas(size):
    rows = lax.broadcasted_iota(jnp.int32, (size, size), 0)
    columns = lax.broadcasted_iota(jnp.int32, (size, size), 1)
    return rows, columns


def folded(tile):
    half = tile.shape[0] // 2
    rows, columns = iotas(half)
    lower_right = tile[half:, half:]
    mixed = jnp.where(rows <= columns, tile[:half, :half], lower_right)
    diagonal = jnp.sum(jnp.where(rows == columns, lower_right, 0.0), axis=0, keepdims=True)
    return mixed, tile[:half, half:], diagonal


def unfold(store, mixed, upper_right, diagonal):
    half = mixed.shape[0]
    rows, columns = iotas(half)
    turned = mixed.T
    store(0, 0, jnp.where(rows <= columns, mixed, turned))
    store(0, half, upper_right)
    store(half, 0, upper_right.T)
    lower_right = jnp.where(rows > columns, mixed, turned)
    store(half, half, jnp.where(rows == columns, diagonal, lower_right))


def slot_table(table, pattern, row, lists):
    for place in range(SLAB * BAND):
        table[place] = -1
    for slot in range(SLAB * lists):
        offset = pattern[row, slot]
        table[jnp.where(offset >= 0, slot // lists * BAND + offset, SLAB * BAND)] = slot


def listing(items, plan, row, first):
    count = jnp.int32(0)
    for i in range(SLAB):
        mask = plan[row, first + i]
        for bit in range(1, BAND):
            items[count] = i * BAND + bit
            count = count + ((mask >> bit) & 1)
    return count


def diagonals_needed(items, first, plan, row):
    count = jnp.int32(0)
    for i in range(SLAB):
        items[first + count] = i
        count = count + (plan[row, i] & 1)
    return count


def slot_copy(source, target, semaphore, slot, lists):
    return pltpu.make_async_copy(source.at[slot // lists, slot % lists], target.at[slot], semaphore)


def call(kernel, **kwargs):
    return pl.pallas_call(
        kernel,
        compiler_params=pltpu.CompilerParams(vmem_limit_bytes=VMEM_LIMIT),
        **kwargs,
    )


def crossing_slot(pattern, row, slot, lists):
    offset = pattern[row, slot]
    return (offset >= 0) & (slot // lists + offset >= SLAB)


def square_kernel(lists, pattern, weights, edges, out, w, e, total, table, sems):
    tile = weights.shape[-1]
    half = tile // 2
    slot_table(table, pattern, 0, lists)

    @pl.loop(0, SLAB * lists)
    def _(slot):
        @pl.when(crossing_slot(pattern, 0, slot, lists))
        def _():
            slot_copy(weights, w, sems.at[0, slot], slot, lists).start()
            slot_copy(edges, e, sems.at[1, slot], slot, lists).start()

    out[SLAB * half :, :] = jnp.zeros((8, tile), F32)
    for j in range(SLAB):
        total[...] = jnp.zeros((tile, tile), F32)

        @pl.loop(j, SLAB)
        def _(i):
            slot = table[i * BAND + SLAB + j - i]

            @pl.when(slot >= 0)
            def _():
                slot_copy(weights, w, sems.at[0, slot], slot, lists).wait()
                slot_copy(edges, e, sems.at[1, slot], slot, lists).wait()
                value = w[slot] * e[slot].astype(F32)
                total[...] += product(*split(value.T), *split(value))

        mixed, upper_right, diagonal = folded(total[...])
        out[j * half : (j + 1) * half, :half] = mixed
        out[j * half : (j + 1) * half, half:] = upper_right
        out[SLAB * half + j : SLAB * half + j + 1, :half] = diagonal


def square_diagonals(pattern, weights, edges):
    _, lists, tile, _ = weights.shape
    return call(
        functools.partial(square_kernel, lists),
        in_specs=[SMEM, ANY, ANY],
        out_specs=VMEM,
        out_shape=jax.ShapeDtypeStruct((SLAB * tile // 2 + 8, tile), F32),
        scratch_shapes=[
            pltpu.VMEM((SLAB * lists, tile, tile), F32),
            pltpu.VMEM((SLAB * lists, tile, tile), jnp.int32),
            pltpu.VMEM((tile, tile), F32),
            pltpu.SMEM((SLAB * BAND + 1,), jnp.int32),
            pltpu.SemaphoreType.DMA((2, SLAB * lists)),
        ],
    )(pattern, weights, edges)


def plan_kernel(lists, patterns, plan, choice):
    offsets = patterns[...]
    slabs = offsets.shape[0]
    lane = lax.broadcasted_iota(jnp.int32, offsets.shape, 1)
    row = lax.broadcasted_iota(jnp.int32, offsets.shape, 0)
    inside = (offsets >= 0) & (lane < SLAB * lists)
    bits = jnp.where(inside, jnp.left_shift(1, jnp.maximum(offsets, 0)), 0)

    def ahead(value, steps):
        return pltpu.roll(value, LANES - steps, 1) if steps else value

    mask = bits
    for a in range(1, lists):
        mask = mask | ahead(bits, a)
    own = [ahead(mask, i * lists) for i in range(SLAB)]
    rows = own + [pltpu.roll(value, slabs - 1, 0) for value in own]

    def has(r, offset):
        return jnp.right_shift(rows[r], offset) & 1

    zero = jnp.zeros_like(mask)
    need = [zero] * SLAB
    for i in range(SLAB):
        for m in range(SLAB - i, BAND):
            middle = i + m
            wanted = zero
            for t in range(BAND):
                target = i + t
                if target >= SLAB:
                    other, offset = (middle, t - m) if m <= t else (target, m - t)
                    used = has(i, t) & has(middle, m) & has(other, offset)
                    wanted = wanted | used
                    place = other - SLAB
                    need[place] = need[place] | jnp.left_shift(used, offset)
                elif m > t:
                    wanted = wanted | (has(i, t) & has(middle, m) & has(target, m - t))
            need[middle - SLAB] = need[middle - SLAB] | jnp.left_shift(wanted, m)
    crossing = [jnp.right_shift(jnp.left_shift(rows[i], i), SLAB) for i in range(SLAB)]
    partial = []
    for j in range(SLAB):
        cover = zero
        for i in range(SLAB):
            cover = cover | jnp.where(jnp.right_shift(crossing[i], j) & 1 == 1, crossing[i], 0)
        listed = jnp.left_shift(rows[SLAB + j], j) & ((1 << SLAB) - (2 << j))
        partial.append(cover & listed)
    def total(group, bits):
        count = zero
        for value in group:
            for bit in bits:
                count = count + (jnp.right_shift(value, bit) & 1)
        return count

    room = jnp.right_shift(2 * BACK - total(need, (0,)), 1)
    extra = []
    for count in (total(need, range(1, BAND)) - room, total(partial, range(1, BAND)) - FORWARD):
        count = jnp.where((lane == 0) & (row < slabs - 1), count, 0)
        extra.append(jnp.max(count.astype(F32)).astype(jnp.int32))
    result = zero
    for place, value in enumerate(need + partial):
        value = pltpu.roll(value, place, 1) if place else value
        result = jnp.where((lane == place) & (row < slabs - 1), value, result)
    plan[...] = result
    level = jnp.int32(0)
    for back, forward in MORE[:-1]:
        level = level + ((extra[0] > back) | (extra[1] > forward)).astype(jnp.int32)
    choice[0] = level


def travel_plan(patterns, lists):
    return call(
        functools.partial(plan_kernel, lists),
        in_specs=[VMEM],
        out_specs=[VMEM, SMEM],
        out_shape=[
            jax.ShapeDtypeStruct(patterns.shape, jnp.int32),
            jax.ShapeDtypeStruct((1,), jnp.int32),
        ],
    )(patterns)


def pack_kernel(
    lists, plan, pattern, weights, edges, message, squares_out, more_tiles_out, more_squares_out,
    w, e, total, halves, table, raw, sums, diagonals, needed, sems, tile_sem, half_sem, total_sem,
):
    tile = weights.shape[-1]
    half = tile // 2
    slots = SLAB * lists
    slot_table(table, pattern, 0, lists)
    raw_count = listing(raw, plan, BEHIND, 0)
    sum_count = listing(sums, plan, AHEAD, SLAB)
    half_count = diagonals_needed(diagonals, 0, plan, BEHIND)
    room = lax.shift_right_logical(2 * BACK - half_count, 1)

    for slot in range(slots + 1):
        needed[slot] = 0

    def factors(k, i):
        first = SLAB + sums[k] // BAND - i
        second = SLAB + sums[k] % BAND - i
        inside = (first < BAND) & (second < BAND)
        left = table[i * BAND + jnp.minimum(first, BAND - 1)]
        right = table[i * BAND + jnp.minimum(second, BAND - 1)]
        return left, right, inside & (left >= 0) & (right >= 0)

    @pl.loop(0, raw_count)
    def _(k):
        needed[table[raw[k]]] = 1

    @pl.loop(0, half_count)
    def _(k):
        needed[table[diagonals[k] * BAND]] = 1

    @pl.loop(0, sum_count)
    def _(k):
        for i in range(SLAB):
            left, right, both = factors(k, i)
            needed[jnp.where(both, left, slots)] = 1
            needed[jnp.where(both, right, slots)] = 1

    @pl.loop(0, slots)
    def _(slot):
        @pl.when(needed[slot] == 1)
        def _():
            slot_copy(weights, w, sems.at[0, slot], slot, lists).start()
            slot_copy(edges, e, sems.at[1, slot], slot, lists).start()

    @pl.loop(0, slots)
    def _(slot):
        @pl.when(needed[slot] == 1)
        def _():
            slot_copy(weights, w, sems.at[0, slot], slot, lists).wait()
            slot_copy(edges, e, sems.at[1, slot], slot, lists).wait()
            w[slot] = w[slot] * e[slot].astype(F32)

    @pl.loop(0, raw_count)
    def _(k):
        source = w.at[table[raw[k]]]

        @pl.when(k < room)
        def _():
            rows = pl.ds(pl.multiple_of(k * tile, tile), tile)
            pltpu.make_async_copy(source, message.at[rows], tile_sem).start()

        @pl.when(k >= room)
        def _():
            rows = pl.ds(pl.multiple_of((k - room) * tile, tile), tile)
            pltpu.make_async_copy(source, more_tiles_out.at[rows], tile_sem).start()

    @pl.loop(0, half_count)
    def _(k):
        mixed, upper_right, _ = folded(w[table[diagonals[k] * BAND]])
        halves[k, :, :half] = mixed
        halves[k, :, half:] = upper_right
        rows = pl.ds(pl.multiple_of((2 * BACK - 1 - k) * half, half), half)
        pltpu.make_async_copy(halves.at[k], message.at[rows], half_sem).start()

    @pl.loop(0, sum_count)
    def _(k):
        total[k] = jnp.zeros((tile, tile), F32)

        @pl.loop(0, SLAB)
        def _(i):
            left, right, both = factors(k, i)

            @pl.when(both)
            def _():
                total[k] += product(*split(w[left].T), *split(w[right]))

        @pl.when(k < FORWARD)
        def _():
            pltpu.make_async_copy(total.at[k], squares_out.at[k], total_sem).start()

        @pl.when(k >= FORWARD)
        def _():
            target = more_squares_out.at[k - FORWARD]
            pltpu.make_async_copy(total.at[k], target, total_sem).start()

    @pl.loop(0, raw_count)
    def _(k):
        pltpu.make_async_copy(w.at[0], message.at[pl.ds(0, tile)], tile_sem).wait()

    @pl.loop(0, half_count)
    def _(k):
        pltpu.make_async_copy(halves.at[0], message.at[pl.ds(0, half)], half_sem).wait()

    @pl.loop(0, sum_count)
    def _(k):
        pltpu.make_async_copy(total.at[k], squares_out.at[0], total_sem).wait()


def pack_tiles(plan, pattern, weights, edges):
    _, lists, tile, _ = weights.shape
    slots = SLAB * lists
    most_back, most_forward = MORE[-1]
    return call(
        functools.partial(pack_kernel, lists),
        in_specs=[SMEM, SMEM, ANY, ANY],
        out_specs=[ANY] * 4,
        out_shape=[
            jax.ShapeDtypeStruct((BACK * tile, tile), F32),
            jax.ShapeDtypeStruct((FORWARD, tile, tile), F32),
            jax.ShapeDtypeStruct((most_back * tile, tile), F32),
            jax.ShapeDtypeStruct((most_forward, tile, tile), F32),
        ],
        scratch_shapes=[
            pltpu.VMEM((slots, tile, tile), F32),
            pltpu.VMEM((slots, tile, tile), jnp.int32),
            pltpu.VMEM((FORWARD + most_forward, tile, tile), F32),
            pltpu.VMEM((SLAB, tile // 2, tile), F32),
            pltpu.SMEM((SLAB * BAND + 1,), jnp.int32),
            pltpu.SMEM((SLAB * BAND,), jnp.int32),
            pltpu.SMEM((SLAB * BAND,), jnp.int32),
            pltpu.SMEM((SLAB + 1,), jnp.int32),
            pltpu.SMEM((slots + 1,), jnp.int32),
            pltpu.SemaphoreType.DMA((2, slots)),
            pltpu.SemaphoreType.DMA,
            pltpu.SemaphoreType.DMA,
            pltpu.SemaphoreType.DMA,
        ],
    )(plan, pattern, weights, edges)


def main_kernel(
    lists, pattern, weights, edges, out,
    w, e, high, low, total, result, table, sems, out_sem,
):
    tile = weights.shape[-1]
    slots = SLAB * lists
    slot_table(table, pattern, 0, lists)

    @pl.loop(0, slots)
    def _(slot):
        @pl.when(pattern[0, slot] >= 0)
        def _():
            slot_copy(weights, w, sems.at[0, slot], slot, lists).start()
            slot_copy(edges, e, sems.at[1, slot], slot, lists).start()

    @pl.loop(0, slots)
    def _(slot):
        @pl.when(pattern[0, slot] >= 0)
        def _():
            slot_copy(weights, w, sems.at[0, slot], slot, lists).wait()
            slot_copy(edges, e, sems.at[1, slot], slot, lists).wait()
            value = w[slot] * e[slot].astype(F32)
            w[slot] = value
            high[slot], low[slot] = split(value)

            @pl.when(pattern[0, slot] > 0)
            def _():
                high[slot + slots], low[slot + slots] = split(value.T)

    def own(row, offset):
        inside = (row >= 0) & (row < SLAB) & (offset >= 0) & (offset < BAND)
        return jnp.where(inside, table[jnp.where(inside, row * BAND + offset, 0)], -1)

    def turned(row, offset):
        slot = own(row, offset)
        return jnp.where(slot >= 0, slot + slots, -1)

    @pl.loop(0, slots)
    def _(slot):
        i = slot // lists
        offset = pattern[0, slot]

        @pl.when(offset >= 0)
        def _():
            total[...] = jnp.zeros((tile, tile), F32)

            @pl.loop(1 - BAND, BAND)
            def _(m):
                left = jnp.where(m < 0, turned(i + m, -m), own(i + m, m))
                right = jnp.where(
                    m <= offset, own(i + m, offset - m), turned(i + offset, m - offset)
                )

                @pl.when((left >= 0) & (right >= 0))
                def _():
                    total[...] += product(high[left], low[left], high[right], low[right])

            result[slot] = w[slot] * total[...]

        @pl.when(offset < 0)
        def _():
            result[slot] = jnp.zeros((tile, tile), F32)

        pltpu.make_async_copy(result.at[slot], out.at[i, slot % lists], out_sem).start()

    @pl.loop(0, slots)
    def _(slot):
        pltpu.make_async_copy(result.at[slot], out.at[slot // lists, slot % lists], out_sem).wait()


def main_part(pattern, weights, edges):
    _, lists, tile, _ = weights.shape
    slots = SLAB * lists
    return call(
        functools.partial(main_kernel, lists),
        in_specs=[SMEM, ANY, ANY],
        out_specs=ANY,
        out_shape=jax.ShapeDtypeStruct(weights.shape, F32),
        scratch_shapes=[
            pltpu.VMEM((slots, tile, tile), F32),
            pltpu.VMEM((slots, tile, tile), jnp.int32),
            pltpu.VMEM((2 * slots, tile, tile), BF16),
            pltpu.VMEM((2 * slots, tile, tile), BF16),
            pltpu.VMEM((tile, tile), F32),
            pltpu.VMEM((slots, tile, tile), F32),
            pltpu.SMEM((SLAB * BAND + 1,), jnp.int32),
            pltpu.SemaphoreType.DMA((2, slots)),
            pltpu.SemaphoreType.DMA,
        ],
        cost_estimate=pl.CostEstimate(
            flops=6 * 60 * tile**3, bytes_accessed=3 * weights.size * 4, transcendentals=0
        ),
    )(pattern, weights, edges)


def middle_kernel(
    lists, pattern, weights, edges, squares, before, out, high_out, low_out,
    w, e, result, high, low, sems, out_sem, factor_sem,
):
    tile = weights.shape[-1]
    half = tile // 2
    slots = SLAB * lists

    def crossing(slot):
        return crossing_slot(pattern, 0, slot, lists)

    def output(slot):
        return pltpu.make_async_copy(result.at[slot], out.at[slot // lists, slot % lists], out_sem)

    def outputs(slot):
        return (
            pltpu.make_async_copy(high.at[slot], high_out.at[slot], factor_sem),
            pltpu.make_async_copy(low.at[slot], low_out.at[slot], factor_sem),
        )

    @pl.loop(0, slots)
    def _(slot):
        @pl.when(crossing(slot) | (pattern[0, slot] == 0))
        def _():
            slot_copy(weights, w, sems.at[0, slot], slot, lists).start()
            slot_copy(edges, e, sems.at[1, slot], slot, lists).start()

        @pl.when(pattern[0, slot] == 0)
        def _():
            slot_copy(before, result, sems.at[2, slot], slot, lists).start()

    @pl.loop(0, slots)
    def _(slot):
        @pl.when(crossing(slot) | (pattern[0, slot] == 0))
        def _():
            slot_copy(weights, w, sems.at[0, slot], slot, lists).wait()
            slot_copy(edges, e, sems.at[1, slot], slot, lists).wait()
            w[slot] = w[slot] * e[slot].astype(F32)

        @pl.when(crossing(slot))
        def _():
            high[slot], low[slot] = split(w[slot].T)
            for copy in outputs(slot):
                copy.start()

        @pl.when(pattern[0, slot] == 0)
        def _():
            slot_copy(before, result, sems.at[2, slot], slot, lists).wait()
            i = slot // lists

            def store(row, column, quarter):
                part = (slot, pl.ds(row, half), pl.ds(column, half))
                result[part] += w[part] * quarter

            part = squares[pl.ds(pl.multiple_of(i * half, half), half), :]
            rows = squares[SLAB * half :, :half]
            row = lax.broadcasted_iota(jnp.int32, rows.shape, 0)
            diagonal = jnp.sum(jnp.where(row == i, rows, 0.0), axis=0, keepdims=True)
            unfold(store, part[:, :half], part[:, half:], diagonal)
            output(slot).start()

    @pl.loop(0, slots)
    def _(slot):
        @pl.when(crossing(slot))
        def _():
            for copy in outputs(slot):
                copy.wait()

        @pl.when(pattern[0, slot] == 0)
        def _():
            output(slot).wait()


def middle_part(pattern, weights, edges, squares, before):
    _, lists, tile, _ = weights.shape
    slots = SLAB * lists
    factors = jax.ShapeDtypeStruct((slots, tile, tile), BF16)
    return call(
        functools.partial(middle_kernel, lists),
        in_specs=[SMEM, ANY, ANY, VMEM, ANY],
        out_specs=[ANY, ANY, ANY],
        out_shape=[jax.ShapeDtypeStruct(weights.shape, F32), factors, factors],
        input_output_aliases={4: 0},
        scratch_shapes=[
            pltpu.VMEM((slots, tile, tile), F32),
            pltpu.VMEM((slots, tile, tile), jnp.int32),
            pltpu.VMEM((slots, tile, tile), F32),
            pltpu.VMEM((slots, tile, tile), BF16),
            pltpu.VMEM((slots, tile, tile), BF16),
            pltpu.SemaphoreType.DMA((3, slots)),
            pltpu.SemaphoreType.DMA,
            pltpu.SemaphoreType.DMA,
        ],
    )(pattern, weights, edges, squares, before)


def list_kernel(lists, back, forward, again, plan, pattern, out, table, index, raw, sums):
    slots = SLAB * lists
    first_raw = slots + SLAB
    slot_table(table, pattern, 0, lists)
    raw_count = listing(raw, plan, AHEAD, 0)
    sum_count = jnp.minimum(listing(sums, plan, BEHIND, SLAB), forward)
    half_count = diagonals_needed(out, DIAGONAL, plan, AHEAD)
    room = lax.shift_right_logical(2 * BACK - half_count, 1)
    raw_count = jnp.minimum(raw_count, room + (back - BACK))

    for row in range(SLAB):
        index[row * BAND] = slots + row
        for offset in range(1, BAND):
            index[row * BAND + offset] = -1

    @pl.loop(0, raw_count)
    def _(k):
        place = jnp.where(k < room, k, BACK + k - room)
        out[PLACE + k] = place
        index[raw[k]] = first_raw + place

    for place in range(TARGET, PLACE):
        out[place] = 0

    def jobs_of(slot, count):
        i = slot // lists
        offset = pattern[0, slot]
        for m in range(1, BAND):
            row = i + m - SLAB
            left = index[jnp.maximum(row, 0) * BAND + m]
            column = i + offset
            straight = m <= offset
            gap = jnp.where(straight, offset - m, m - offset)
            later = straight | (column >= SLAB)
            next_row = jnp.where(straight, row, column - SLAB)
            theirs = index[jnp.clip(next_row, 0, SLAB - 1) * BAND + gap]
            ours = table[jnp.clip(column, 0, SLAB - 1) * BAND + gap]
            right = jnp.where(later, theirs, ours)
            valid = (offset >= 0) & (row >= 0) & (left >= 0) & (right >= 0)
            if again:
                fresh = first_raw + BACK
                valid = valid & ((left >= fresh) | (right >= fresh))
            turned = valid & later & ~straight
            out[JOB_SLOT + count] = slot
            out[JOB_LEFT + count] = left
            out[JOB_RIGHT + count] = jnp.where(turned, right + back, right)
            out[TARGET + jnp.where(valid, slot, slots)] = 1
            out[FACTOR + jnp.where(valid & (right < first_raw), right, first_raw)] = 1
            out[TURNED + jnp.where(turned, right - first_raw, back)] = 1
            count = count + valid.astype(jnp.int32)
        return count

    jobs = lax.fori_loop(0, slots, jobs_of, jnp.int32(0))

    @pl.loop(0, sum_count)
    def _(k):
        slot = table[sums[k] // BAND * BAND + sums[k] % BAND - sums[k] // BAND]
        out[SUM_SLOT + k] = slot
        if again:
            out[TARGET + jnp.where(k >= FORWARD, slot, slots)] = 1
        else:
            out[TARGET + slot] = 1

    out[JOBS] = jobs
    out[RAWS] = raw_count
    out[SUMS] = sum_count
    out[DIAGONALS] = half_count


def product_list(back, forward, again, plan, pattern, lists):
    small = pltpu.SMEM((SLAB * BAND,), jnp.int32)
    return call(
        functools.partial(list_kernel, lists, back, forward, again),
        in_specs=[SMEM, SMEM],
        out_specs=SMEM,
        out_shape=jax.ShapeDtypeStruct((LIST_SIZE,), jnp.int32),
        scratch_shapes=[pltpu.SMEM((SLAB * BAND + 1,), jnp.int32), small, small, small],
    )(plan, pattern)


def rest_kernel(
    lists, again, todo, weights, edges, turned_high, turned_low, message, sums, before, out,
    w, e, high, low, result, sems, out_sem,
):
    tile = weights.shape[-1]
    half = tile // 2
    slots = SLAB * lists
    back = message.shape[0] // tile
    first_raw = slots + SLAB

    def inputs(slot):
        return (
            slot_copy(weights, w, sems.at[0, slot], slot, lists),
            slot_copy(edges, e, sems.at[1, slot], slot, lists),
            slot_copy(before, result, sems.at[2, slot], slot, lists),
        )

    def factors(slot):
        return (
            pltpu.make_async_copy(turned_high.at[slot], high.at[slot], sems.at[3, slot]),
            pltpu.make_async_copy(turned_low.at[slot], low.at[slot], sems.at[4, slot]),
        )

    def output(slot):
        return pltpu.make_async_copy(result.at[slot], out.at[slot // lists, slot % lists], out_sem)

    @pl.loop(0, slots)
    def _(slot):
        @pl.when(todo[FACTOR + slot] == 1)
        def _():
            for copy in factors(slot):
                copy.start()

        @pl.when(todo[TARGET + slot] == 1)
        def _():
            for copy in inputs(slot):
                copy.start()

    @pl.loop(0, todo[DIAGONALS])
    def _(k):
        row = todo[DIAGONAL + k]

        @pl.when(todo[FACTOR + slots + row] == 1)
        def _():
            def store(first, column, quarter):
                part = (slots + row, pl.ds(first, half), pl.ds(column, half))
                high[part], low[part] = split(quarter)

            part = message[pl.ds(pl.multiple_of((2 * BACK - 1 - k) * half, half), half), :]
            unfold(store, part[:, :half], part[:, half:], jnp.zeros((1, half), F32))

    @pl.loop(0, todo[RAWS])
    def _(k):
        place = todo[PLACE + k]
        value = message[pl.ds(pl.multiple_of(place * tile, tile), tile), :]
        high[first_raw + place], low[first_raw + place] = split(value)

        @pl.when(todo[TURNED + place] == 1)
        def _():
            high[first_raw + back + place], low[first_raw + back + place] = split(value.T)

    @pl.loop(0, slots)
    def _(slot):
        @pl.when(todo[FACTOR + slot] == 1)
        def _():
            for copy in factors(slot):
                copy.wait()

        @pl.when(todo[TARGET + slot] == 1)
        def _():
            for copy in inputs(slot):
                copy.wait()
            w[slot] = w[slot] * e[slot].astype(F32)

    @pl.loop(FORWARD if again else 0, todo[SUMS])
    def _(k):
        slot = todo[SUM_SLOT + k]
        result[slot] += w[slot] * sums[k]

    @pl.loop(0, todo[JOBS])
    def _(job):
        slot, left, right = todo[JOB_SLOT + job], todo[JOB_LEFT + job], todo[JOB_RIGHT + job]
        value = product(high[left], low[left], high[right], low[right])
        result[slot] += w[slot] * value

    @pl.loop(0, slots)
    def _(slot):
        @pl.when(todo[TARGET + slot] == 1)
        def _():
            output(slot).start()

    @pl.loop(0, slots)
    def _(slot):
        @pl.when(todo[TARGET + slot] == 1)
        def _():
            output(slot).wait()


def rest_part(again, todo, weights, edges, high, low, message, sums, before):
    _, lists, tile, _ = weights.shape
    slots = SLAB * lists
    factors = slots + SLAB + 2 * (message.shape[0] // tile)
    return call(
        functools.partial(rest_kernel, lists, again),
        in_specs=[SMEM, ANY, ANY, ANY, ANY, VMEM, VMEM, ANY],
        out_specs=ANY,
        out_shape=jax.ShapeDtypeStruct(weights.shape, F32),
        input_output_aliases={7: 0},
        scratch_shapes=[
            pltpu.VMEM((slots, tile, tile), F32),
            pltpu.VMEM((slots, tile, tile), jnp.int32),
            pltpu.VMEM((factors, tile, tile), BF16),
            pltpu.VMEM((factors, tile, tile), BF16),
            pltpu.VMEM((slots, tile, tile), F32),
            pltpu.SemaphoreType.DMA((5, slots)),
            pltpu.SemaphoreType.DMA,
        ],
    )(todo, weights, edges, high, low, message, sums, before)


def largest(value):
    columns = lax.axis_size(AXES[1])
    count = lax.axis_size(AXES)
    if count & (count - 1):
        return lax.pmax(value, AXES)
    bits = [1 << bit for bit in range(count.bit_length() - 1)]
    for bit in sorted(bits, key=lambda bit: (bit < columns, bit)):
        other = lax.ppermute(value, AXES, [(device, device ^ bit) for device in range(count)])
        value = jnp.maximum(value, other)
    return value


def shards(weights, edges, offsets, counts):
    slab_count, lists = offsets.shape
    tile = weights.shape[-1]
    listed = jnp.arange(lists)[None, :] < counts[:, None]
    pattern = jnp.where(listed, offsets, -1).reshape(1, slab_count * lists)
    pattern = jnp.pad(pattern, ((0, 0), (0, LANES - slab_count * lists)), constant_values=-1)
    empty = jnp.full((5, LANES), -1, jnp.int32)
    patterns = jnp.concatenate([shifted(pattern, 1), pattern, shifted(pattern, -1), empty])

    squares_out = square_diagonals(pattern, weights, edges)
    squares_out, patterns = lax.optimization_barrier((squares_out, patterns))
    squares = shifted(squares_out, 1)
    plan, level = travel_plan(patterns, lists)
    message_out, sums_out, more_message, more_sums = pack_tiles(plan, pattern, weights, edges)
    message = shifted(message_out, -1)
    sums = shifted(sums_out, 1)

    todo = product_list(BACK, FORWARD, False, plan, pattern, lists)
    support = main_part(pattern, weights, edges)
    level, support = lax.optimization_barrier((level, support))
    level = largest(level)
    support, high, low = middle_part(pattern, weights, edges, squares, support)
    support = rest_part(False, todo, weights, edges, high, low, message, sums, support)

    def branch(back, forward):
        def run(support, plan, pattern, weights, edges, high, low, message, sums, more_message, more_sums):
            if not back:
                return support
            message = jnp.concatenate([message, shifted(more_message[: back * tile], -1)])
            sums = jnp.concatenate([sums, shifted(more_sums[:forward], 1)])
            todo = product_list(BACK + back, FORWARD + forward, True, plan, pattern, lists)
            return rest_part(True, todo, weights, edges, high, low, message, sums, support)

        return run

    return lax.switch(
        level[0],
        [branch(*sizes) for sizes in MORE],
        support, plan, pattern, weights, edges, high, low, message, sums, more_message, more_sums,
    )


def solution(mesh):
    in_specs = (
        P(AXES, None, None, None),
        P(AXES, None, None, None),
        P(AXES, None),
        P(AXES),
    )
    out_specs = P(AXES, None, None, None)
    return jax.shard_map(shards, mesh=mesh, in_specs=in_specs, out_specs=out_specs, check_vma=False)
```

```python
import functools

import jax
import jax.numpy as jnp
from jax import lax
from jax.experimental import pallas as pl
from jax.experimental.pallas import tpu as pltpu
from jax.sharding import PartitionSpec as P

BAND = 6
SLAB = BAND - 1
LANES = 128
AXES = ("row", "col")
BACK, FORWARD = 10, 3
MORE = ((0, 0), (2, 1), (8, 6))
BEHIND, AHEAD = 0, 1
JOBS, RAWS, SUMS, DIAGONALS = 0, 1, 2, 3
TARGET, FACTOR, TURNED, PLACE, SUM_SLOT, DIAGONAL = 8, 32, 64, 96, 128, 144
JOB_SLOT, JOB_LEFT, JOB_RIGHT, LIST_SIZE = 160, 272, 384, 512
VMEM_LIMIT = 56 * 1024 * 1024

F32 = jnp.float32
BF16 = jnp.bfloat16
ANY = pl.BlockSpec(memory_space=pl.ANY)
SMEM = pl.BlockSpec(memory_space=pltpu.SMEM)
VMEM = pl.BlockSpec(memory_space=pltpu.VMEM)


def shifted(value, steps):
    count = lax.axis_size(AXES)
    first, last = (max(0, -steps), min(count, count - steps))
    return lax.ppermute(value, AXES, [(source, source + steps) for source in range(first, last)])


def split(value):
    high = value.astype(BF16)
    low = (value - high.astype(F32)).astype(BF16)
    return high, low


def dot(left, right):
    return jnp.dot(left, right, preferred_element_type=F32)


def product(left_high, left_low, right_high, right_low):
    return dot(left_high, right_high) + (dot(left_high, right_low) + dot(left_low, right_high))


def iotas(size):
    rows = lax.broadcasted_iota(jnp.int32, (size, size), 0)
    columns = lax.broadcasted_iota(jnp.int32, (size, size), 1)
    return rows, columns


def folded(tile):
    half = tile.shape[0] // 2
    rows, columns = iotas(half)
    lower_right = tile[half:, half:]
    mixed = jnp.where(rows <= columns, tile[:half, :half], lower_right)
    diagonal = jnp.sum(jnp.where(rows == columns, lower_right, 0.0), axis=0, keepdims=True)
    return mixed, tile[:half, half:], diagonal


def unfold(store, mixed, upper_right, diagonal):
    half = mixed.shape[0]
    rows, columns = iotas(half)
    turned = mixed.T
    store(0, 0, jnp.where(rows <= columns, mixed, turned))
    store(0, half, upper_right)
    store(half, 0, upper_right.T)
    lower_right = jnp.where(rows > columns, mixed, turned)
    store(half, half, jnp.where(rows == columns, diagonal, lower_right))


def slot_table(table, pattern, row, lists):
    for place in range(SLAB * BAND):
        table[place] = -1
    for slot in range(SLAB * lists):
        offset = pattern[row, slot]
        table[jnp.where(offset >= 0, slot // lists * BAND + offset, SLAB * BAND)] = slot


def listing(items, plan, row, first):
    count = jnp.int32(0)
    for i in range(SLAB):
        mask = plan[row, first + i]
        for bit in range(1, BAND):
            items[count] = i * BAND + bit
            count = count + ((mask >> bit) & 1)
    return count


def diagonals_needed(items, first, plan, row):
    count = jnp.int32(0)
    for i in range(SLAB):
        items[first + count] = i
        count = count + (plan[row, i] & 1)
    return count


def slot_copy(source, target, semaphore, slot, lists):
    return pltpu.make_async_copy(source.at[slot // lists, slot % lists], target.at[slot], semaphore)


def call(kernel, **kwargs):
    return pl.pallas_call(
        kernel,
        compiler_params=pltpu.CompilerParams(vmem_limit_bytes=VMEM_LIMIT),
        **kwargs,
    )


def crossing_slot(pattern, row, slot, lists):
    offset = pattern[row, slot]
    return (offset >= 0) & (slot // lists + offset >= SLAB)


def square_kernel(lists, pattern, weights, edges, out, w, e, total, table, sems):
    tile = weights.shape[-1]
    half = tile // 2
    slot_table(table, pattern, 0, lists)

    @pl.loop(0, SLAB * lists)
    def _(slot):
        @pl.when(crossing_slot(pattern, 0, slot, lists))
        def _():
            slot_copy(weights, w, sems.at[0, slot], slot, lists).start()
            slot_copy(edges, e, sems.at[1, slot], slot, lists).start()

    out[SLAB * half :, :] = jnp.zeros((8, tile), F32)
    for j in range(SLAB):
        total[...] = jnp.zeros((tile, tile), F32)

        @pl.loop(j, SLAB)
        def _(i):
            slot = table[i * BAND + SLAB + j - i]

            @pl.when(slot >= 0)
            def _():
                slot_copy(weights, w, sems.at[0, slot], slot, lists).wait()
                slot_copy(edges, e, sems.at[1, slot], slot, lists).wait()
                value = w[slot] * e[slot].astype(F32)
                total[...] += product(*split(value.T), *split(value))

        mixed, upper_right, diagonal = folded(total[...])
        out[j * half : (j + 1) * half, :half] = mixed
        out[j * half : (j + 1) * half, half:] = upper_right
        out[SLAB * half + j : SLAB * half + j + 1, :half] = diagonal


def square_diagonals(pattern, weights, edges):
    _, lists, tile, _ = weights.shape
    return call(
        functools.partial(square_kernel, lists),
        in_specs=[SMEM, ANY, ANY],
        out_specs=VMEM,
        out_shape=jax.ShapeDtypeStruct((SLAB * tile // 2 + 8, tile), F32),
        scratch_shapes=[
            pltpu.VMEM((SLAB * lists, tile, tile), F32),
            pltpu.VMEM((SLAB * lists, tile, tile), jnp.int32),
            pltpu.VMEM((tile, tile), F32),
            pltpu.SMEM((SLAB * BAND + 1,), jnp.int32),
            pltpu.SemaphoreType.DMA((2, SLAB * lists)),
        ],
    )(pattern, weights, edges)


def plan_kernel(lists, patterns, plan, choice):
    offsets = patterns[...]
    slabs = offsets.shape[0]
    lane = lax.broadcasted_iota(jnp.int32, offsets.shape, 1)
    row = lax.broadcasted_iota(jnp.int32, offsets.shape, 0)
    inside = (offsets >= 0) & (lane < SLAB * lists)
    bits = jnp.where(inside, jnp.left_shift(1, jnp.maximum(offsets, 0)), 0)

    def ahead(value, steps):
        return pltpu.roll(value, LANES - steps, 1) if steps else value

    mask = bits
    for a in range(1, lists):
        mask = mask | ahead(bits, a)
    own = [ahead(mask, i * lists) for i in range(SLAB)]
    rows = own + [pltpu.roll(value, slabs - 1, 0) for value in own]

    def has(r, offset):
        return jnp.right_shift(rows[r], offset) & 1

    zero = jnp.zeros_like(mask)
    need = [zero] * SLAB
    for i in range(SLAB):
        for m in range(SLAB - i, BAND):
            middle = i + m
            wanted = zero
            for t in range(BAND):
                target = i + t
                if target >= SLAB:
                    other, offset = (middle, t - m) if m <= t else (target, m - t)
                    used = has(i, t) & has(middle, m) & has(other, offset)
                    wanted = wanted | used
                    place = other - SLAB
                    need[place] = need[place] | jnp.left_shift(used, offset)
                elif m > t:
                    wanted = wanted | (has(i, t) & has(middle, m) & has(target, m - t))
            need[middle - SLAB] = need[middle - SLAB] | jnp.left_shift(wanted, m)
    crossing = [jnp.right_shift(jnp.left_shift(rows[i], i), SLAB) for i in range(SLAB)]
    partial = []
    for j in range(SLAB):
        cover = zero
        for i in range(SLAB):
            cover = cover | jnp.where(jnp.right_shift(crossing[i], j) & 1 == 1, crossing[i], 0)
        listed = jnp.left_shift(rows[SLAB + j], j) & ((1 << SLAB) - (2 << j))
        partial.append(cover & listed)
    def total(group, bits):
        count = zero
        for value in group:
            for bit in bits:
                count = count + (jnp.right_shift(value, bit) & 1)
        return count

    room = jnp.right_shift(2 * BACK - total(need, (0,)), 1)
    extra = []
    for count in (total(need, range(1, BAND)) - room, total(partial, range(1, BAND)) - FORWARD):
        count = jnp.where((lane == 0) & (row < slabs - 1), count, 0)
        extra.append(jnp.max(count.astype(F32)).astype(jnp.int32))
    result = zero
    for place, value in enumerate(need + partial):
        value = pltpu.roll(value, place, 1) if place else value
        result = jnp.where((lane == place) & (row < slabs - 1), value, result)
    plan[...] = result
    level = jnp.int32(0)
    for back, forward in MORE[:-1]:
        level = level + ((extra[0] > back) | (extra[1] > forward)).astype(jnp.int32)
    choice[0] = level


def travel_plan(patterns, lists):
    return call(
        functools.partial(plan_kernel, lists),
        in_specs=[VMEM],
        out_specs=[VMEM, SMEM],
        out_shape=[
            jax.ShapeDtypeStruct(patterns.shape, jnp.int32),
            jax.ShapeDtypeStruct((1,), jnp.int32),
        ],
    )(patterns)


def pack_kernel(
    lists, plan, pattern, weights, edges, message, squares_out, more_tiles_out, more_squares_out,
    w, e, total, halves, table, raw, sums, diagonals, needed, sems, tile_sem, half_sem, total_sem,
):
    tile = weights.shape[-1]
    half = tile // 2
    slots = SLAB * lists
    slot_table(table, pattern, 0, lists)
    raw_count = listing(raw, plan, BEHIND, 0)
    sum_count = listing(sums, plan, AHEAD, SLAB)
    half_count = diagonals_needed(diagonals, 0, plan, BEHIND)
    room = lax.shift_right_logical(2 * BACK - half_count, 1)

    for slot in range(slots + 1):
        needed[slot] = 0

    def factors(k, i):
        first = SLAB + sums[k] // BAND - i
        second = SLAB + sums[k] % BAND - i
        inside = (first < BAND) & (second < BAND)
        left = table[i * BAND + jnp.minimum(first, BAND - 1)]
        right = table[i * BAND + jnp.minimum(second, BAND - 1)]
        return left, right, inside & (left >= 0) & (right >= 0)

    @pl.loop(0, raw_count)
    def _(k):
        needed[table[raw[k]]] = 1

    @pl.loop(0, half_count)
    def _(k):
        needed[table[diagonals[k] * BAND]] = 1

    @pl.loop(0, sum_count)
    def _(k):
        for i in range(SLAB):
            left, right, both = factors(k, i)
            needed[jnp.where(both, left, slots)] = 1
            needed[jnp.where(both, right, slots)] = 1

    @pl.loop(0, slots)
    def _(slot):
        @pl.when(needed[slot] == 1)
        def _():
            slot_copy(weights, w, sems.at[0, slot], slot, lists).start()
            slot_copy(edges, e, sems.at[1, slot], slot, lists).start()

    @pl.loop(0, slots)
    def _(slot):
        @pl.when(needed[slot] == 1)
        def _():
            slot_copy(weights, w, sems.at[0, slot], slot, lists).wait()
            slot_copy(edges, e, sems.at[1, slot], slot, lists).wait()
            w[slot] = w[slot] * e[slot].astype(F32)

    @pl.loop(0, raw_count)
    def _(k):
        source = w.at[table[raw[k]]]

        @pl.when(k < room)
        def _():
            rows = pl.ds(pl.multiple_of(k * tile, tile), tile)
            pltpu.make_async_copy(source, message.at[rows], tile_sem).start()

        @pl.when(k >= room)
        def _():
            rows = pl.ds(pl.multiple_of((k - room) * tile, tile), tile)
            pltpu.make_async_copy(source, more_tiles_out.at[rows], tile_sem).start()

    @pl.loop(0, half_count)
    def _(k):
        mixed, upper_right, _ = folded(w[table[diagonals[k] * BAND]])
        halves[k, :, :half] = mixed
        halves[k, :, half:] = upper_right
        rows = pl.ds(pl.multiple_of((2 * BACK - 1 - k) * half, half), half)
        pltpu.make_async_copy(halves.at[k], message.at[rows], half_sem).start()

    @pl.loop(0, sum_count)
    def _(k):
        total[k] = jnp.zeros((tile, tile), F32)

        @pl.loop(0, SLAB)
        def _(i):
            left, right, both = factors(k, i)

            @pl.when(both)
            def _():
                total[k] += product(*split(w[left].T), *split(w[right]))

        @pl.when(k < FORWARD)
        def _():
            pltpu.make_async_copy(total.at[k], squares_out.at[k], total_sem).start()

        @pl.when(k >= FORWARD)
        def _():
            target = more_squares_out.at[k - FORWARD]
            pltpu.make_async_copy(total.at[k], target, total_sem).start()

    @pl.loop(0, raw_count)
    def _(k):
        pltpu.make_async_copy(w.at[0], message.at[pl.ds(0, tile)], tile_sem).wait()

    @pl.loop(0, half_count)
    def _(k):
        pltpu.make_async_copy(halves.at[0], message.at[pl.ds(0, half)], half_sem).wait()

    @pl.loop(0, sum_count)
    def _(k):
        pltpu.make_async_copy(total.at[k], squares_out.at[0], total_sem).wait()


def pack_tiles(plan, pattern, weights, edges):
    _, lists, tile, _ = weights.shape
    slots = SLAB * lists
    most_back, most_forward = MORE[-1]
    return call(
        functools.partial(pack_kernel, lists),
        in_specs=[SMEM, SMEM, ANY, ANY],
        out_specs=[ANY] * 4,
        out_shape=[
            jax.ShapeDtypeStruct((BACK * tile, tile), F32),
            jax.ShapeDtypeStruct((FORWARD, tile, tile), F32),
            jax.ShapeDtypeStruct((most_back * tile, tile), F32),
            jax.ShapeDtypeStruct((most_forward, tile, tile), F32),
        ],
        scratch_shapes=[
            pltpu.VMEM((slots, tile, tile), F32),
            pltpu.VMEM((slots, tile, tile), jnp.int32),
            pltpu.VMEM((FORWARD + most_forward, tile, tile), F32),
            pltpu.VMEM((SLAB, tile // 2, tile), F32),
            pltpu.SMEM((SLAB * BAND + 1,), jnp.int32),
            pltpu.SMEM((SLAB * BAND,), jnp.int32),
            pltpu.SMEM((SLAB * BAND,), jnp.int32),
            pltpu.SMEM((SLAB + 1,), jnp.int32),
            pltpu.SMEM((slots + 1,), jnp.int32),
            pltpu.SemaphoreType.DMA((2, slots)),
            pltpu.SemaphoreType.DMA,
            pltpu.SemaphoreType.DMA,
            pltpu.SemaphoreType.DMA,
        ],
    )(plan, pattern, weights, edges)


def main_kernel(
    lists, pattern, weights, edges, squares, out, turned_high, turned_low,
    w, e, high, low, total, result, table, sems, out_sem, factor_sem,
):
    tile = weights.shape[-1]
    half = tile // 2
    slots = SLAB * lists
    slot_table(table, pattern, 0, lists)

    @pl.loop(0, slots)
    def _(slot):
        @pl.when(pattern[0, slot] >= 0)
        def _():
            slot_copy(weights, w, sems.at[0, slot], slot, lists).start()
            slot_copy(edges, e, sems.at[1, slot], slot, lists).start()

    def factors(slot):
        return (
            pltpu.make_async_copy(high.at[slot + slots], turned_high.at[slot], factor_sem),
            pltpu.make_async_copy(low.at[slot + slots], turned_low.at[slot], factor_sem),
        )

    @pl.loop(0, slots)
    def _(slot):
        @pl.when(pattern[0, slot] >= 0)
        def _():
            slot_copy(weights, w, sems.at[0, slot], slot, lists).wait()
            slot_copy(edges, e, sems.at[1, slot], slot, lists).wait()
            value = w[slot] * e[slot].astype(F32)
            w[slot] = value
            high[slot], low[slot] = split(value)

            @pl.when(pattern[0, slot] > 0)
            def _():
                high[slot + slots], low[slot + slots] = split(value.T)

            @pl.when(crossing_slot(pattern, 0, slot, lists))
            def _():
                for copy in factors(slot):
                    copy.start()

    def own(row, offset):
        inside = (row >= 0) & (row < SLAB) & (offset >= 0) & (offset < BAND)
        return jnp.where(inside, table[jnp.where(inside, row * BAND + offset, 0)], -1)

    def turned(row, offset):
        slot = own(row, offset)
        return jnp.where(slot >= 0, slot + slots, -1)

    @pl.loop(0, slots)
    def _(slot):
        i = slot // lists
        offset = pattern[0, slot]

        @pl.when(offset > 0)
        def _():
            total[...] = jnp.zeros((tile, tile), F32)

        @pl.when(offset == 0)
        def _():
            def store(row, column, quarter):
                total[pl.ds(row, half), pl.ds(column, half)] = quarter

            part = squares[pl.ds(pl.multiple_of(i * half, half), half), :]
            rows = squares[SLAB * half :, :half]
            row = lax.broadcasted_iota(jnp.int32, rows.shape, 0)
            diagonal = jnp.sum(jnp.where(row == i, rows, 0.0), axis=0, keepdims=True)
            unfold(store, part[:, :half], part[:, half:], diagonal)

        @pl.when(offset >= 0)
        def _():
            @pl.loop(1 - BAND, BAND)
            def _(m):
                left = jnp.where(m < 0, turned(i + m, -m), own(i + m, m))
                right = jnp.where(
                    m <= offset, own(i + m, offset - m), turned(i + offset, m - offset)
                )

                @pl.when((left >= 0) & (right >= 0))
                def _():
                    total[...] += product(high[left], low[left], high[right], low[right])

            result[slot] = w[slot] * total[...]

        @pl.when(offset < 0)
        def _():
            result[slot] = jnp.zeros((tile, tile), F32)

        pltpu.make_async_copy(result.at[slot], out.at[i, slot % lists], out_sem).start()

    @pl.loop(0, slots)
    def _(slot):
        pltpu.make_async_copy(result.at[slot], out.at[slot // lists, slot % lists], out_sem).wait()

        @pl.when(crossing_slot(pattern, 0, slot, lists))
        def _():
            for copy in factors(slot):
                copy.wait()


def main_part(pattern, weights, edges, squares):
    _, lists, tile, _ = weights.shape
    slots = SLAB * lists
    turned = jax.ShapeDtypeStruct((slots, tile, tile), BF16)
    return call(
        functools.partial(main_kernel, lists),
        in_specs=[SMEM, ANY, ANY, VMEM],
        out_specs=[ANY, ANY, ANY],
        out_shape=[jax.ShapeDtypeStruct(weights.shape, F32), turned, turned],
        scratch_shapes=[
            pltpu.VMEM((slots, tile, tile), F32),
            pltpu.VMEM((slots, tile, tile), jnp.int32),
            pltpu.VMEM((2 * slots, tile, tile), BF16),
            pltpu.VMEM((2 * slots, tile, tile), BF16),
            pltpu.VMEM((tile, tile), F32),
            pltpu.VMEM((slots, tile, tile), F32),
            pltpu.SMEM((SLAB * BAND + 1,), jnp.int32),
            pltpu.SemaphoreType.DMA((2, slots)),
            pltpu.SemaphoreType.DMA,
            pltpu.SemaphoreType.DMA,
        ],
        cost_estimate=pl.CostEstimate(
            flops=6 * 60 * tile**3, bytes_accessed=3 * weights.size * 4, transcendentals=0
        ),
    )(pattern, weights, edges, squares)


def list_kernel(lists, back, forward, again, plan, pattern, out, table, index, raw, sums):
    slots = SLAB * lists
    first_raw = slots + SLAB
    slot_table(table, pattern, 0, lists)
    raw_count = listing(raw, plan, AHEAD, 0)
    sum_count = jnp.minimum(listing(sums, plan, BEHIND, SLAB), forward)
    half_count = diagonals_needed(out, DIAGONAL, plan, AHEAD)
    room = lax.shift_right_logical(2 * BACK - half_count, 1)
    raw_count = jnp.minimum(raw_count, room + (back - BACK))

    for row in range(SLAB):
        index[row * BAND] = slots + row
        for offset in range(1, BAND):
            index[row * BAND + offset] = -1

    @pl.loop(0, raw_count)
    def _(k):
        place = jnp.where(k < room, k, BACK + k - room)
        out[PLACE + k] = place
        index[raw[k]] = first_raw + place

    for place in range(TARGET, PLACE):
        out[place] = 0

    def jobs_of(slot, count):
        i = slot // lists
        offset = pattern[0, slot]
        for m in range(1, BAND):
            row = i + m - SLAB
            left = index[jnp.maximum(row, 0) * BAND + m]
            column = i + offset
            straight = m <= offset
            gap = jnp.where(straight, offset - m, m - offset)
            later = straight | (column >= SLAB)
            next_row = jnp.where(straight, row, column - SLAB)
            theirs = index[jnp.clip(next_row, 0, SLAB - 1) * BAND + gap]
            ours = table[jnp.clip(column, 0, SLAB - 1) * BAND + gap]
            right = jnp.where(later, theirs, ours)
            valid = (offset >= 0) & (row >= 0) & (left >= 0) & (right >= 0)
            if again:
                fresh = first_raw + BACK
                valid = valid & ((left >= fresh) | (right >= fresh))
            turned = valid & later & ~straight
            out[JOB_SLOT + count] = slot
            out[JOB_LEFT + count] = left
            out[JOB_RIGHT + count] = jnp.where(turned, right + back, right)
            out[TARGET + jnp.where(valid, slot, slots)] = 1
            out[FACTOR + jnp.where(valid & (right < first_raw), right, first_raw)] = 1
            out[TURNED + jnp.where(turned, right - first_raw, back)] = 1
            count = count + valid.astype(jnp.int32)
        return count

    jobs = lax.fori_loop(0, slots, jobs_of, jnp.int32(0))

    @pl.loop(0, sum_count)
    def _(k):
        slot = table[sums[k] // BAND * BAND + sums[k] % BAND - sums[k] // BAND]
        out[SUM_SLOT + k] = slot
        if again:
            out[TARGET + jnp.where(k >= FORWARD, slot, slots)] = 1
        else:
            out[TARGET + slot] = 1

    out[JOBS] = jobs
    out[RAWS] = raw_count
    out[SUMS] = sum_count
    out[DIAGONALS] = half_count


def product_list(back, forward, again, plan, pattern, lists):
    small = pltpu.SMEM((SLAB * BAND,), jnp.int32)
    return call(
        functools.partial(list_kernel, lists, back, forward, again),
        in_specs=[SMEM, SMEM],
        out_specs=SMEM,
        out_shape=jax.ShapeDtypeStruct((LIST_SIZE,), jnp.int32),
        scratch_shapes=[pltpu.SMEM((SLAB * BAND + 1,), jnp.int32), small, small, small],
    )(plan, pattern)


def rest_kernel(
    lists, again, todo, weights, edges, turned_high, turned_low, message, sums, before, out,
    w, e, high, low, result, sems, out_sem,
):
    tile = weights.shape[-1]
    half = tile // 2
    slots = SLAB * lists
    back = message.shape[0] // tile
    first_raw = slots + SLAB

    def inputs(slot):
        return (
            slot_copy(weights, w, sems.at[0, slot], slot, lists),
            slot_copy(edges, e, sems.at[1, slot], slot, lists),
            slot_copy(before, result, sems.at[2, slot], slot, lists),
        )

    def factors(slot):
        return (
            pltpu.make_async_copy(turned_high.at[slot], high.at[slot], sems.at[3, slot]),
            pltpu.make_async_copy(turned_low.at[slot], low.at[slot], sems.at[4, slot]),
        )

    def output(slot):
        return pltpu.make_async_copy(result.at[slot], out.at[slot // lists, slot % lists], out_sem)

    @pl.loop(0, slots)
    def _(slot):
        @pl.when(todo[FACTOR + slot] == 1)
        def _():
            for copy in factors(slot):
                copy.start()

        @pl.when(todo[TARGET + slot] == 1)
        def _():
            for copy in inputs(slot):
                copy.start()

    @pl.loop(0, todo[DIAGONALS])
    def _(k):
        row = todo[DIAGONAL + k]

        @pl.when(todo[FACTOR + slots + row] == 1)
        def _():
            def store(first, column, quarter):
                part = (slots + row, pl.ds(first, half), pl.ds(column, half))
                high[part], low[part] = split(quarter)

            part = message[pl.ds(pl.multiple_of((2 * BACK - 1 - k) * half, half), half), :]
            unfold(store, part[:, :half], part[:, half:], jnp.zeros((1, half), F32))

    @pl.loop(0, todo[RAWS])
    def _(k):
        place = todo[PLACE + k]
        value = message[pl.ds(pl.multiple_of(place * tile, tile), tile), :]
        high[first_raw + place], low[first_raw + place] = split(value)

        @pl.when(todo[TURNED + place] == 1)
        def _():
            high[first_raw + back + place], low[first_raw + back + place] = split(value.T)

    @pl.loop(0, slots)
    def _(slot):
        @pl.when(todo[FACTOR + slot] == 1)
        def _():
            for copy in factors(slot):
                copy.wait()

        @pl.when(todo[TARGET + slot] == 1)
        def _():
            for copy in inputs(slot):
                copy.wait()
            w[slot] = w[slot] * e[slot].astype(F32)

    @pl.loop(FORWARD if again else 0, todo[SUMS])
    def _(k):
        slot = todo[SUM_SLOT + k]
        result[slot] += w[slot] * sums[k]

    @pl.loop(0, todo[JOBS])
    def _(job):
        slot, left, right = todo[JOB_SLOT + job], todo[JOB_LEFT + job], todo[JOB_RIGHT + job]
        value = product(high[left], low[left], high[right], low[right])
        result[slot] += w[slot] * value

    @pl.loop(0, slots)
    def _(slot):
        @pl.when(todo[TARGET + slot] == 1)
        def _():
            output(slot).start()

    @pl.loop(0, slots)
    def _(slot):
        @pl.when(todo[TARGET + slot] == 1)
        def _():
            output(slot).wait()


def rest_part(again, todo, weights, edges, high, low, message, sums, before):
    _, lists, tile, _ = weights.shape
    slots = SLAB * lists
    factors = slots + SLAB + 2 * (message.shape[0] // tile)
    return call(
        functools.partial(rest_kernel, lists, again),
        in_specs=[SMEM, ANY, ANY, ANY, ANY, VMEM, VMEM, ANY],
        out_specs=ANY,
        out_shape=jax.ShapeDtypeStruct(weights.shape, F32),
        input_output_aliases={7: 0},
        scratch_shapes=[
            pltpu.VMEM((slots, tile, tile), F32),
            pltpu.VMEM((slots, tile, tile), jnp.int32),
            pltpu.VMEM((factors, tile, tile), BF16),
            pltpu.VMEM((factors, tile, tile), BF16),
            pltpu.VMEM((slots, tile, tile), F32),
            pltpu.SemaphoreType.DMA((5, slots)),
            pltpu.SemaphoreType.DMA,
        ],
    )(todo, weights, edges, high, low, message, sums, before)


def merged(value, bits):
    count = lax.axis_size(AXES)
    for bit in bits:
        other = lax.ppermute(value, AXES, [(device, device ^ bit) for device in range(count)])
        value = jnp.maximum(value, other)
    return value


def shards(weights, edges, offsets, counts):
    slab_count, lists = offsets.shape
    tile = weights.shape[-1]
    slabs = lax.axis_size(AXES)
    columns = lax.axis_size(AXES[1])
    bits = [1 << bit for bit in range(slabs.bit_length() - 1)]
    listed = jnp.arange(lists)[None, :] < counts[:, None]
    pattern = jnp.where(listed, offsets, -1).reshape(1, slab_count * lists)
    pattern = jnp.pad(pattern, ((0, 0), (0, LANES - slab_count * lists)), constant_values=-1)
    empty = jnp.full((5, LANES), -1, jnp.int32)
    patterns = jnp.concatenate([shifted(pattern, 1), pattern, shifted(pattern, -1), empty])
    mine = jnp.arange(slabs)[:, None] == lax.axis_index(AXES)
    everyone = merged(jnp.where(mine, pattern, -1), [bit for bit in bits if bit < columns])

    squares_out = square_diagonals(pattern, weights, edges)
    squares_out, everyone, patterns = lax.optimization_barrier((squares_out, everyone, patterns))
    squares = shifted(squares_out, 1)
    plan, _ = travel_plan(patterns, lists)
    message_out, sums_out, more_message, more_sums = pack_tiles(plan, pattern, weights, edges)
    message_out, sums_out, squares = lax.optimization_barrier((message_out, sums_out, squares))
    message = shifted(message_out, -1)
    sums = shifted(sums_out, 1)

    todo = product_list(BACK, FORWARD, False, plan, pattern, lists)
    support, high, low = main_part(pattern, weights, edges, squares)
    everyone, support = lax.optimization_barrier((everyone, support))
    _, level = travel_plan(merged(everyone, [bit for bit in bits if bit >= columns]), lists)
    support = rest_part(False, todo, weights, edges, high, low, message, sums, support)

    def branch(back, forward):
        def run(support, plan, pattern, weights, edges, high, low, message, sums, more_message, more_sums):
            if not back:
                return support
            message = jnp.concatenate([message, shifted(more_message[: back * tile], -1)])
            sums = jnp.concatenate([sums, shifted(more_sums[:forward], 1)])
            todo = product_list(BACK + back, FORWARD + forward, True, plan, pattern, lists)
            return rest_part(True, todo, weights, edges, high, low, message, sums, support)

        return run

    return lax.switch(
        level[0],
        [branch(*sizes) for sizes in MORE],
        support, plan, pattern, weights, edges, high, low, message, sums, more_message, more_sums,
    )


def solution(mesh):
    in_specs = (
        P(AXES, None, None, None),
        P(AXES, None, None, None),
        P(AXES, None),
        P(AXES),
    )
    out_specs = P(AXES, None, None, None)
    return jax.shard_map(shards, mesh=mesh, in_specs=in_specs, out_specs=out_specs, check_vma=False)
```

```python
import functools

import jax
import jax.numpy as jnp
from jax import lax
from jax.experimental import pallas as pl
from jax.experimental.pallas import tpu as pltpu
from jax.sharding import PartitionSpec as P

BAND = 6
SLAB = BAND - 1
LANES = 128
AXES = ("row", "col")
BACK, FORWARD = 10, 3
MORE = ((0, 0), (2, 1), (8, 6))
BEHIND, AHEAD = 0, 1
JOBS, RAWS, SUMS, DIAGONALS = 0, 1, 2, 3
TARGET, FACTOR, TURNED, PLACE, SUM_SLOT, DIAGONAL = 8, 32, 64, 96, 128, 144
JOB_SLOT, JOB_LEFT, JOB_RIGHT, LIST_SIZE = 160, 272, 384, 512
VMEM_LIMIT = 56 * 1024 * 1024

F32 = jnp.float32
BF16 = jnp.bfloat16
ANY = pl.BlockSpec(memory_space=pl.ANY)
SMEM = pl.BlockSpec(memory_space=pltpu.SMEM)
VMEM = pl.BlockSpec(memory_space=pltpu.VMEM)


def shifted(value, steps):
    count = lax.axis_size(AXES)
    first, last = (max(0, -steps), min(count, count - steps))
    return lax.ppermute(value, AXES, [(source, source + steps) for source in range(first, last)])


def split(value):
    high = value.astype(BF16)
    low = (value - high.astype(F32)).astype(BF16)
    return high, low


def dot(left, right):
    return jnp.dot(left, right, preferred_element_type=F32)


def product(left_high, left_low, right_high, right_low):
    return dot(left_high, right_high) + (dot(left_high, right_low) + dot(left_low, right_high))


def iotas(size):
    rows = lax.broadcasted_iota(jnp.int32, (size, size), 0)
    columns = lax.broadcasted_iota(jnp.int32, (size, size), 1)
    return rows, columns


def folded(tile):
    half = tile.shape[0] // 2
    rows, columns = iotas(half)
    lower_right = tile[half:, half:]
    mixed = jnp.where(rows <= columns, tile[:half, :half], lower_right)
    diagonal = jnp.sum(jnp.where(rows == columns, lower_right, 0.0), axis=0, keepdims=True)
    return mixed, tile[:half, half:], diagonal


def unfold(store, mixed, upper_right, diagonal):
    half = mixed.shape[0]
    rows, columns = iotas(half)
    turned = mixed.T
    store(0, 0, jnp.where(rows <= columns, mixed, turned))
    store(0, half, upper_right)
    store(half, 0, upper_right.T)
    lower_right = jnp.where(rows > columns, mixed, turned)
    store(half, half, jnp.where(rows == columns, diagonal, lower_right))


def slot_table(table, pattern, row, lists):
    for place in range(SLAB * BAND):
        table[place] = -1
    for slot in range(SLAB * lists):
        offset = pattern[row, slot]
        table[jnp.where(offset >= 0, slot // lists * BAND + offset, SLAB * BAND)] = slot


def listing(items, plan, row, first):
    count = jnp.int32(0)
    for i in range(SLAB):
        mask = plan[row, first + i]
        for bit in range(1, BAND):
            items[count] = i * BAND + bit
            count = count + ((mask >> bit) & 1)
    return count


def diagonals_needed(items, first, plan, row):
    count = jnp.int32(0)
    for i in range(SLAB):
        items[first + count] = i
        count = count + (plan[row, i] & 1)
    return count


def slot_copy(source, target, semaphore, slot, lists):
    return pltpu.make_async_copy(source.at[slot // lists, slot % lists], target.at[slot], semaphore)


def call(kernel, **kwargs):
    return pl.pallas_call(
        kernel,
        compiler_params=pltpu.CompilerParams(vmem_limit_bytes=VMEM_LIMIT),
        **kwargs,
    )


def crossing_slot(pattern, row, slot, lists):
    offset = pattern[row, slot]
    return (offset >= 0) & (slot // lists + offset >= SLAB)


def square_kernel(lists, pattern, weights, edges, out, w, e, total, table, sems):
    tile = weights.shape[-1]
    half = tile // 2
    slot_table(table, pattern, 0, lists)

    @pl.loop(0, SLAB * lists)
    def _(slot):
        @pl.when(crossing_slot(pattern, 0, slot, lists))
        def _():
            slot_copy(weights, w, sems.at[0, slot], slot, lists).start()
            slot_copy(edges, e, sems.at[1, slot], slot, lists).start()

    out[SLAB * half :, :] = jnp.zeros((8, tile), F32)
    for j in range(SLAB):
        total[...] = jnp.zeros((tile, tile), F32)

        @pl.loop(j, SLAB)
        def _(i):
            slot = table[i * BAND + SLAB + j - i]

            @pl.when(slot >= 0)
            def _():
                slot_copy(weights, w, sems.at[0, slot], slot, lists).wait()
                slot_copy(edges, e, sems.at[1, slot], slot, lists).wait()
                value = w[slot] * e[slot].astype(F32)
                total[...] += product(*split(value.T), *split(value))

        mixed, upper_right, diagonal = folded(total[...])
        out[j * half : (j + 1) * half, :half] = mixed
        out[j * half : (j + 1) * half, half:] = upper_right
        out[SLAB * half + j : SLAB * half + j + 1, :half] = diagonal


def square_diagonals(pattern, weights, edges):
    _, lists, tile, _ = weights.shape
    return call(
        functools.partial(square_kernel, lists),
        in_specs=[SMEM, ANY, ANY],
        out_specs=VMEM,
        out_shape=jax.ShapeDtypeStruct((SLAB * tile // 2 + 8, tile), F32),
        scratch_shapes=[
            pltpu.VMEM((SLAB * lists, tile, tile), F32),
            pltpu.VMEM((SLAB * lists, tile, tile), jnp.int32),
            pltpu.VMEM((tile, tile), F32),
            pltpu.SMEM((SLAB * BAND + 1,), jnp.int32),
            pltpu.SemaphoreType.DMA((2, SLAB * lists)),
        ],
    )(pattern, weights, edges)


def plan_kernel(lists, patterns, plan, choice):
    offsets = patterns[...]
    slabs = offsets.shape[0]
    lane = lax.broadcasted_iota(jnp.int32, offsets.shape, 1)
    row = lax.broadcasted_iota(jnp.int32, offsets.shape, 0)
    inside = (offsets >= 0) & (lane < SLAB * lists)
    bits = jnp.where(inside, jnp.left_shift(1, jnp.maximum(offsets, 0)), 0)

    def ahead(value, steps):
        return pltpu.roll(value, LANES - steps, 1) if steps else value

    mask = bits
    for a in range(1, lists):
        mask = mask | ahead(bits, a)
    own = [ahead(mask, i * lists) for i in range(SLAB)]
    rows = own + [pltpu.roll(value, slabs - 1, 0) for value in own]

    def has(r, offset):
        return jnp.right_shift(rows[r], offset) & 1

    zero = jnp.zeros_like(mask)
    need = [zero] * SLAB
    for i in range(SLAB):
        for m in range(SLAB - i, BAND):
            middle = i + m
            wanted = zero
            for t in range(BAND):
                target = i + t
                if target >= SLAB:
                    other, offset = (middle, t - m) if m <= t else (target, m - t)
                    used = has(i, t) & has(middle, m) & has(other, offset)
                    wanted = wanted | used
                    place = other - SLAB
                    need[place] = need[place] | jnp.left_shift(used, offset)
                elif m > t:
                    wanted = wanted | (has(i, t) & has(middle, m) & has(target, m - t))
            need[middle - SLAB] = need[middle - SLAB] | jnp.left_shift(wanted, m)
    crossing = [jnp.right_shift(jnp.left_shift(rows[i], i), SLAB) for i in range(SLAB)]
    partial = []
    for j in range(SLAB):
        cover = zero
        for i in range(SLAB):
            cover = cover | jnp.where(jnp.right_shift(crossing[i], j) & 1 == 1, crossing[i], 0)
        listed = jnp.left_shift(rows[SLAB + j], j) & ((1 << SLAB) - (2 << j))
        partial.append(cover & listed)
    def total(group, bits):
        count = zero
        for value in group:
            for bit in bits:
                count = count + (jnp.right_shift(value, bit) & 1)
        return count

    room = jnp.right_shift(2 * BACK - total(need, (0,)), 1)
    extra = []
    for count in (total(need, range(1, BAND)) - room, total(partial, range(1, BAND)) - FORWARD):
        count = jnp.where((lane == 0) & (row < slabs - 1), count, 0)
        extra.append(jnp.max(count.astype(F32)).astype(jnp.int32))
    result = zero
    for place, value in enumerate(need + partial):
        value = pltpu.roll(value, place, 1) if place else value
        result = jnp.where((lane == place) & (row < slabs - 1), value, result)
    plan[...] = result
    level = jnp.int32(0)
    for back, forward in MORE[:-1]:
        level = level + ((extra[0] > back) | (extra[1] > forward)).astype(jnp.int32)
    choice[0] = level


def travel_plan(patterns, lists):
    return call(
        functools.partial(plan_kernel, lists),
        in_specs=[VMEM],
        out_specs=[VMEM, SMEM],
        out_shape=[
            jax.ShapeDtypeStruct(patterns.shape, jnp.int32),
            jax.ShapeDtypeStruct((1,), jnp.int32),
        ],
    )(patterns)


def pack_kernel(
    lists, plan, pattern, weights, edges, message, squares_out, more_tiles_out, more_squares_out,
    w, e, total, halves, table, raw, sums, diagonals, needed, sems, tile_sem, half_sem, total_sem,
):
    tile = weights.shape[-1]
    half = tile // 2
    slots = SLAB * lists
    slot_table(table, pattern, 0, lists)
    raw_count = listing(raw, plan, BEHIND, 0)
    sum_count = listing(sums, plan, AHEAD, SLAB)
    half_count = diagonals_needed(diagonals, 0, plan, BEHIND)
    room = lax.shift_right_logical(2 * BACK - half_count, 1)

    for slot in range(slots + 1):
        needed[slot] = 0

    def factors(k, i):
        first = SLAB + sums[k] // BAND - i
        second = SLAB + sums[k] % BAND - i
        inside = (first < BAND) & (second < BAND)
        left = table[i * BAND + jnp.minimum(first, BAND - 1)]
        right = table[i * BAND + jnp.minimum(second, BAND - 1)]
        return left, right, inside & (left >= 0) & (right >= 0)

    @pl.loop(0, raw_count)
    def _(k):
        needed[table[raw[k]]] = 1

    @pl.loop(0, half_count)
    def _(k):
        needed[table[diagonals[k] * BAND]] = 1

    @pl.loop(0, sum_count)
    def _(k):
        for i in range(SLAB):
            left, right, both = factors(k, i)
            needed[jnp.where(both, left, slots)] = 1
            needed[jnp.where(both, right, slots)] = 1

    @pl.loop(0, slots)
    def _(slot):
        @pl.when(needed[slot] == 1)
        def _():
            slot_copy(weights, w, sems.at[0, slot], slot, lists).start()
            slot_copy(edges, e, sems.at[1, slot], slot, lists).start()

    @pl.loop(0, slots)
    def _(slot):
        @pl.when(needed[slot] == 1)
        def _():
            slot_copy(weights, w, sems.at[0, slot], slot, lists).wait()
            slot_copy(edges, e, sems.at[1, slot], slot, lists).wait()
            w[slot] = w[slot] * e[slot].astype(F32)

    @pl.loop(0, raw_count)
    def _(k):
        source = w.at[table[raw[k]]]

        @pl.when(k < room)
        def _():
            rows = pl.ds(pl.multiple_of(k * tile, tile), tile)
            pltpu.make_async_copy(source, message.at[rows], tile_sem).start()

        @pl.when(k >= room)
        def _():
            rows = pl.ds(pl.multiple_of((k - room) * tile, tile), tile)
            pltpu.make_async_copy(source, more_tiles_out.at[rows], tile_sem).start()

    @pl.loop(0, half_count)
    def _(k):
        mixed, upper_right, _ = folded(w[table[diagonals[k] * BAND]])
        halves[k, :, :half] = mixed
        halves[k, :, half:] = upper_right
        rows = pl.ds(pl.multiple_of((2 * BACK - 1 - k) * half, half), half)
        pltpu.make_async_copy(halves.at[k], message.at[rows], half_sem).start()

    @pl.loop(0, sum_count)
    def _(k):
        total[k] = jnp.zeros((tile, tile), F32)

        @pl.loop(0, SLAB)
        def _(i):
            left, right, both = factors(k, i)

            @pl.when(both)
            def _():
                total[k] += product(*split(w[left].T), *split(w[right]))

        @pl.when(k < FORWARD)
        def _():
            pltpu.make_async_copy(total.at[k], squares_out.at[k], total_sem).start()

        @pl.when(k >= FORWARD)
        def _():
            target = more_squares_out.at[k - FORWARD]
            pltpu.make_async_copy(total.at[k], target, total_sem).start()

    @pl.loop(0, raw_count)
    def _(k):
        pltpu.make_async_copy(w.at[0], message.at[pl.ds(0, tile)], tile_sem).wait()

    @pl.loop(0, half_count)
    def _(k):
        pltpu.make_async_copy(halves.at[0], message.at[pl.ds(0, half)], half_sem).wait()

    @pl.loop(0, sum_count)
    def _(k):
        pltpu.make_async_copy(total.at[k], squares_out.at[0], total_sem).wait()


def pack_tiles(plan, pattern, weights, edges):
    _, lists, tile, _ = weights.shape
    slots = SLAB * lists
    most_back, most_forward = MORE[-1]
    return call(
        functools.partial(pack_kernel, lists),
        in_specs=[SMEM, SMEM, ANY, ANY],
        out_specs=[ANY] * 4,
        out_shape=[
            jax.ShapeDtypeStruct((BACK * tile, tile), F32),
            jax.ShapeDtypeStruct((FORWARD, tile, tile), F32),
            jax.ShapeDtypeStruct((most_back * tile, tile), F32),
            jax.ShapeDtypeStruct((most_forward, tile, tile), F32),
        ],
        scratch_shapes=[
            pltpu.VMEM((slots, tile, tile), F32),
            pltpu.VMEM((slots, tile, tile), jnp.int32),
            pltpu.VMEM((FORWARD + most_forward, tile, tile), F32),
            pltpu.VMEM((SLAB, tile // 2, tile), F32),
            pltpu.SMEM((SLAB * BAND + 1,), jnp.int32),
            pltpu.SMEM((SLAB * BAND,), jnp.int32),
            pltpu.SMEM((SLAB * BAND,), jnp.int32),
            pltpu.SMEM((SLAB + 1,), jnp.int32),
            pltpu.SMEM((slots + 1,), jnp.int32),
            pltpu.SemaphoreType.DMA((2, slots)),
            pltpu.SemaphoreType.DMA,
            pltpu.SemaphoreType.DMA,
            pltpu.SemaphoreType.DMA,
        ],
    )(plan, pattern, weights, edges)


def main_kernel(
    lists, pattern, weights, edges, out, turned_high, turned_low,
    w, e, high, low, total, result, table, sems, out_sem, factor_sem,
):
    tile = weights.shape[-1]
    slots = SLAB * lists
    slot_table(table, pattern, 0, lists)

    @pl.loop(0, slots)
    def _(slot):
        @pl.when(pattern[0, slot] >= 0)
        def _():
            slot_copy(weights, w, sems.at[0, slot], slot, lists).start()
            slot_copy(edges, e, sems.at[1, slot], slot, lists).start()

    def factors(slot):
        return (
            pltpu.make_async_copy(high.at[slot + slots], turned_high.at[slot], factor_sem),
            pltpu.make_async_copy(low.at[slot + slots], turned_low.at[slot], factor_sem),
        )

    @pl.loop(0, slots)
    def _(slot):
        @pl.when(pattern[0, slot] >= 0)
        def _():
            slot_copy(weights, w, sems.at[0, slot], slot, lists).wait()
            slot_copy(edges, e, sems.at[1, slot], slot, lists).wait()
            value = w[slot] * e[slot].astype(F32)
            w[slot] = value
            high[slot], low[slot] = split(value)

            @pl.when(pattern[0, slot] > 0)
            def _():
                high[slot + slots], low[slot + slots] = split(value.T)

            @pl.when(crossing_slot(pattern, 0, slot, lists))
            def _():
                for copy in factors(slot):
                    copy.start()

    def own(row, offset):
        inside = (row >= 0) & (row < SLAB) & (offset >= 0) & (offset < BAND)
        return jnp.where(inside, table[jnp.where(inside, row * BAND + offset, 0)], -1)

    def turned(row, offset):
        slot = own(row, offset)
        return jnp.where(slot >= 0, slot + slots, -1)

    @pl.loop(0, slots)
    def _(slot):
        i = slot // lists
        offset = pattern[0, slot]

        @pl.when(offset >= 0)
        def _():
            total[...] = jnp.zeros((tile, tile), F32)

            @pl.loop(1 - BAND, BAND)
            def _(m):
                left = jnp.where(m < 0, turned(i + m, -m), own(i + m, m))
                right = jnp.where(
                    m <= offset, own(i + m, offset - m), turned(i + offset, m - offset)
                )

                @pl.when((left >= 0) & (right >= 0))
                def _():
                    total[...] += product(high[left], low[left], high[right], low[right])

            result[slot] = w[slot] * total[...]

        @pl.when(offset < 0)
        def _():
            result[slot] = jnp.zeros((tile, tile), F32)

        pltpu.make_async_copy(result.at[slot], out.at[i, slot % lists], out_sem).start()

    @pl.loop(0, slots)
    def _(slot):
        pltpu.make_async_copy(result.at[slot], out.at[slot // lists, slot % lists], out_sem).wait()

        @pl.when(crossing_slot(pattern, 0, slot, lists))
        def _():
            for copy in factors(slot):
                copy.wait()


def main_part(pattern, weights, edges):
    _, lists, tile, _ = weights.shape
    slots = SLAB * lists
    turned = jax.ShapeDtypeStruct((slots, tile, tile), BF16)
    return call(
        functools.partial(main_kernel, lists),
        in_specs=[SMEM, ANY, ANY],
        out_specs=[ANY, ANY, ANY],
        out_shape=[jax.ShapeDtypeStruct(weights.shape, F32), turned, turned],
        scratch_shapes=[
            pltpu.VMEM((slots, tile, tile), F32),
            pltpu.VMEM((slots, tile, tile), jnp.int32),
            pltpu.VMEM((2 * slots, tile, tile), BF16),
            pltpu.VMEM((2 * slots, tile, tile), BF16),
            pltpu.VMEM((tile, tile), F32),
            pltpu.VMEM((slots, tile, tile), F32),
            pltpu.SMEM((SLAB * BAND + 1,), jnp.int32),
            pltpu.SemaphoreType.DMA((2, slots)),
            pltpu.SemaphoreType.DMA,
            pltpu.SemaphoreType.DMA,
        ],
        cost_estimate=pl.CostEstimate(
            flops=6 * 60 * tile**3, bytes_accessed=3 * weights.size * 4, transcendentals=0
        ),
    )(pattern, weights, edges)


def list_kernel(lists, back, forward, again, plan, pattern, out, table, index, raw, sums):
    slots = SLAB * lists
    first_raw = slots + SLAB
    slot_table(table, pattern, 0, lists)
    raw_count = listing(raw, plan, AHEAD, 0)
    sum_count = jnp.minimum(listing(sums, plan, BEHIND, SLAB), forward)
    half_count = diagonals_needed(out, DIAGONAL, plan, AHEAD)
    room = lax.shift_right_logical(2 * BACK - half_count, 1)
    raw_count = jnp.minimum(raw_count, room + (back - BACK))

    for row in range(SLAB):
        index[row * BAND] = slots + row
        for offset in range(1, BAND):
            index[row * BAND + offset] = -1

    @pl.loop(0, raw_count)
    def _(k):
        place = jnp.where(k < room, k, BACK + k - room)
        out[PLACE + k] = place
        index[raw[k]] = first_raw + place

    for place in range(TARGET, PLACE):
        out[place] = 0
    if not again:
        for row in range(SLAB):
            out[TARGET + row * lists] = 1

    def jobs_of(slot, count):
        i = slot // lists
        offset = pattern[0, slot]
        for m in range(1, BAND):
            row = i + m - SLAB
            left = index[jnp.maximum(row, 0) * BAND + m]
            column = i + offset
            straight = m <= offset
            gap = jnp.where(straight, offset - m, m - offset)
            later = straight | (column >= SLAB)
            next_row = jnp.where(straight, row, column - SLAB)
            theirs = index[jnp.clip(next_row, 0, SLAB - 1) * BAND + gap]
            ours = table[jnp.clip(column, 0, SLAB - 1) * BAND + gap]
            right = jnp.where(later, theirs, ours)
            valid = (offset >= 0) & (row >= 0) & (left >= 0) & (right >= 0)
            if again:
                fresh = first_raw + BACK
                valid = valid & ((left >= fresh) | (right >= fresh))
            turned = valid & later & ~straight
            out[JOB_SLOT + count] = slot
            out[JOB_LEFT + count] = left
            out[JOB_RIGHT + count] = jnp.where(turned, right + back, right)
            out[TARGET + jnp.where(valid, slot, slots)] = 1
            out[FACTOR + jnp.where(valid & (right < first_raw), right, first_raw)] = 1
            out[TURNED + jnp.where(turned, right - first_raw, back)] = 1
            count = count + valid.astype(jnp.int32)
        return count

    jobs = lax.fori_loop(0, slots, jobs_of, jnp.int32(0))

    @pl.loop(0, sum_count)
    def _(k):
        slot = table[sums[k] // BAND * BAND + sums[k] % BAND - sums[k] // BAND]
        out[SUM_SLOT + k] = slot
        if again:
            out[TARGET + jnp.where(k >= FORWARD, slot, slots)] = 1
        else:
            out[TARGET + slot] = 1

    out[JOBS] = jobs
    out[RAWS] = raw_count
    out[SUMS] = sum_count
    out[DIAGONALS] = half_count


def product_list(back, forward, again, plan, pattern, lists):
    small = pltpu.SMEM((SLAB * BAND,), jnp.int32)
    return call(
        functools.partial(list_kernel, lists, back, forward, again),
        in_specs=[SMEM, SMEM],
        out_specs=SMEM,
        out_shape=jax.ShapeDtypeStruct((LIST_SIZE,), jnp.int32),
        scratch_shapes=[pltpu.SMEM((SLAB * BAND + 1,), jnp.int32), small, small, small],
    )(plan, pattern)


def rest_kernel(
    lists, again, todo, weights, edges, turned_high, turned_low, squares, message, sums, before, out,
    w, e, high, low, result, sems, out_sem,
):
    tile = weights.shape[-1]
    half = tile // 2
    slots = SLAB * lists
    back = message.shape[0] // tile
    first_raw = slots + SLAB

    def inputs(slot):
        return (
            slot_copy(weights, w, sems.at[0, slot], slot, lists),
            slot_copy(edges, e, sems.at[1, slot], slot, lists),
            slot_copy(before, result, sems.at[2, slot], slot, lists),
        )

    def factors(slot):
        return (
            pltpu.make_async_copy(turned_high.at[slot], high.at[slot], sems.at[3, slot]),
            pltpu.make_async_copy(turned_low.at[slot], low.at[slot], sems.at[4, slot]),
        )

    def output(slot):
        return pltpu.make_async_copy(result.at[slot], out.at[slot // lists, slot % lists], out_sem)

    @pl.loop(0, slots)
    def _(slot):
        @pl.when(todo[FACTOR + slot] == 1)
        def _():
            for copy in factors(slot):
                copy.start()

        @pl.when(todo[TARGET + slot] == 1)
        def _():
            for copy in inputs(slot):
                copy.start()

    @pl.loop(0, todo[DIAGONALS])
    def _(k):
        row = todo[DIAGONAL + k]

        @pl.when(todo[FACTOR + slots + row] == 1)
        def _():
            def store(first, column, quarter):
                part = (slots + row, pl.ds(first, half), pl.ds(column, half))
                high[part], low[part] = split(quarter)

            part = message[pl.ds(pl.multiple_of((2 * BACK - 1 - k) * half, half), half), :]
            unfold(store, part[:, :half], part[:, half:], jnp.zeros((1, half), F32))

    @pl.loop(0, todo[RAWS])
    def _(k):
        place = todo[PLACE + k]
        value = message[pl.ds(pl.multiple_of(place * tile, tile), tile), :]
        high[first_raw + place], low[first_raw + place] = split(value)

        @pl.when(todo[TURNED + place] == 1)
        def _():
            high[first_raw + back + place], low[first_raw + back + place] = split(value.T)

    @pl.loop(0, slots)
    def _(slot):
        @pl.when(todo[FACTOR + slot] == 1)
        def _():
            for copy in factors(slot):
                copy.wait()

        @pl.when(todo[TARGET + slot] == 1)
        def _():
            for copy in inputs(slot):
                copy.wait()
            w[slot] = w[slot] * e[slot].astype(F32)

    @pl.loop(0, 0 if again else SLAB)
    def _(i):
        def store(first, column, quarter):
            part = (i * lists, pl.ds(first, half), pl.ds(column, half))
            result[part] += w[part] * quarter

        part = squares[pl.ds(pl.multiple_of(i * half, half), half), :]
        rows = squares[SLAB * half :, :half]
        row = lax.broadcasted_iota(jnp.int32, rows.shape, 0)
        diagonal = jnp.sum(jnp.where(row == i, rows, 0.0), axis=0, keepdims=True)
        unfold(store, part[:, :half], part[:, half:], diagonal)

    @pl.loop(FORWARD if again else 0, todo[SUMS])
    def _(k):
        slot = todo[SUM_SLOT + k]
        result[slot] += w[slot] * sums[k]

    @pl.loop(0, todo[JOBS])
    def _(job):
        slot, left, right = todo[JOB_SLOT + job], todo[JOB_LEFT + job], todo[JOB_RIGHT + job]
        value = product(high[left], low[left], high[right], low[right])
        result[slot] += w[slot] * value

    @pl.loop(0, slots)
    def _(slot):
        @pl.when(todo[TARGET + slot] == 1)
        def _():
            output(slot).start()

    @pl.loop(0, slots)
    def _(slot):
        @pl.when(todo[TARGET + slot] == 1)
        def _():
            output(slot).wait()


def rest_part(again, todo, weights, edges, high, low, squares, message, sums, before):
    _, lists, tile, _ = weights.shape
    slots = SLAB * lists
    factors = slots + SLAB + 2 * (message.shape[0] // tile)
    return call(
        functools.partial(rest_kernel, lists, again),
        in_specs=[SMEM, ANY, ANY, ANY, ANY, VMEM, VMEM, VMEM, ANY],
        out_specs=ANY,
        out_shape=jax.ShapeDtypeStruct(weights.shape, F32),
        input_output_aliases={8: 0},
        scratch_shapes=[
            pltpu.VMEM((slots, tile, tile), F32),
            pltpu.VMEM((slots, tile, tile), jnp.int32),
            pltpu.VMEM((factors, tile, tile), BF16),
            pltpu.VMEM((factors, tile, tile), BF16),
            pltpu.VMEM((slots, tile, tile), F32),
            pltpu.SemaphoreType.DMA((5, slots)),
            pltpu.SemaphoreType.DMA,
        ],
    )(todo, weights, edges, high, low, squares, message, sums, before)


def merged(value, bits):
    count = lax.axis_size(AXES)
    for bit in bits:
        other = lax.ppermute(value, AXES, [(device, device ^ bit) for device in range(count)])
        value = jnp.maximum(value, other)
    return value


def shards(weights, edges, offsets, counts):
    slab_count, lists = offsets.shape
    tile = weights.shape[-1]
    slabs = lax.axis_size(AXES)
    columns = lax.axis_size(AXES[1])
    bits = [1 << bit for bit in range(slabs.bit_length() - 1)]
    listed = jnp.arange(lists)[None, :] < counts[:, None]
    pattern = jnp.where(listed, offsets, -1).reshape(1, slab_count * lists)
    pattern = jnp.pad(pattern, ((0, 0), (0, LANES - slab_count * lists)), constant_values=-1)
    empty = jnp.full((5, LANES), -1, jnp.int32)
    patterns = jnp.concatenate([shifted(pattern, 1), pattern, shifted(pattern, -1), empty])
    mine = jnp.arange(slabs)[:, None] == lax.axis_index(AXES)
    everyone = merged(jnp.where(mine, pattern, -1), [bit for bit in bits if bit < columns])

    everyone, patterns = lax.optimization_barrier((everyone, patterns))
    plan, _ = travel_plan(patterns, lists)
    message_out, sums_out, more_message, more_sums = pack_tiles(plan, pattern, weights, edges)
    message_out, sums_out, pattern = lax.optimization_barrier((message_out, sums_out, pattern))
    message = shifted(message_out, -1)
    sums = shifted(sums_out, 1)
    squares_out = square_diagonals(pattern, weights, edges)
    squares_out, pattern = lax.optimization_barrier((squares_out, pattern))
    squares = shifted(squares_out, 1)

    todo = product_list(BACK, FORWARD, False, plan, pattern, lists)
    support, high, low = main_part(pattern, weights, edges)
    everyone, support = lax.optimization_barrier((everyone, support))
    _, level = travel_plan(merged(everyone, [bit for bit in bits if bit >= columns]), lists)
    support = rest_part(
        False, todo, weights, edges, high, low, squares, message, sums, support
    )

    def branch(back, forward):
        def run(
            support, plan, pattern, weights, edges, high, low, squares, message, sums, more_message, more_sums
        ):
            if not back:
                return support
            message = jnp.concatenate([message, shifted(more_message[: back * tile], -1)])
            sums = jnp.concatenate([sums, shifted(more_sums[:forward], 1)])
            todo = product_list(BACK + back, FORWARD + forward, True, plan, pattern, lists)
            return rest_part(
                True, todo, weights, edges, high, low, squares, message, sums, support
            )

        return run

    return lax.switch(
        level[0],
        [branch(*sizes) for sizes in MORE],
        support, plan, pattern, weights, edges, high, low, squares, message, sums, more_message, more_sums,
    )


def solution(mesh):
    in_specs = (
        P(AXES, None, None, None),
        P(AXES, None, None, None),
        P(AXES, None),
        P(AXES),
    )
    out_specs = P(AXES, None, None, None)
    return jax.shard_map(shards, mesh=mesh, in_specs=in_specs, out_specs=out_specs, check_vma=False)
```

```python
import functools

import jax
import jax.numpy as jnp
from jax import lax
from jax.experimental import pallas as pl
from jax.experimental.pallas import tpu as pltpu
from jax.sharding import PartitionSpec as P

BAND = 6
SLAB = BAND - 1
LANES = 128
AXES = ("row", "col")
BACK, FORWARD = 10, 3
MORE = ((0, 0), (2, 1), (8, 6))
BEHIND, AHEAD = 0, 1
JOBS, RAWS, SUMS, DIAGONALS = 0, 1, 2, 3
TARGET, FACTOR, TURNED, PLACE, SUM_SLOT, DIAGONAL = 8, 32, 64, 96, 128, 144
JOB_SLOT, JOB_LEFT, JOB_RIGHT, LIST_SIZE = 160, 272, 384, 512
VMEM_LIMIT = 56 * 1024 * 1024

F32 = jnp.float32
BF16 = jnp.bfloat16
ANY = pl.BlockSpec(memory_space=pl.ANY)
SMEM = pl.BlockSpec(memory_space=pltpu.SMEM)
VMEM = pl.BlockSpec(memory_space=pltpu.VMEM)


def shifted(value, steps):
    count = lax.axis_size(AXES)
    first, last = (max(0, -steps), min(count, count - steps))
    return lax.ppermute(value, AXES, [(source, source + steps) for source in range(first, last)])


def split(value):
    high = value.astype(BF16)
    low = (value - high.astype(F32)).astype(BF16)
    return high, low


def dot(left, right):
    return jnp.dot(left, right, preferred_element_type=F32)


def product(left_high, left_low, right_high, right_low):
    return dot(left_high, right_high) + (dot(left_high, right_low) + dot(left_low, right_high))


def iotas(size):
    rows = lax.broadcasted_iota(jnp.int32, (size, size), 0)
    columns = lax.broadcasted_iota(jnp.int32, (size, size), 1)
    return rows, columns


def folded(tile):
    half = tile.shape[0] // 2
    rows, columns = iotas(half)
    lower_right = tile[half:, half:]
    mixed = jnp.where(rows <= columns, tile[:half, :half], lower_right)
    diagonal = jnp.sum(jnp.where(rows == columns, lower_right, 0.0), axis=0, keepdims=True)
    return mixed, tile[:half, half:], diagonal


def unfold(store, mixed, upper_right, diagonal):
    half = mixed.shape[0]
    rows, columns = iotas(half)
    turned = mixed.T
    store(0, 0, jnp.where(rows <= columns, mixed, turned))
    store(0, half, upper_right)
    store(half, 0, upper_right.T)
    lower_right = jnp.where(rows > columns, mixed, turned)
    store(half, half, jnp.where(rows == columns, diagonal, lower_right))


def slot_table(table, pattern, row, lists):
    for place in range(SLAB * BAND):
        table[place] = -1
    for slot in range(SLAB * lists):
        offset = pattern[row, slot]
        table[jnp.where(offset >= 0, slot // lists * BAND + offset, SLAB * BAND)] = slot


def listing(items, plan, row, first):
    count = jnp.int32(0)
    for i in range(SLAB):
        mask = plan[row, first + i]
        for bit in range(1, BAND):
            items[count] = i * BAND + bit
            count = count + ((mask >> bit) & 1)
    return count


def diagonals_needed(items, first, plan, row):
    count = jnp.int32(0)
    for i in range(SLAB):
        items[first + count] = i
        count = count + (plan[row, i] & 1)
    return count


def slot_copy(source, target, semaphore, slot, lists):
    return pltpu.make_async_copy(source.at[slot // lists, slot % lists], target.at[slot], semaphore)


def call(kernel, **kwargs):
    return pl.pallas_call(
        kernel,
        compiler_params=pltpu.CompilerParams(vmem_limit_bytes=VMEM_LIMIT),
        **kwargs,
    )


def crossing_slot(pattern, row, slot, lists):
    offset = pattern[row, slot]
    return (offset >= 0) & (slot // lists + offset >= SLAB)


def square_kernel(lists, pattern, weights, edges, out, w, e, total, table, sems):
    tile = weights.shape[-1]
    half = tile // 2
    slot_table(table, pattern, 0, lists)

    @pl.loop(0, SLAB * lists)
    def _(slot):
        @pl.when(crossing_slot(pattern, 0, slot, lists))
        def _():
            slot_copy(weights, w, sems.at[0, slot], slot, lists).start()
            slot_copy(edges, e, sems.at[1, slot], slot, lists).start()

    out[SLAB * half :, :] = jnp.zeros((8, tile), F32)
    for j in range(SLAB):
        total[...] = jnp.zeros((tile, tile), F32)

        @pl.loop(j, SLAB)
        def _(i):
            slot = table[i * BAND + SLAB + j - i]

            @pl.when(slot >= 0)
            def _():
                slot_copy(weights, w, sems.at[0, slot], slot, lists).wait()
                slot_copy(edges, e, sems.at[1, slot], slot, lists).wait()
                value = w[slot] * e[slot].astype(F32)
                total[...] += product(*split(value.T), *split(value))

        mixed, upper_right, diagonal = folded(total[...])
        out[j * half : (j + 1) * half, :half] = mixed
        out[j * half : (j + 1) * half, half:] = upper_right
        out[SLAB * half + j : SLAB * half + j + 1, :half] = diagonal


def square_diagonals(pattern, weights, edges):
    _, lists, tile, _ = weights.shape
    return call(
        functools.partial(square_kernel, lists),
        in_specs=[SMEM, ANY, ANY],
        out_specs=VMEM,
        out_shape=jax.ShapeDtypeStruct((SLAB * tile // 2 + 8, tile), F32),
        scratch_shapes=[
            pltpu.VMEM((SLAB * lists, tile, tile), F32),
            pltpu.VMEM((SLAB * lists, tile, tile), jnp.int32),
            pltpu.VMEM((tile, tile), F32),
            pltpu.SMEM((SLAB * BAND + 1,), jnp.int32),
            pltpu.SemaphoreType.DMA((2, SLAB * lists)),
        ],
    )(pattern, weights, edges)


def plan_kernel(lists, patterns, plan, choice):
    offsets = patterns[...]
    slabs = offsets.shape[0]
    lane = lax.broadcasted_iota(jnp.int32, offsets.shape, 1)
    row = lax.broadcasted_iota(jnp.int32, offsets.shape, 0)
    inside = (offsets >= 0) & (lane < SLAB * lists)
    bits = jnp.where(inside, jnp.left_shift(1, jnp.maximum(offsets, 0)), 0)

    def ahead(value, steps):
        return pltpu.roll(value, LANES - steps, 1) if steps else value

    mask = bits
    for a in range(1, lists):
        mask = mask | ahead(bits, a)
    own = [ahead(mask, i * lists) for i in range(SLAB)]
    rows = own + [pltpu.roll(value, slabs - 1, 0) for value in own]

    def has(r, offset):
        return jnp.right_shift(rows[r], offset) & 1

    zero = jnp.zeros_like(mask)
    need = [zero] * SLAB
    for i in range(SLAB):
        for m in range(SLAB - i, BAND):
            middle = i + m
            wanted = zero
            for t in range(BAND):
                target = i + t
                if target >= SLAB:
                    other, offset = (middle, t - m) if m <= t else (target, m - t)
                    used = has(i, t) & has(middle, m) & has(other, offset)
                    wanted = wanted | used
                    place = other - SLAB
                    need[place] = need[place] | jnp.left_shift(used, offset)
                elif m > t:
                    wanted = wanted | (has(i, t) & has(middle, m) & has(target, m - t))
            need[middle - SLAB] = need[middle - SLAB] | jnp.left_shift(wanted, m)
    crossing = [jnp.right_shift(jnp.left_shift(rows[i], i), SLAB) for i in range(SLAB)]
    partial = []
    for j in range(SLAB):
        cover = zero
        for i in range(SLAB):
            cover = cover | jnp.where(jnp.right_shift(crossing[i], j) & 1 == 1, crossing[i], 0)
        listed = jnp.left_shift(rows[SLAB + j], j) & ((1 << SLAB) - (2 << j))
        partial.append(cover & listed)
    def total(group, bits):
        count = zero
        for value in group:
            for bit in bits:
                count = count + (jnp.right_shift(value, bit) & 1)
        return count

    room = jnp.right_shift(2 * BACK - total(need, (0,)), 1)
    extra = []
    for count in (total(need, range(1, BAND)) - room, total(partial, range(1, BAND)) - FORWARD):
        count = jnp.where((lane == 0) & (row < slabs - 1), count, 0)
        extra.append(jnp.max(count.astype(F32)).astype(jnp.int32))
    result = zero
    for place, value in enumerate(need + partial):
        value = pltpu.roll(value, place, 1) if place else value
        result = jnp.where((lane == place) & (row < slabs - 1), value, result)
    plan[...] = result
    level = jnp.int32(0)
    for back, forward in MORE[:-1]:
        level = level + ((extra[0] > back) | (extra[1] > forward)).astype(jnp.int32)
    choice[0] = level


def travel_plan(patterns, lists):
    return call(
        functools.partial(plan_kernel, lists),
        in_specs=[VMEM],
        out_specs=[VMEM, SMEM],
        out_shape=[
            jax.ShapeDtypeStruct(patterns.shape, jnp.int32),
            jax.ShapeDtypeStruct((1,), jnp.int32),
        ],
    )(patterns)


def pack_kernel(
    lists, plan, pattern, weights, edges, message, squares_out, more_tiles_out, more_squares_out,
    w, e, total, halves, table, raw, sums, diagonals, needed, sems, tile_sem, half_sem, total_sem,
):
    tile = weights.shape[-1]
    half = tile // 2
    slots = SLAB * lists
    slot_table(table, pattern, 0, lists)
    raw_count = listing(raw, plan, BEHIND, 0)
    sum_count = listing(sums, plan, AHEAD, SLAB)
    half_count = diagonals_needed(diagonals, 0, plan, BEHIND)
    room = lax.shift_right_logical(2 * BACK - half_count, 1)

    for slot in range(slots + 1):
        needed[slot] = 0

    def factors(k, i):
        first = SLAB + sums[k] // BAND - i
        second = SLAB + sums[k] % BAND - i
        inside = (first < BAND) & (second < BAND)
        left = table[i * BAND + jnp.minimum(first, BAND - 1)]
        right = table[i * BAND + jnp.minimum(second, BAND - 1)]
        return left, right, inside & (left >= 0) & (right >= 0)

    @pl.loop(0, raw_count)
    def _(k):
        needed[table[raw[k]]] = 1

    @pl.loop(0, half_count)
    def _(k):
        needed[table[diagonals[k] * BAND]] = 1

    @pl.loop(0, sum_count)
    def _(k):
        for i in range(SLAB):
            left, right, both = factors(k, i)
            needed[jnp.where(both, left, slots)] = 1
            needed[jnp.where(both, right, slots)] = 1

    @pl.loop(0, slots)
    def _(slot):
        @pl.when(needed[slot] == 1)
        def _():
            slot_copy(weights, w, sems.at[0, slot], slot, lists).start()
            slot_copy(edges, e, sems.at[1, slot], slot, lists).start()

    @pl.loop(0, slots)
    def _(slot):
        @pl.when(needed[slot] == 1)
        def _():
            slot_copy(weights, w, sems.at[0, slot], slot, lists).wait()
            slot_copy(edges, e, sems.at[1, slot], slot, lists).wait()
            w[slot] = w[slot] * e[slot].astype(F32)

    @pl.loop(0, raw_count)
    def _(k):
        source = w.at[table[raw[k]]]

        @pl.when(k < room)
        def _():
            rows = pl.ds(pl.multiple_of(k * tile, tile), tile)
            pltpu.make_async_copy(source, message.at[rows], tile_sem).start()

        @pl.when(k >= room)
        def _():
            rows = pl.ds(pl.multiple_of((k - room) * tile, tile), tile)
            pltpu.make_async_copy(source, more_tiles_out.at[rows], tile_sem).start()

    @pl.loop(0, half_count)
    def _(k):
        mixed, upper_right, _ = folded(w[table[diagonals[k] * BAND]])
        halves[k, :, :half] = mixed
        halves[k, :, half:] = upper_right
        rows = pl.ds(pl.multiple_of((2 * BACK - 1 - k) * half, half), half)
        pltpu.make_async_copy(halves.at[k], message.at[rows], half_sem).start()

    @pl.loop(0, sum_count)
    def _(k):
        total[k] = jnp.zeros((tile, tile), F32)

        @pl.loop(0, SLAB)
        def _(i):
            left, right, both = factors(k, i)

            @pl.when(both)
            def _():
                total[k] += product(*split(w[left].T), *split(w[right]))

        @pl.when(k < FORWARD)
        def _():
            pltpu.make_async_copy(total.at[k], squares_out.at[k], total_sem).start()

        @pl.when(k >= FORWARD)
        def _():
            target = more_squares_out.at[k - FORWARD]
            pltpu.make_async_copy(total.at[k], target, total_sem).start()

    @pl.loop(0, raw_count)
    def _(k):
        pltpu.make_async_copy(w.at[0], message.at[pl.ds(0, tile)], tile_sem).wait()

    @pl.loop(0, half_count)
    def _(k):
        pltpu.make_async_copy(halves.at[0], message.at[pl.ds(0, half)], half_sem).wait()

    @pl.loop(0, sum_count)
    def _(k):
        pltpu.make_async_copy(total.at[k], squares_out.at[0], total_sem).wait()


def pack_tiles(plan, pattern, weights, edges):
    _, lists, tile, _ = weights.shape
    slots = SLAB * lists
    most_back, most_forward = MORE[-1]
    return call(
        functools.partial(pack_kernel, lists),
        in_specs=[SMEM, SMEM, ANY, ANY],
        out_specs=[ANY] * 4,
        out_shape=[
            jax.ShapeDtypeStruct((BACK * tile, tile), F32),
            jax.ShapeDtypeStruct((FORWARD, tile, tile), F32),
            jax.ShapeDtypeStruct((most_back * tile, tile), F32),
            jax.ShapeDtypeStruct((most_forward, tile, tile), F32),
        ],
        scratch_shapes=[
            pltpu.VMEM((slots, tile, tile), F32),
            pltpu.VMEM((slots, tile, tile), jnp.int32),
            pltpu.VMEM((FORWARD + most_forward, tile, tile), F32),
            pltpu.VMEM((SLAB, tile // 2, tile), F32),
            pltpu.SMEM((SLAB * BAND + 1,), jnp.int32),
            pltpu.SMEM((SLAB * BAND,), jnp.int32),
            pltpu.SMEM((SLAB * BAND,), jnp.int32),
            pltpu.SMEM((SLAB + 1,), jnp.int32),
            pltpu.SMEM((slots + 1,), jnp.int32),
            pltpu.SemaphoreType.DMA((2, slots)),
            pltpu.SemaphoreType.DMA,
            pltpu.SemaphoreType.DMA,
            pltpu.SemaphoreType.DMA,
        ],
    )(plan, pattern, weights, edges)


def main_kernel(
    lists, pattern, weights, edges, out, turned_high, turned_low,
    w, e, high, low, total, result, table, sems, out_sem, factor_sem,
):
    tile = weights.shape[-1]
    slots = SLAB * lists
    slot_table(table, pattern, 0, lists)

    @pl.loop(0, slots)
    def _(slot):
        @pl.when(pattern[0, slot] >= 0)
        def _():
            slot_copy(weights, w, sems.at[0, slot], slot, lists).start()
            slot_copy(edges, e, sems.at[1, slot], slot, lists).start()

    def factors(slot):
        return (
            pltpu.make_async_copy(high.at[slot + slots], turned_high.at[slot], factor_sem),
            pltpu.make_async_copy(low.at[slot + slots], turned_low.at[slot], factor_sem),
        )

    @pl.loop(0, slots)
    def _(slot):
        @pl.when(pattern[0, slot] >= 0)
        def _():
            slot_copy(weights, w, sems.at[0, slot], slot, lists).wait()
            slot_copy(edges, e, sems.at[1, slot], slot, lists).wait()
            value = w[slot] * e[slot].astype(F32)
            w[slot] = value
            high[slot], low[slot] = split(value)

            @pl.when(pattern[0, slot] > 0)
            def _():
                high[slot + slots], low[slot + slots] = split(value.T)

            @pl.when(crossing_slot(pattern, 0, slot, lists))
            def _():
                for copy in factors(slot):
                    copy.start()

    def own(row, offset):
        inside = (row >= 0) & (row < SLAB) & (offset >= 0) & (offset < BAND)
        return jnp.where(inside, table[jnp.where(inside, row * BAND + offset, 0)], -1)

    def turned(row, offset):
        slot = own(row, offset)
        return jnp.where(slot >= 0, slot + slots, -1)

    @pl.loop(0, slots)
    def _(slot):
        i = slot // lists
        offset = pattern[0, slot]

        @pl.when(offset >= 0)
        def _():
            total[...] = jnp.zeros((tile, tile), F32)

            @pl.loop(1 - BAND, BAND)
            def _(m):
                left = jnp.where(m < 0, turned(i + m, -m), own(i + m, m))
                right = jnp.where(
                    m <= offset, own(i + m, offset - m), turned(i + offset, m - offset)
                )

                @pl.when((left >= 0) & (right >= 0))
                def _():
                    total[...] += product(high[left], low[left], high[right], low[right])

            result[slot] = w[slot] * total[...]

        @pl.when(offset < 0)
        def _():
            result[slot] = jnp.zeros((tile, tile), F32)

        pltpu.make_async_copy(result.at[slot], out.at[i, slot % lists], out_sem).start()

    @pl.loop(0, slots)
    def _(slot):
        pltpu.make_async_copy(result.at[slot], out.at[slot // lists, slot % lists], out_sem).wait()

        @pl.when(crossing_slot(pattern, 0, slot, lists))
        def _():
            for copy in factors(slot):
                copy.wait()


def main_part(pattern, weights, edges):
    _, lists, tile, _ = weights.shape
    slots = SLAB * lists
    turned = jax.ShapeDtypeStruct((slots, tile, tile), BF16)
    return call(
        functools.partial(main_kernel, lists),
        in_specs=[SMEM, ANY, ANY],
        out_specs=[ANY, ANY, ANY],
        out_shape=[jax.ShapeDtypeStruct(weights.shape, F32), turned, turned],
        scratch_shapes=[
            pltpu.VMEM((slots, tile, tile), F32),
            pltpu.VMEM((slots, tile, tile), jnp.int32),
            pltpu.VMEM((2 * slots, tile, tile), BF16),
            pltpu.VMEM((2 * slots, tile, tile), BF16),
            pltpu.VMEM((tile, tile), F32),
            pltpu.VMEM((slots, tile, tile), F32),
            pltpu.SMEM((SLAB * BAND + 1,), jnp.int32),
            pltpu.SemaphoreType.DMA((2, slots)),
            pltpu.SemaphoreType.DMA,
            pltpu.SemaphoreType.DMA,
        ],
        cost_estimate=pl.CostEstimate(
            flops=6 * 60 * tile**3, bytes_accessed=3 * weights.size * 4, transcendentals=0
        ),
    )(pattern, weights, edges)


def list_kernel(lists, plan, pattern, out, table, index, raw, sums):
    back = BACK + MORE[-1][0]
    slots = SLAB * lists
    first_raw = slots + SLAB
    slot_table(table, pattern, 0, lists)
    raw_count = listing(raw, plan, AHEAD, 0)
    sum_count = listing(sums, plan, BEHIND, SLAB)
    half_count = diagonals_needed(out, DIAGONAL, plan, AHEAD)
    room = lax.shift_right_logical(2 * BACK - half_count, 1)

    for row in range(SLAB):
        index[row * BAND] = slots + row
        for offset in range(1, BAND):
            index[row * BAND + offset] = -1

    @pl.loop(0, raw_count)
    def _(k):
        place = jnp.where(k < room, k, BACK + k - room)
        out[PLACE + k] = place
        index[raw[k]] = first_raw + place

    for place in range(TARGET, PLACE):
        out[place] = 0
    for row in range(SLAB):
        out[TARGET + row * lists] = 1

    def jobs_of(slot, count):
        i = slot // lists
        offset = pattern[0, slot]
        for m in range(1, BAND):
            row = i + m - SLAB
            left = index[jnp.maximum(row, 0) * BAND + m]
            column = i + offset
            straight = m <= offset
            gap = jnp.where(straight, offset - m, m - offset)
            later = straight | (column >= SLAB)
            next_row = jnp.where(straight, row, column - SLAB)
            theirs = index[jnp.clip(next_row, 0, SLAB - 1) * BAND + gap]
            ours = table[jnp.clip(column, 0, SLAB - 1) * BAND + gap]
            right = jnp.where(later, theirs, ours)
            valid = (offset >= 0) & (row >= 0) & (left >= 0) & (right >= 0)
            turned = valid & later & ~straight
            out[JOB_SLOT + count] = slot
            out[JOB_LEFT + count] = left
            out[JOB_RIGHT + count] = jnp.where(turned, right + back, right)
            out[TARGET + jnp.where(valid, slot, slots)] = 1
            out[FACTOR + jnp.where(valid & (right < first_raw), right, first_raw)] = 1
            out[TURNED + jnp.where(turned, right - first_raw, back)] = 1
            count = count + valid.astype(jnp.int32)
        return count

    jobs = lax.fori_loop(0, slots, jobs_of, jnp.int32(0))

    @pl.loop(0, sum_count)
    def _(k):
        slot = table[sums[k] // BAND * BAND + sums[k] % BAND - sums[k] // BAND]
        out[SUM_SLOT + k] = slot
        out[TARGET + slot] = 1

    out[JOBS] = jobs
    out[RAWS] = raw_count
    out[SUMS] = sum_count
    out[DIAGONALS] = half_count


def product_list(plan, pattern, lists):
    small = pltpu.SMEM((SLAB * BAND,), jnp.int32)
    return call(
        functools.partial(list_kernel, lists),
        in_specs=[SMEM, SMEM],
        out_specs=SMEM,
        out_shape=jax.ShapeDtypeStruct((LIST_SIZE,), jnp.int32),
        scratch_shapes=[pltpu.SMEM((SLAB * BAND + 1,), jnp.int32), small, small, small],
    )(plan, pattern)


def rest_kernel(
    lists, todo, weights, edges, turned_high, turned_low, squares, message, sums, more_message, more_sums,
    before, out, w, e, high, low, result, stage, sems, out_sem, stage_sem,
):
    tile = weights.shape[-1]
    half = tile // 2
    slots = SLAB * lists
    back = (message.shape[0] + more_message.shape[0]) // tile
    first_raw = slots + SLAB

    def inputs(slot):
        return (
            slot_copy(weights, w, sems.at[0, slot], slot, lists),
            slot_copy(edges, e, sems.at[1, slot], slot, lists),
            slot_copy(before, result, sems.at[2, slot], slot, lists),
        )

    def factors(slot):
        return (
            pltpu.make_async_copy(turned_high.at[slot], high.at[slot], sems.at[3, slot]),
            pltpu.make_async_copy(turned_low.at[slot], low.at[slot], sems.at[4, slot]),
        )

    def output(slot):
        return pltpu.make_async_copy(result.at[slot], out.at[slot // lists, slot % lists], out_sem)

    @pl.loop(0, slots)
    def _(slot):
        @pl.when(todo[FACTOR + slot] == 1)
        def _():
            for copy in factors(slot):
                copy.start()

        @pl.when(todo[TARGET + slot] == 1)
        def _():
            for copy in inputs(slot):
                copy.start()

    @pl.loop(0, todo[DIAGONALS])
    def _(k):
        row = todo[DIAGONAL + k]

        @pl.when(todo[FACTOR + slots + row] == 1)
        def _():
            def store(first, column, quarter):
                part = (slots + row, pl.ds(first, half), pl.ds(column, half))
                high[part], low[part] = split(quarter)

            part = message[pl.ds(pl.multiple_of((2 * BACK - 1 - k) * half, half), half), :]
            unfold(store, part[:, :half], part[:, half:], jnp.zeros((1, half), F32))

    @pl.loop(0, todo[RAWS])
    def _(k):
        place = todo[PLACE + k]

        @pl.when(place < BACK)
        def _():
            stage[...] = message[pl.ds(pl.multiple_of(place * tile, tile), tile), :]

        @pl.when(place >= BACK)
        def _():
            rows = pl.ds(pl.multiple_of((place - BACK) * tile, tile), tile)
            copy = pltpu.make_async_copy(more_message.at[rows], stage, stage_sem)
            copy.start()
            copy.wait()

        value = stage[...]
        high[first_raw + place], low[first_raw + place] = split(value)

        @pl.when(todo[TURNED + place] == 1)
        def _():
            high[first_raw + back + place], low[first_raw + back + place] = split(value.T)

    @pl.loop(0, slots)
    def _(slot):
        @pl.when(todo[FACTOR + slot] == 1)
        def _():
            for copy in factors(slot):
                copy.wait()

        @pl.when(todo[TARGET + slot] == 1)
        def _():
            for copy in inputs(slot):
                copy.wait()
            w[slot] = w[slot] * e[slot].astype(F32)

    @pl.loop(0, SLAB)
    def _(i):
        def store(first, column, quarter):
            part = (i * lists, pl.ds(first, half), pl.ds(column, half))
            result[part] += w[part] * quarter

        part = squares[pl.ds(pl.multiple_of(i * half, half), half), :]
        rows = squares[SLAB * half :, :half]
        row = lax.broadcasted_iota(jnp.int32, rows.shape, 0)
        diagonal = jnp.sum(jnp.where(row == i, rows, 0.0), axis=0, keepdims=True)
        unfold(store, part[:, :half], part[:, half:], diagonal)

    @pl.loop(0, todo[SUMS])
    def _(k):
        slot = todo[SUM_SLOT + k]

        @pl.when(k < FORWARD)
        def _():
            stage[...] = sums[k]

        @pl.when(k >= FORWARD)
        def _():
            copy = pltpu.make_async_copy(more_sums.at[k - FORWARD], stage, stage_sem)
            copy.start()
            copy.wait()

        result[slot] += w[slot] * stage[...]

    @pl.loop(0, todo[JOBS])
    def _(job):
        slot, left, right = todo[JOB_SLOT + job], todo[JOB_LEFT + job], todo[JOB_RIGHT + job]
        value = product(high[left], low[left], high[right], low[right])
        result[slot] += w[slot] * value

    @pl.loop(0, slots)
    def _(slot):
        @pl.when(todo[TARGET + slot] == 1)
        def _():
            output(slot).start()

    @pl.loop(0, slots)
    def _(slot):
        @pl.when(todo[TARGET + slot] == 1)
        def _():
            output(slot).wait()


def rest_part(todo, weights, edges, high, low, squares, message, sums, more_message, more_sums, before):
    _, lists, tile, _ = weights.shape
    slots = SLAB * lists
    factors = slots + SLAB + 2 * (BACK + MORE[-1][0])
    return call(
        functools.partial(rest_kernel, lists),
        in_specs=[SMEM, ANY, ANY, ANY, ANY, VMEM, VMEM, VMEM, ANY, ANY, ANY],
        out_specs=ANY,
        out_shape=jax.ShapeDtypeStruct(weights.shape, F32),
        input_output_aliases={10: 0},
        scratch_shapes=[
            pltpu.VMEM((slots, tile, tile), F32),
            pltpu.VMEM((slots, tile, tile), jnp.int32),
            pltpu.VMEM((factors, tile, tile), BF16),
            pltpu.VMEM((factors, tile, tile), BF16),
            pltpu.VMEM((slots, tile, tile), F32),
            pltpu.VMEM((tile, tile), F32),
            pltpu.SemaphoreType.DMA((5, slots)),
            pltpu.SemaphoreType.DMA,
            pltpu.SemaphoreType.DMA,
        ],
    )(todo, weights, edges, high, low, squares, message, sums, more_message, more_sums, before)


def merged(value, bits):
    count = lax.axis_size(AXES)
    for bit in bits:
        other = lax.ppermute(value, AXES, [(device, device ^ bit) for device in range(count)])
        value = jnp.maximum(value, other)
    return value


def shards(weights, edges, offsets, counts):
    slab_count, lists = offsets.shape
    tile = weights.shape[-1]
    slabs = lax.axis_size(AXES)
    columns = lax.axis_size(AXES[1])
    bits = [1 << bit for bit in range(slabs.bit_length() - 1)]
    listed = jnp.arange(lists)[None, :] < counts[:, None]
    pattern = jnp.where(listed, offsets, -1).reshape(1, slab_count * lists)
    pattern = jnp.pad(pattern, ((0, 0), (0, LANES - slab_count * lists)), constant_values=-1)
    empty = jnp.full((5, LANES), -1, jnp.int32)
    patterns = jnp.concatenate([shifted(pattern, 1), pattern, shifted(pattern, -1), empty])
    mine = jnp.arange(slabs)[:, None] == lax.axis_index(AXES)
    everyone = merged(jnp.where(mine, pattern, -1), [bit for bit in bits if bit < columns])

    everyone, patterns = lax.optimization_barrier((everyone, patterns))
    plan, _ = travel_plan(patterns, lists)
    message_out, sums_out, more_message, more_sums = pack_tiles(plan, pattern, weights, edges)
    message_out, sums_out, pattern = lax.optimization_barrier((message_out, sums_out, pattern))
    message = shifted(message_out, -1)
    sums = shifted(sums_out, 1)
    squares_out = square_diagonals(pattern, weights, edges)
    squares_out, pattern = lax.optimization_barrier((squares_out, pattern))
    squares = shifted(squares_out, 1)

    todo = product_list(plan, pattern, lists)
    support, high, low = main_part(pattern, weights, edges)
    everyone, support = lax.optimization_barrier((everyone, support))
    _, level = travel_plan(merged(everyone, [bit for bit in bits if bit >= columns]), lists)

    def branch(back, forward):
        def run(more_message, more_sums):
            if not back:
                return more_message, more_sums
            tiles = shifted(more_message[: back * tile], -1)
            partial = shifted(more_sums[:forward], 1)
            spare = ((0, more_message.shape[0] - back * tile), (0, 0))
            spare_sums = ((0, more_sums.shape[0] - forward), (0, 0), (0, 0))
            return jnp.pad(tiles, spare), jnp.pad(partial, spare_sums)

        return run

    more_message, more_sums = lax.switch(
        level[0], [branch(*sizes) for sizes in MORE], more_message, more_sums
    )
    return rest_part(
        todo, weights, edges, high, low, squares, message, sums, more_message, more_sums, support
    )


def solution(mesh):
    in_specs = (
        P(AXES, None, None, None),
        P(AXES, None, None, None),
        P(AXES, None),
        P(AXES),
    )
    out_specs = P(AXES, None, None, None)
    return jax.shard_map(shards, mesh=mesh, in_specs=in_specs, out_specs=out_specs, check_vma=False)
```

```python
import functools

import jax
import jax.numpy as jnp
from jax import lax
from jax.experimental import pallas as pl
from jax.experimental.pallas import tpu as pltpu
from jax.sharding import PartitionSpec as P

BAND = 6
SLAB = BAND - 1
LANES = 128
AXES = ("row", "col")
BACK, FORWARD = 10, 3
MORE = ((0, 0), (1, 1), (2, 1), (3, 2), (8, 6))
BEHIND, AHEAD = 0, 1
JOBS, RAWS, SUMS, DIAGONALS = 0, 1, 2, 3
TARGET, FACTOR, TURNED, PLACE, SUM_SLOT, DIAGONAL = 8, 32, 64, 96, 128, 144
JOB_SLOT, JOB_LEFT, JOB_RIGHT, LIST_SIZE = 160, 272, 384, 512
VMEM_LIMIT = 56 * 1024 * 1024

F32 = jnp.float32
BF16 = jnp.bfloat16
ANY = pl.BlockSpec(memory_space=pl.ANY)
SMEM = pl.BlockSpec(memory_space=pltpu.SMEM)
VMEM = pl.BlockSpec(memory_space=pltpu.VMEM)


def shifted(value, steps):
    count = lax.axis_size(AXES)
    first, last = (max(0, -steps), min(count, count - steps))
    return lax.ppermute(value, AXES, [(source, source + steps) for source in range(first, last)])


def split(value):
    high = value.astype(BF16)
    low = (value - high.astype(F32)).astype(BF16)
    return high, low


def dot(left, right):
    return jnp.dot(left, right, preferred_element_type=F32)


def product(left_high, left_low, right_high, right_low):
    return dot(left_high, right_high) + (dot(left_high, right_low) + dot(left_low, right_high))


def iotas(size):
    rows = lax.broadcasted_iota(jnp.int32, (size, size), 0)
    columns = lax.broadcasted_iota(jnp.int32, (size, size), 1)
    return rows, columns


def folded(tile):
    half = tile.shape[0] // 2
    rows, columns = iotas(half)
    lower_right = tile[half:, half:]
    mixed = jnp.where(rows <= columns, tile[:half, :half], lower_right)
    diagonal = jnp.sum(jnp.where(rows == columns, lower_right, 0.0), axis=0, keepdims=True)
    return mixed, tile[:half, half:], diagonal


def unfold(store, mixed, upper_right, diagonal):
    half = mixed.shape[0]
    rows, columns = iotas(half)
    turned = mixed.T
    store(0, 0, jnp.where(rows <= columns, mixed, turned))
    store(0, half, upper_right)
    store(half, 0, upper_right.T)
    lower_right = jnp.where(rows > columns, mixed, turned)
    store(half, half, jnp.where(rows == columns, diagonal, lower_right))


def slot_table(table, pattern, row, lists):
    for place in range(SLAB * BAND):
        table[place] = -1
    for slot in range(SLAB * lists):
        offset = pattern[row, slot]
        table[jnp.where(offset >= 0, slot // lists * BAND + offset, SLAB * BAND)] = slot


def listing(items, plan, row, first):
    count = jnp.int32(0)
    for i in range(SLAB):
        mask = plan[row, first + i]
        for bit in range(1, BAND):
            items[count] = i * BAND + bit
            count = count + ((mask >> bit) & 1)
    return count


def diagonals_needed(items, first, plan, row):
    count = jnp.int32(0)
    for i in range(SLAB):
        items[first + count] = i
        count = count + (plan[row, i] & 1)
    return count


def slot_copy(source, target, semaphore, slot, lists):
    return pltpu.make_async_copy(source.at[slot // lists, slot % lists], target.at[slot], semaphore)


def call(kernel, **kwargs):
    return pl.pallas_call(
        kernel,
        compiler_params=pltpu.CompilerParams(vmem_limit_bytes=VMEM_LIMIT),
        **kwargs,
    )


def crossing_slot(pattern, row, slot, lists):
    offset = pattern[row, slot]
    return (offset >= 0) & (slot // lists + offset >= SLAB)


def square_kernel(lists, pattern, weights, edges, out, w, e, total, table, sems):
    tile = weights.shape[-1]
    half = tile // 2
    slot_table(table, pattern, 0, lists)

    @pl.loop(0, SLAB * lists)
    def _(slot):
        @pl.when(crossing_slot(pattern, 0, slot, lists))
        def _():
            slot_copy(weights, w, sems.at[0, slot], slot, lists).start()
            slot_copy(edges, e, sems.at[1, slot], slot, lists).start()

    out[SLAB * half :, :] = jnp.zeros((8, tile), F32)
    for j in range(SLAB):
        total[...] = jnp.zeros((tile, tile), F32)

        @pl.loop(j, SLAB)
        def _(i):
            slot = table[i * BAND + SLAB + j - i]

            @pl.when(slot >= 0)
            def _():
                slot_copy(weights, w, sems.at[0, slot], slot, lists).wait()
                slot_copy(edges, e, sems.at[1, slot], slot, lists).wait()
                value = w[slot] * e[slot].astype(F32)
                total[...] += product(*split(value.T), *split(value))

        mixed, upper_right, diagonal = folded(total[...])
        out[j * half : (j + 1) * half, :half] = mixed
        out[j * half : (j + 1) * half, half:] = upper_right
        out[SLAB * half + j : SLAB * half + j + 1, :half] = diagonal


def square_diagonals(pattern, weights, edges):
    _, lists, tile, _ = weights.shape
    return call(
        functools.partial(square_kernel, lists),
        in_specs=[SMEM, ANY, ANY],
        out_specs=VMEM,
        out_shape=jax.ShapeDtypeStruct((SLAB * tile // 2 + 8, tile), F32),
        scratch_shapes=[
            pltpu.VMEM((SLAB * lists, tile, tile), F32),
            pltpu.VMEM((SLAB * lists, tile, tile), jnp.int32),
            pltpu.VMEM((tile, tile), F32),
            pltpu.SMEM((SLAB * BAND + 1,), jnp.int32),
            pltpu.SemaphoreType.DMA((2, SLAB * lists)),
        ],
    )(pattern, weights, edges)


def plan_kernel(lists, patterns, plan, choice):
    offsets = patterns[...]
    slabs = offsets.shape[0]
    lane = lax.broadcasted_iota(jnp.int32, offsets.shape, 1)
    row = lax.broadcasted_iota(jnp.int32, offsets.shape, 0)
    inside = (offsets >= 0) & (lane < SLAB * lists)
    bits = jnp.where(inside, jnp.left_shift(1, jnp.maximum(offsets, 0)), 0)

    def ahead(value, steps):
        return pltpu.roll(value, LANES - steps, 1) if steps else value

    mask = bits
    for a in range(1, lists):
        mask = mask | ahead(bits, a)
    own = [ahead(mask, i * lists) for i in range(SLAB)]
    rows = own + [pltpu.roll(value, slabs - 1, 0) for value in own]

    def has(r, offset):
        return jnp.right_shift(rows[r], offset) & 1

    zero = jnp.zeros_like(mask)
    need = [zero] * SLAB
    for i in range(SLAB):
        for m in range(SLAB - i, BAND):
            middle = i + m
            wanted = zero
            for t in range(BAND):
                target = i + t
                if target >= SLAB:
                    other, offset = (middle, t - m) if m <= t else (target, m - t)
                    used = has(i, t) & has(middle, m) & has(other, offset)
                    wanted = wanted | used
                    place = other - SLAB
                    need[place] = need[place] | jnp.left_shift(used, offset)
                elif m > t:
                    wanted = wanted | (has(i, t) & has(middle, m) & has(target, m - t))
            need[middle - SLAB] = need[middle - SLAB] | jnp.left_shift(wanted, m)
    crossing = [jnp.right_shift(jnp.left_shift(rows[i], i), SLAB) for i in range(SLAB)]
    partial = []
    for j in range(SLAB):
        cover = zero
        for i in range(SLAB):
            cover = cover | jnp.where(jnp.right_shift(crossing[i], j) & 1 == 1, crossing[i], 0)
        listed = jnp.left_shift(rows[SLAB + j], j) & ((1 << SLAB) - (2 << j))
        partial.append(cover & listed)
    def total(group, bits):
        count = zero
        for value in group:
            for bit in bits:
                count = count + (jnp.right_shift(value, bit) & 1)
        return count

    room = jnp.right_shift(2 * BACK - total(need, (0,)), 1)
    extra = []
    for count in (total(need, range(1, BAND)) - room, total(partial, range(1, BAND)) - FORWARD):
        count = jnp.where((lane == 0) & (row < slabs - 1), count, 0)
        extra.append(jnp.max(count.astype(F32)).astype(jnp.int32))
    result = zero
    for place, value in enumerate(need + partial):
        value = pltpu.roll(value, place, 1) if place else value
        result = jnp.where((lane == place) & (row < slabs - 1), value, result)
    plan[...] = result
    level = jnp.int32(0)
    for back, forward in MORE[:-1]:
        level = level + ((extra[0] > back) | (extra[1] > forward)).astype(jnp.int32)
    choice[0] = level


def travel_plan(patterns, lists):
    return call(
        functools.partial(plan_kernel, lists),
        in_specs=[VMEM],
        out_specs=[VMEM, SMEM],
        out_shape=[
            jax.ShapeDtypeStruct(patterns.shape, jnp.int32),
            jax.ShapeDtypeStruct((1,), jnp.int32),
        ],
    )(patterns)


def pack_kernel(
    lists, plan, pattern, weights, edges, message, squares_out, more_tiles_out, more_squares_out,
    w, e, total, halves, table, raw, sums, diagonals, needed, sems, tile_sem, half_sem, total_sem,
):
    tile = weights.shape[-1]
    half = tile // 2
    slots = SLAB * lists
    slot_table(table, pattern, 0, lists)
    raw_count = listing(raw, plan, BEHIND, 0)
    sum_count = listing(sums, plan, AHEAD, SLAB)
    half_count = diagonals_needed(diagonals, 0, plan, BEHIND)
    room = lax.shift_right_logical(2 * BACK - half_count, 1)

    for slot in range(slots + 1):
        needed[slot] = 0

    def factors(k, i):
        first = SLAB + sums[k] // BAND - i
        second = SLAB + sums[k] % BAND - i
        inside = (first < BAND) & (second < BAND)
        left = table[i * BAND + jnp.minimum(first, BAND - 1)]
        right = table[i * BAND + jnp.minimum(second, BAND - 1)]
        return left, right, inside & (left >= 0) & (right >= 0)

    @pl.loop(0, raw_count)
    def _(k):
        needed[table[raw[k]]] = 1

    @pl.loop(0, half_count)
    def _(k):
        needed[table[diagonals[k] * BAND]] = 1

    @pl.loop(0, sum_count)
    def _(k):
        for i in range(SLAB):
            left, right, both = factors(k, i)
            needed[jnp.where(both, left, slots)] = 1
            needed[jnp.where(both, right, slots)] = 1

    @pl.loop(0, slots)
    def _(slot):
        @pl.when(needed[slot] == 1)
        def _():
            slot_copy(weights, w, sems.at[0, slot], slot, lists).start()
            slot_copy(edges, e, sems.at[1, slot], slot, lists).start()

    @pl.loop(0, slots)
    def _(slot):
        @pl.when(needed[slot] == 1)
        def _():
            slot_copy(weights, w, sems.at[0, slot], slot, lists).wait()
            slot_copy(edges, e, sems.at[1, slot], slot, lists).wait()
            w[slot] = w[slot] * e[slot].astype(F32)

    @pl.loop(0, raw_count)
    def _(k):
        source = w.at[table[raw[k]]]

        @pl.when(k < room)
        def _():
            rows = pl.ds(pl.multiple_of(k * tile, tile), tile)
            pltpu.make_async_copy(source, message.at[rows], tile_sem).start()

        @pl.when(k >= room)
        def _():
            rows = pl.ds(pl.multiple_of((k - room) * tile, tile), tile)
            pltpu.make_async_copy(source, more_tiles_out.at[rows], tile_sem).start()

    @pl.loop(0, half_count)
    def _(k):
        mixed, upper_right, _ = folded(w[table[diagonals[k] * BAND]])
        halves[k, :, :half] = mixed
        halves[k, :, half:] = upper_right
        rows = pl.ds(pl.multiple_of((2 * BACK - 1 - k) * half, half), half)
        pltpu.make_async_copy(halves.at[k], message.at[rows], half_sem).start()

    @pl.loop(0, sum_count)
    def _(k):
        total[k] = jnp.zeros((tile, tile), F32)

        @pl.loop(0, SLAB)
        def _(i):
            left, right, both = factors(k, i)

            @pl.when(both)
            def _():
                total[k] += product(*split(w[left].T), *split(w[right]))

        @pl.when(k < FORWARD)
        def _():
            pltpu.make_async_copy(total.at[k], squares_out.at[k], total_sem).start()

        @pl.when(k >= FORWARD)
        def _():
            target = more_squares_out.at[k - FORWARD]
            pltpu.make_async_copy(total.at[k], target, total_sem).start()

    @pl.loop(0, raw_count)
    def _(k):
        pltpu.make_async_copy(w.at[0], message.at[pl.ds(0, tile)], tile_sem).wait()

    @pl.loop(0, half_count)
    def _(k):
        pltpu.make_async_copy(halves.at[0], message.at[pl.ds(0, half)], half_sem).wait()

    @pl.loop(0, sum_count)
    def _(k):
        pltpu.make_async_copy(total.at[k], squares_out.at[0], total_sem).wait()


def pack_tiles(plan, pattern, weights, edges):
    _, lists, tile, _ = weights.shape
    slots = SLAB * lists
    most_back, most_forward = MORE[-1]
    return call(
        functools.partial(pack_kernel, lists),
        in_specs=[SMEM, SMEM, ANY, ANY],
        out_specs=[ANY] * 4,
        out_shape=[
            jax.ShapeDtypeStruct((BACK * tile, tile), F32),
            jax.ShapeDtypeStruct((FORWARD, tile, tile), F32),
            jax.ShapeDtypeStruct((most_back * tile, tile), F32),
            jax.ShapeDtypeStruct((most_forward, tile, tile), F32),
        ],
        scratch_shapes=[
            pltpu.VMEM((slots, tile, tile), F32),
            pltpu.VMEM((slots, tile, tile), jnp.int32),
            pltpu.VMEM((FORWARD + most_forward, tile, tile), F32),
            pltpu.VMEM((SLAB, tile // 2, tile), F32),
            pltpu.SMEM((SLAB * BAND + 1,), jnp.int32),
            pltpu.SMEM((SLAB * BAND,), jnp.int32),
            pltpu.SMEM((SLAB * BAND,), jnp.int32),
            pltpu.SMEM((SLAB + 1,), jnp.int32),
            pltpu.SMEM((slots + 1,), jnp.int32),
            pltpu.SemaphoreType.DMA((2, slots)),
            pltpu.SemaphoreType.DMA,
            pltpu.SemaphoreType.DMA,
            pltpu.SemaphoreType.DMA,
        ],
    )(plan, pattern, weights, edges)


def main_kernel(
    lists, pattern, weights, edges, out, turned_high, turned_low,
    w, e, high, low, total, result, table, sems, out_sem, factor_sem,
):
    tile = weights.shape[-1]
    slots = SLAB * lists
    slot_table(table, pattern, 0, lists)

    @pl.loop(0, slots)
    def _(slot):
        @pl.when(pattern[0, slot] >= 0)
        def _():
            slot_copy(weights, w, sems.at[0, slot], slot, lists).start()
            slot_copy(edges, e, sems.at[1, slot], slot, lists).start()

    def factors(slot):
        return (
            pltpu.make_async_copy(high.at[slot + slots], turned_high.at[slot], factor_sem),
            pltpu.make_async_copy(low.at[slot + slots], turned_low.at[slot], factor_sem),
        )

    @pl.loop(0, slots)
    def _(slot):
        @pl.when(pattern[0, slot] >= 0)
        def _():
            slot_copy(weights, w, sems.at[0, slot], slot, lists).wait()
            slot_copy(edges, e, sems.at[1, slot], slot, lists).wait()
            value = w[slot] * e[slot].astype(F32)
            w[slot] = value
            high[slot], low[slot] = split(value)

            @pl.when(pattern[0, slot] > 0)
            def _():
                high[slot + slots], low[slot + slots] = split(value.T)

            @pl.when(crossing_slot(pattern, 0, slot, lists))
            def _():
                for copy in factors(slot):
                    copy.start()

    def own(row, offset):
        inside = (row >= 0) & (row < SLAB) & (offset >= 0) & (offset < BAND)
        return jnp.where(inside, table[jnp.where(inside, row * BAND + offset, 0)], -1)

    def turned(row, offset):
        slot = own(row, offset)
        return jnp.where(slot >= 0, slot + slots, -1)

    @pl.loop(0, slots)
    def _(slot):
        i = slot // lists
        offset = pattern[0, slot]

        @pl.when(offset >= 0)
        def _():
            total[...] = jnp.zeros((tile, tile), F32)

            @pl.loop(1 - BAND, BAND)
            def _(m):
                left = jnp.where(m < 0, turned(i + m, -m), own(i + m, m))
                right = jnp.where(
                    m <= offset, own(i + m, offset - m), turned(i + offset, m - offset)
                )

                @pl.when((left >= 0) & (right >= 0))
                def _():
                    total[...] += product(high[left], low[left], high[right], low[right])

            result[slot] = w[slot] * total[...]

        @pl.when(offset < 0)
        def _():
            result[slot] = jnp.zeros((tile, tile), F32)

        pltpu.make_async_copy(result.at[slot], out.at[i, slot % lists], out_sem).start()

    @pl.loop(0, slots)
    def _(slot):
        pltpu.make_async_copy(result.at[slot], out.at[slot // lists, slot % lists], out_sem).wait()

        @pl.when(crossing_slot(pattern, 0, slot, lists))
        def _():
            for copy in factors(slot):
                copy.wait()


def main_part(pattern, weights, edges):
    _, lists, tile, _ = weights.shape
    slots = SLAB * lists
    turned = jax.ShapeDtypeStruct((slots, tile, tile), BF16)
    return call(
        functools.partial(main_kernel, lists),
        in_specs=[SMEM, ANY, ANY],
        out_specs=[ANY, ANY, ANY],
        out_shape=[jax.ShapeDtypeStruct(weights.shape, F32), turned, turned],
        scratch_shapes=[
            pltpu.VMEM((slots, tile, tile), F32),
            pltpu.VMEM((slots, tile, tile), jnp.int32),
            pltpu.VMEM((2 * slots, tile, tile), BF16),
            pltpu.VMEM((2 * slots, tile, tile), BF16),
            pltpu.VMEM((tile, tile), F32),
            pltpu.VMEM((slots, tile, tile), F32),
            pltpu.SMEM((SLAB * BAND + 1,), jnp.int32),
            pltpu.SemaphoreType.DMA((2, slots)),
            pltpu.SemaphoreType.DMA,
            pltpu.SemaphoreType.DMA,
        ],
        cost_estimate=pl.CostEstimate(
            flops=6 * 60 * tile**3, bytes_accessed=3 * weights.size * 4, transcendentals=0
        ),
    )(pattern, weights, edges)


def list_kernel(lists, plan, pattern, out, table, index, raw, sums):
    back = BACK + MORE[-1][0]
    slots = SLAB * lists
    first_raw = slots + SLAB
    slot_table(table, pattern, 0, lists)
    raw_count = listing(raw, plan, AHEAD, 0)
    sum_count = listing(sums, plan, BEHIND, SLAB)
    half_count = diagonals_needed(out, DIAGONAL, plan, AHEAD)
    room = lax.shift_right_logical(2 * BACK - half_count, 1)

    for row in range(SLAB):
        index[row * BAND] = slots + row
        for offset in range(1, BAND):
            index[row * BAND + offset] = -1

    @pl.loop(0, raw_count)
    def _(k):
        place = jnp.where(k < room, k, BACK + k - room)
        out[PLACE + k] = place
        index[raw[k]] = first_raw + place

    for place in range(TARGET, PLACE):
        out[place] = 0
    for row in range(SLAB):
        out[TARGET + row * lists] = 1

    def jobs_of(slot, count):
        i = slot // lists
        offset = pattern[0, slot]
        for m in range(1, BAND):
            row = i + m - SLAB
            left = index[jnp.maximum(row, 0) * BAND + m]
            column = i + offset
            straight = m <= offset
            gap = jnp.where(straight, offset - m, m - offset)
            later = straight | (column >= SLAB)
            next_row = jnp.where(straight, row, column - SLAB)
            theirs = index[jnp.clip(next_row, 0, SLAB - 1) * BAND + gap]
            ours = table[jnp.clip(column, 0, SLAB - 1) * BAND + gap]
            right = jnp.where(later, theirs, ours)
            valid = (offset >= 0) & (row >= 0) & (left >= 0) & (right >= 0)
            turned = valid & later & ~straight
            out[JOB_SLOT + count] = slot
            out[JOB_LEFT + count] = left
            out[JOB_RIGHT + count] = jnp.where(turned, right + back, right)
            out[TARGET + jnp.where(valid, slot, slots)] = 1
            out[FACTOR + jnp.where(valid & (right < first_raw), right, first_raw)] = 1
            out[TURNED + jnp.where(turned, right - first_raw, back)] = 1
            count = count + valid.astype(jnp.int32)
        return count

    jobs = lax.fori_loop(0, slots, jobs_of, jnp.int32(0))

    @pl.loop(0, sum_count)
    def _(k):
        slot = table[sums[k] // BAND * BAND + sums[k] % BAND - sums[k] // BAND]
        out[SUM_SLOT + k] = slot
        out[TARGET + slot] = 1

    out[JOBS] = jobs
    out[RAWS] = raw_count
    out[SUMS] = sum_count
    out[DIAGONALS] = half_count


def product_list(plan, pattern, lists):
    small = pltpu.SMEM((SLAB * BAND,), jnp.int32)
    return call(
        functools.partial(list_kernel, lists),
        in_specs=[SMEM, SMEM],
        out_specs=SMEM,
        out_shape=jax.ShapeDtypeStruct((LIST_SIZE,), jnp.int32),
        scratch_shapes=[pltpu.SMEM((SLAB * BAND + 1,), jnp.int32), small, small, small],
    )(plan, pattern)


def rest_kernel(
    lists, todo, weights, edges, turned_high, turned_low, squares, message, sums, more_message, more_sums,
    before, out, w, e, high, low, result, stage, sems, out_sem, stage_sem,
):
    tile = weights.shape[-1]
    half = tile // 2
    slots = SLAB * lists
    back = (message.shape[0] + more_message.shape[0]) // tile
    first_raw = slots + SLAB

    def inputs(slot):
        return (
            slot_copy(weights, w, sems.at[0, slot], slot, lists),
            slot_copy(edges, e, sems.at[1, slot], slot, lists),
            slot_copy(before, result, sems.at[2, slot], slot, lists),
        )

    def factors(slot):
        return (
            pltpu.make_async_copy(turned_high.at[slot], high.at[slot], sems.at[3, slot]),
            pltpu.make_async_copy(turned_low.at[slot], low.at[slot], sems.at[4, slot]),
        )

    def output(slot):
        return pltpu.make_async_copy(result.at[slot], out.at[slot // lists, slot % lists], out_sem)

    @pl.loop(0, slots)
    def _(slot):
        @pl.when(todo[FACTOR + slot] == 1)
        def _():
            for copy in factors(slot):
                copy.start()

        @pl.when(todo[TARGET + slot] == 1)
        def _():
            for copy in inputs(slot):
                copy.start()

    @pl.loop(0, todo[DIAGONALS])
    def _(k):
        row = todo[DIAGONAL + k]

        @pl.when(todo[FACTOR + slots + row] == 1)
        def _():
            def store(first, column, quarter):
                part = (slots + row, pl.ds(first, half), pl.ds(column, half))
                high[part], low[part] = split(quarter)

            part = message[pl.ds(pl.multiple_of((2 * BACK - 1 - k) * half, half), half), :]
            unfold(store, part[:, :half], part[:, half:], jnp.zeros((1, half), F32))

    @pl.loop(0, todo[RAWS])
    def _(k):
        place = todo[PLACE + k]

        @pl.when(place < BACK)
        def _():
            stage[...] = message[pl.ds(pl.multiple_of(place * tile, tile), tile), :]

        @pl.when(place >= BACK)
        def _():
            rows = pl.ds(pl.multiple_of((place - BACK) * tile, tile), tile)
            copy = pltpu.make_async_copy(more_message.at[rows], stage, stage_sem)
            copy.start()
            copy.wait()

        value = stage[...]
        high[first_raw + place], low[first_raw + place] = split(value)

        @pl.when(todo[TURNED + place] == 1)
        def _():
            high[first_raw + back + place], low[first_raw + back + place] = split(value.T)

    @pl.loop(0, slots)
    def _(slot):
        @pl.when(todo[FACTOR + slot] == 1)
        def _():
            for copy in factors(slot):
                copy.wait()

        @pl.when(todo[TARGET + slot] == 1)
        def _():
            for copy in inputs(slot):
                copy.wait()
            w[slot] = w[slot] * e[slot].astype(F32)

    @pl.loop(0, SLAB)
    def _(i):
        def store(first, column, quarter):
            part = (i * lists, pl.ds(first, half), pl.ds(column, half))
            result[part] += w[part] * quarter

        part = squares[pl.ds(pl.multiple_of(i * half, half), half), :]
        rows = squares[SLAB * half :, :half]
        row = lax.broadcasted_iota(jnp.int32, rows.shape, 0)
        diagonal = jnp.sum(jnp.where(row == i, rows, 0.0), axis=0, keepdims=True)
        unfold(store, part[:, :half], part[:, half:], diagonal)

    @pl.loop(0, todo[SUMS])
    def _(k):
        slot = todo[SUM_SLOT + k]

        @pl.when(k < FORWARD)
        def _():
            stage[...] = sums[k]

        @pl.when(k >= FORWARD)
        def _():
            copy = pltpu.make_async_copy(more_sums.at[k - FORWARD], stage, stage_sem)
            copy.start()
            copy.wait()

        result[slot] += w[slot] * stage[...]

    @pl.loop(0, todo[JOBS])
    def _(job):
        slot, left, right = todo[JOB_SLOT + job], todo[JOB_LEFT + job], todo[JOB_RIGHT + job]
        value = product(high[left], low[left], high[right], low[right])
        result[slot] += w[slot] * value

    @pl.loop(0, slots)
    def _(slot):
        @pl.when(todo[TARGET + slot] == 1)
        def _():
            output(slot).start()

    @pl.loop(0, slots)
    def _(slot):
        @pl.when(todo[TARGET + slot] == 1)
        def _():
            output(slot).wait()


def rest_part(todo, weights, edges, high, low, squares, message, sums, more_message, more_sums, before):
    _, lists, tile, _ = weights.shape
    slots = SLAB * lists
    factors = slots + SLAB + 2 * (BACK + MORE[-1][0])
    return call(
        functools.partial(rest_kernel, lists),
        in_specs=[SMEM, ANY, ANY, ANY, ANY, VMEM, VMEM, VMEM, ANY, ANY, ANY],
        out_specs=ANY,
        out_shape=jax.ShapeDtypeStruct(weights.shape, F32),
        input_output_aliases={10: 0},
        scratch_shapes=[
            pltpu.VMEM((slots, tile, tile), F32),
            pltpu.VMEM((slots, tile, tile), jnp.int32),
            pltpu.VMEM((factors, tile, tile), BF16),
            pltpu.VMEM((factors, tile, tile), BF16),
            pltpu.VMEM((slots, tile, tile), F32),
            pltpu.VMEM((tile, tile), F32),
            pltpu.SemaphoreType.DMA((5, slots)),
            pltpu.SemaphoreType.DMA,
            pltpu.SemaphoreType.DMA,
        ],
    )(todo, weights, edges, high, low, squares, message, sums, more_message, more_sums, before)


def merged(value, bits):
    count = lax.axis_size(AXES)
    for bit in bits:
        other = lax.ppermute(value, AXES, [(device, device ^ bit) for device in range(count)])
        value = jnp.maximum(value, other)
    return value


def shards(weights, edges, offsets, counts):
    slab_count, lists = offsets.shape
    tile = weights.shape[-1]
    slabs = lax.axis_size(AXES)
    columns = lax.axis_size(AXES[1])
    bits = [1 << bit for bit in range(slabs.bit_length() - 1)]
    listed = jnp.arange(lists)[None, :] < counts[:, None]
    pattern = jnp.where(listed, offsets, -1).reshape(1, slab_count * lists)
    pattern = jnp.pad(pattern, ((0, 0), (0, LANES - slab_count * lists)), constant_values=-1)
    empty = jnp.full((5, LANES), -1, jnp.int32)
    patterns = jnp.concatenate([shifted(pattern, 1), pattern, shifted(pattern, -1), empty])
    mine = jnp.arange(slabs)[:, None] == lax.axis_index(AXES)
    everyone = merged(jnp.where(mine, pattern, -1), [bit for bit in bits if bit < columns])

    everyone, patterns = lax.optimization_barrier((everyone, patterns))
    plan, _ = travel_plan(patterns, lists)
    message_out, sums_out, more_message, more_sums = pack_tiles(plan, pattern, weights, edges)
    message_out, sums_out, pattern = lax.optimization_barrier((message_out, sums_out, pattern))
    message = shifted(message_out, -1)
    sums = shifted(sums_out, 1)
    squares_out = square_diagonals(pattern, weights, edges)
    squares_out, pattern = lax.optimization_barrier((squares_out, pattern))
    squares = shifted(squares_out, 1)

    todo = product_list(plan, pattern, lists)
    support, high, low = main_part(pattern, weights, edges)
    everyone, support = lax.optimization_barrier((everyone, support))
    _, level = travel_plan(merged(everyone, [bit for bit in bits if bit >= columns]), lists)

    def branch(back, forward):
        def run(more_message, more_sums):
            if not back:
                return more_message, more_sums
            tiles = shifted(more_message[: back * tile], -1)
            partial = shifted(more_sums[:forward], 1)
            spare = ((0, more_message.shape[0] - back * tile), (0, 0))
            spare_sums = ((0, more_sums.shape[0] - forward), (0, 0), (0, 0))
            return jnp.pad(tiles, spare), jnp.pad(partial, spare_sums)

        return run

    more_message, more_sums = lax.switch(
        level[0], [branch(*sizes) for sizes in MORE], more_message, more_sums
    )
    return rest_part(
        todo, weights, edges, high, low, squares, message, sums, more_message, more_sums, support
    )


def solution(mesh):
    in_specs = (
        P(AXES, None, None, None),
        P(AXES, None, None, None),
        P(AXES, None),
        P(AXES),
    )
    out_specs = P(AXES, None, None, None)
    return jax.shard_map(shards, mesh=mesh, in_specs=in_specs, out_specs=out_specs, check_vma=False)
```
